128 devices in a mesh: dp: 32 (over x, y, z_lo), tensor: 4 (over z_hi, core).
Axes of the slice: x: 4, y: 4, z: 4 (z_hi: 2, z_lo: 2; z = z_hi * 2 + z_lo), core: 2. Of those that a mesh axis runs over, the one named last changes fastest.
Arguments:
- tokens: bfloat16 [16384, 1536], P('dp'), may hold values from -6 to 6
- segments: int32 [32, 512], P('dp'), may hold values from 0 to 3, never falling along the last dimension, each value on 1 to 384 neighbouring positions
- norm_one: float32 [1536], replicated, may hold values from 0.1 to 1.9
- w_query: bfloat16 [1536, 1536], P(None, 'tensor'), may hold values from -0.15625 to 0.15625
- key_projection: bfloat16 [1536, 512], P(None, 'tensor'), may hold values from -0.15625 to 0.15625
- value_projection: bfloat16 [1536, 512], P(None, 'tensor'), may hold values from -0.15625 to 0.15625
- w_out: bfloat16 [1536, 1536], P('tensor'), may hold values from -0.625 to 0.625
- q_gain: float32 [64], replicated, may hold values from 0.1 to 1.9
- k_gain: float32 [64], replicated, may hold values from 0.1 to 1.9
- norm_two: float32 [1536], replicated, may hold values from 0.1 to 1.9
- w_gate: bfloat16 [1536, 6912], P(None, 'tensor'), may hold values from -0.15625 to 0.15625
- w_up: bfloat16 [1536, 6912], P(None, 'tensor'), may hold values from -0.15625 to 0.15625
- w_down: bfloat16 [6912, 1536], P('tensor'), may hold values from -0.078125 to 0.078125
- cotangent: bfloat16 [16384, 1536], P('dp'), may hold values from -6 to 6
Outputs:
- block_out: bfloat16 [16384, 1536], P('dp')
- grad_tokens: bfloat16 [16384, 1536], P('dp')
- grad_norm_one: float32 [1536], P('dp')
- grad_query: float32 [1536, 1536], P('dp', 'tensor')
- grad_key: float32 [1536, 512], P('dp', 'tensor')
- grad_value: float32 [1536, 512], P('dp', 'tensor')
- grad_out: float32 [1536, 1536], P('tensor', 'dp')
- grad_q_gain: float32 [64], replicated
- grad_k_gain: float32 [64], replicated
- grad_norm_two: float32 [1536], P('dp')
- grad_gate: float32 [1536, 6912], P('dp', 'tensor')
- grad_up: float32 [1536, 6912], P('dp', 'tensor')
- grad_down: float32 [6912, 1536], P('tensor', 'dp')
The draws below stay inside these ranges and needn't reach their ends.
Inputs may be any that keep to these rules, and one draw needn't show every extreme that they name: `segments`: within a row document numbers never fall; a document holds 1 to 384 tokens of its row, and some holds exactly that many.
All inputs are finite; a program needn't handle non-finite values.
Results may differ from the reference program's by a relative error of at most 0.014.
Values sent between devices are 32-bit elements; how exact they have to be, the bound alone decides.
A program may use at most 192 MiB of HBM per device.

```python
import math
import jax
import jax.numpy as jnp
import numpy as np
from jax import lax

MODEL_WIDTH = 1536
QUERY_HEADS = 24
KEY_VALUE_HEADS = 8
HEAD_SIZE = 64
FF = 6912
TOK_DEV = 512
SEQS = 32
TOKENS = 16384


def raised(drawn, stream_key, source, target, shards_of, factor):
    owner, partner = [(jnp.arange(drawn.shape[dim]) // (drawn.shape[dim] // shards_of)).reshape([-1 if axis == dim else 1 for axis in range(drawn.ndim)]) for dim in (source, target)]
    chosen = jax.random.permutation(stream_key, shards_of)[partner]
    strong = (owner == chosen) | (owner == (partner + shards_of // 2) % shards_of)
    return jnp.where(strong, factor * drawn, drawn)


def block_scale(stream_key, dims, cuts, least, largest):
    level = 1.0
    for dim, blocks in cuts:
        heights = jax.random.uniform(jax.random.fold_in(jax.random.fold_in(stream_key, 6), dim), (blocks,), jnp.float32, least / len(cuts), largest / len(cuts))
        level = level * jnp.repeat(jnp.exp(heights), dims[dim] // blocks).reshape((-1,) + (1,) * (len(dims) - 1 - dim))
    return level


def split_up(count, total, limit, lean):
    portions = [(1 << 20) // math.isqrt(rank ** lean) + 1 for rank in range(2, count + 1)]
    spare, given = total - limit - (count - 1), [1] * (count - 1)
    while spare > 0:
        candidates = [i for i in range(count - 1) if given[i] < limit]
        mass, remaining = sum([portions[i] for i in candidates]), spare
        for i in candidates:
            more = min(limit - given[i], max(1, remaining * portions[i] // mass), spare)
            given[i] = given[i] + more
            spare = spare - more
    return np.array([limit] + given)


def ragged(own_key, number_of, total, limit, skew):
    if number_of == 2:
        one = jax.random.randint(own_key, (), max(1, total - limit), min(limit, total - 1) + 1)
        return jnp.stack([one, total - one])
    lengths = jnp.asarray(split_up(number_of, total, limit, skew), jnp.int32)
    twos = (number_of - 1) // 2
    giver, taker = lengths[1:1 + 2 * twos:2], lengths[2:2 + 2 * twos:2]
    margin = jnp.minimum(giver - 1, limit - taker)
    passed = jax.random.randint(jax.random.fold_in(own_key, 1), (twos,), 0, 1 << 20) % (margin + 1)
    lengths = lengths.at[1:1 + 2 * twos:2].set(giver - passed).at[2:2 + 2 * twos:2].set(taker + passed)
    return lengths[jax.random.permutation(jax.random.fold_in(own_key, 2), number_of)]


def centred(own_key, extent, spread, bound, cuts=(), held_as=jnp.bfloat16):
    factor_of = block_scale(own_key, extent, cuts, -0.22, 0.18) if cuts else 1.0
    values = jax.random.normal(own_key, extent, jnp.float32) * spread * factor_of
    return jnp.minimum(jnp.maximum(values, -bound), bound).astype(held_as)


def gaussian_with(stream_key, dims, spread, reach, cuts, heavy, kind=jnp.bfloat16):
    entries = spread * jax.random.normal(stream_key, dims, jnp.float32)
    if cuts:
        entries = entries * block_scale(stream_key, dims, cuts, -0.22, 0.18)
    return jnp.clip(raised(entries, jax.random.fold_in(stream_key, 3), *heavy), -reach, reach).astype(kind)


def setup_inputs(seed: int = 0) -> dict:
    splits = jax.random.split(jax.random.key(seed), 15)
    return {
        "tokens": gaussian_with(splits[0], (TOKENS, MODEL_WIDTH), 1.0, 6.0, ((0, 32),), (0, 1, 32, 2.75)),
        "segments": jax.vmap(lambda own: jnp.searchsorted(jnp.cumsum(ragged(own, max(2, TOK_DEV // 128), TOK_DEV, TOK_DEV * 3 // 4, 0)), jnp.arange(TOK_DEV), side="right"))(jax.random.split(splits[1], SEQS)).reshape((SEQS, TOK_DEV)).astype(jnp.int32),
        "norm_one": jnp.clip(1.0 + 0.18 * jax.random.normal(splits[2], (MODEL_WIDTH,), jnp.float32), 0.1, 1.9),
        "w_query": centred(splits[3], (MODEL_WIDTH, QUERY_HEADS * HEAD_SIZE), MODEL_WIDTH ** -0.5, 0.15625, ((1, 4),)),
        "key_projection": centred(splits[4], (MODEL_WIDTH, KEY_VALUE_HEADS * HEAD_SIZE), MODEL_WIDTH ** -0.5, 0.15625, ((1, 4),)),
        "value_projection": centred(splits[5], (MODEL_WIDTH, KEY_VALUE_HEADS * HEAD_SIZE), MODEL_WIDTH ** -0.5, 0.15625, ((1, 4),)),
        "w_out": centred(splits[6], (QUERY_HEADS * HEAD_SIZE, MODEL_WIDTH), (QUERY_HEADS * HEAD_SIZE // 16) ** -0.5, 0.625, ((0, 4),)),
        "q_gain": jnp.clip(1.0 + 0.18 * jax.random.normal(splits[7], (HEAD_SIZE,), jnp.float32), 0.1, 1.9),
        "k_gain": jnp.clip(1.0 + 0.18 * jax.random.normal(splits[8], (HEAD_SIZE,), jnp.float32), 0.1, 1.9),
        "norm_two": jnp.clip(1.0 + 0.18 * jax.random.normal(splits[9], (MODEL_WIDTH,), jnp.float32), 0.1, 1.9),
        "w_gate": centred(splits[10], (MODEL_WIDTH, FF), MODEL_WIDTH ** -0.5, 0.15625, ((1, 4),)),
        "w_up": centred(splits[11], (MODEL_WIDTH, FF), MODEL_WIDTH ** -0.5, 0.15625, ((1, 4),)),
        "w_down": centred(splits[12], (FF, MODEL_WIDTH), FF ** -0.5, 0.078125, ((0, 4),)),
        "cotangent": gaussian_with(splits[13], (TOKENS, MODEL_WIDTH), 1.0, 6.0, ((0, 32),), (0, 1, 32, 2.75)),
    }


EPSILON = 1e-05
THETA = 1000000.0

@jax.custom_vjp
def reduced_precision(v):
    return lax.optimization_barrier(v.astype(jnp.bfloat16)).astype(jnp.float32)

@jax.custom_vjp
def reduced_backward(v):
    return v

def low_keep(v):
    return (reduced_precision(v), None)

def low_pass(kept, grad):
    return (grad,)

def back_keep(v):
    return (v, None)

def back_low(kept, grad):
    return (reduced_precision(grad),)
reduced_precision.defvjp(low_keep, low_pass)
reduced_backward.defvjp(back_keep, back_low)

def product_accurate(left, right):
    return jnp.dot(left, right, precision=lax.Precision.HIGHEST)

def scale_of_norm(values, gain):
    return values * lax.rsqrt(lax.optimization_barrier(jnp.mean(values * values, axis=-1, keepdims=True)) + EPSILON) * gain

def rope_tables(segments):
    sequence_count, sequence_length = segments.shape
    index_row = jnp.arange(sequence_length, dtype=jnp.int32)[None, :]
    change = jnp.concatenate([jnp.ones((sequence_count, 1), jnp.bool_), segments[:, 1:] != segments[:, :-1]], axis=1)
    starts = lax.cummax(jnp.where(change, index_row, 0).astype(jnp.int32), axis=1)
    position = (index_row - starts).astype(jnp.float32)
    frequency = THETA ** (-jnp.arange(HEAD_SIZE // 2, dtype=jnp.float32) * 2.0 / HEAD_SIZE)
    angles = position[:, :, None] * frequency
    allowed = (segments[:, :, None] == segments[:, None, :]) & (index_row[:, :, None] >= index_row[:, None, :])
    return (jnp.cos(angles), jnp.sin(angles), allowed)

def apply_rotary(values, cosine_table, sine_table):
    first, second = jnp.split(values, 2, axis=-1)
    return jnp.concatenate([first * cosine_table - second * sine_table, second * cosine_table + first * sine_table], axis=-1)

def reference(tokens, segments, norm_one, w_query, key_projection, value_projection, w_out, q_gain, k_gain, norm_two, w_gate, w_up, w_down, cotangent):
    cosine_table, sine_table, allowed = rope_tables(segments)
    cosine_table = cosine_table[:, :, None, :]
    sine_table = sine_table[:, :, None, :]
    sequence_count, sequence_length = segments.shape
    group_count = QUERY_HEADS // KEY_VALUE_HEADS
    scale = HEAD_SIZE ** (-0.5)

    def attend(inputs):
        queries, keys, values, mask = inputs
        scores = jnp.einsum('qhgd,khd->hgqk', queries, keys, precision=lax.Precision.HIGHEST) * scale
        scores = reduced_backward(scores)
        scores = jnp.where(mask[None, None], scores, -1e+30)
        weights = reduced_precision(jax.nn.softmax(scores, axis=-1))
        return jnp.einsum('hgqk,khd->qhgd', weights, values, precision=lax.Precision.HIGHEST)

    def forward(tokens_in, gain_one, query_w, key_matrix, value_matrix, out_w, query_gain, gain_k, gain_two, gate_w, up_w, down_w):
        first_hidden = reduced_precision(scale_of_norm(tokens_in, gain_one))
        query_unrotated = reduced_backward(product_accurate(first_hidden, query_w)).reshape(sequence_count, sequence_length, QUERY_HEADS, HEAD_SIZE)
        key_unrotated = reduced_backward(product_accurate(first_hidden, key_matrix)).reshape(sequence_count, sequence_length, KEY_VALUE_HEADS, HEAD_SIZE)
        value_expanded = reduced_precision(reduced_backward(product_accurate(first_hidden, value_matrix))).reshape(sequence_count, sequence_length, KEY_VALUE_HEADS, HEAD_SIZE)
        query_rotated = reduced_precision(apply_rotary(scale_of_norm(query_unrotated, query_gain), cosine_table, sine_table)).reshape(sequence_count, sequence_length, KEY_VALUE_HEADS, group_count, HEAD_SIZE)
        key_rot = reduced_precision(apply_rotary(scale_of_norm(key_unrotated, gain_k), cosine_table, sine_table))
        mixed = lax.map(jax.checkpoint(attend), (query_rotated, key_rot, value_expanded, allowed))
        mixed = reduced_precision(reduced_backward(mixed.reshape(sequence_count * sequence_length, QUERY_HEADS * HEAD_SIZE)))
        resid = tokens_in + reduced_backward(product_accurate(mixed, out_w))
        hidden_two = reduced_precision(scale_of_norm(resid, gain_two))
        gate = reduced_backward(product_accurate(hidden_two, gate_w))
        upper = reduced_backward(product_accurate(hidden_two, up_w))
        activ = reduced_precision(jax.nn.silu(gate) * upper)
        return resid + reduced_backward(product_accurate(activ, down_w))
    primals = (tokens.astype(jnp.float32), norm_one, w_query.astype(jnp.float32), key_projection.astype(jnp.float32), value_projection.astype(jnp.float32), w_out.astype(jnp.float32), q_gain, k_gain, norm_two, w_gate.astype(jnp.float32), w_up.astype(jnp.float32), w_down.astype(jnp.float32))
    result, pullback = jax.vjp(forward, *primals)
    grads = pullback(cotangent.astype(jnp.float32))
    return (result.astype(jnp.bfloat16), grads[0].astype(jnp.bfloat16), grads[1], grads[2], grads[3], grads[4], grads[5], grads[6], grads[7], grads[8], grads[9], grads[10], grads[11])
```

```python
import jax
import jax.numpy as jnp
from jax import lax
from jax.experimental import pallas as pl
from jax.experimental.pallas import tpu as pltpu
from jax.sharding import PartitionSpec as P

QUERY_HEADS = 24
KEY_VALUE_HEADS = 8
HEAD_SIZE = 64


EPSILON = 1e-05
THETA = 1000000.0


def rope_tables(segments):
    sequence_count, sequence_length = segments.shape
    index_row = jnp.arange(sequence_length, dtype=jnp.int32)[None, :]
    change = jnp.concatenate(
        [jnp.ones((sequence_count, 1), jnp.bool_), segments[:, 1:] != segments[:, :-1]], axis=1
    )
    starts = lax.cummax(jnp.where(change, index_row, 0), axis=1)
    position = (index_row - starts).astype(jnp.float32)
    frequency = THETA ** (-jnp.arange(HEAD_SIZE // 2, dtype=jnp.float32) * 2.0 / HEAD_SIZE)
    angles = position[:, :, None] * frequency
    allowed = (segments[:, :, None] == segments[:, None, :]) & (
        index_row[:, :, None] >= index_row[:, None, :]
    )
    return (jnp.cos(angles), jnp.sin(angles), allowed)


def apply_rotary(values, cosine_table, sine_table):
    first, second = jnp.split(values, 2, axis=-1)
    return jnp.concatenate(
        [first * cosine_table - second * sine_table, second * cosine_table + first * sine_table],
        axis=-1,
    )


def rotate_back(upstream, cosine_table, sine_table):
    first, second = jnp.split(upstream, 2, axis=-1)
    return jnp.concatenate(
        [first * cosine_table + second * sine_table, second * cosine_table - first * sine_table],
        axis=-1,
    )


def norm_rows(values, gain):
    inverse = lax.rsqrt(jnp.mean(values * values, axis=-1, keepdims=True) + EPSILON)
    return (values * inverse * gain, inverse)


def norm_back(values, inverse, gain, upstream):
    scaled = upstream * gain
    grad_in = inverse * scaled - values * inverse**3 * jnp.mean(
        scaled * values, axis=-1, keepdims=True
    )
    gain_grad = jnp.sum((upstream * values * inverse).reshape(-1, values.shape[-1]), axis=0)
    return (grad_in, gain_grad)


MESH = pl.DeviceIdType.MESH
F32 = jnp.float32
BF16 = jnp.bfloat16
WIDTH = 1536
TOK = 512
HALF = 256
FFL = 1728
MIB = 1 << 20


def place():
    dp = lax.axis_index("dp")
    tensor = lax.axis_index("tensor")
    x = lax.div(dp, 8)
    y = lax.rem(lax.div(dp, 2), 4)
    z = lax.div(tensor, 2) * 2 + lax.rem(dp, 2)
    return x, y, z, lax.rem(tensor, 2)


def device(x, y, z, core):
    return (x * 8 + y * 2 + lax.rem(z, 2), lax.div(z, 2) * 2 + core)


def greet(partners):
    barrier = pltpu.get_barrier_semaphore()
    for partner in partners:
        pl.semaphore_signal(barrier, inc=1, device_id=partner, device_id_type=MESH)
    pl.semaphore_wait(barrier, len(partners))


def remote(source, target, send_sem, recv_sem, partner):
    return pltpu.make_async_remote_copy(
        src_ref=source,
        dst_ref=target,
        send_sem=send_sem,
        recv_sem=recv_sem,
        device_id=partner,
        device_id_type=MESH,
    )


def by_rows(count, step, work):
    def body(i, carry):
        work(pl.ds(pl.multiple_of(i * step, step), step))
        return carry

    lax.fori_loop(0, count // step, body, 0)


PARTS = 4
PART = HALF // PARTS


def start_norm_kernel(
    part, tokens, gain, x1_out, h2_out, own, near, far, back, fin, sems, near_s, near_r, far_s, far_r, back_s, back_r
):
    x, y, z, core = place()
    mate = device(x, y, z, 1 - core)
    across = device(x, y, lax.rem(z + 2, 4), core)
    greet([mate, across])
    load = pltpu.make_async_copy(part.at[core], own, sems)
    load.start()
    first, second, third = [], [], []
    for j in range(PARTS):
        rows = pl.ds(j * PART, PART)
        copy = remote(part.at[1 - core, rows], near.at[rows], near_s.at[j], near_r.at[j], mate)
        copy.start()
        first.append(copy)
    load.wait()
    for j in range(PARTS):
        rows = pl.ds(j * PART, PART)
        first[j].wait_recv()

        def add(r, j=j):
            r = pl.ds(r.start + j * PART, r.size)
            own[r] = own[r] + near[r]

        by_rows(PART, 16, add)
        copy = remote(own.at[rows], far.at[rows], far_s.at[j], far_r.at[j], across)
        copy.start()
        second.append(copy)
    for j in range(PARTS):
        rows = pl.ds(j * PART, PART)
        second[j].wait_recv()

        def norm(r, j=j):
            r = pl.ds(pl.multiple_of(r.start + j * PART, 16), r.size)
            value = tokens[core, r].astype(F32) + (own[r] + far[r])
            inverse = lax.rsqrt(jnp.mean(value * value, axis=-1, keepdims=True) + EPSILON)
            low = (value * inverse * gain[...]).astype(BF16)
            x1_out[r] = value
            h2_out[core, r] = low
            fin[r] = low.astype(F32)

        by_rows(PART, 16, norm)
        copy = remote(fin.at[rows], back.at[rows], back_s.at[j], back_r.at[j], mate)
        copy.start()
        third.append(copy)
    for j in range(PARTS):
        third[j].wait_recv()

        def keep(r, j=j):
            r = pl.ds(pl.multiple_of(r.start + j * PART, 16), r.size)
            h2_out[1 - core, r] = back[r].astype(BF16)

        by_rows(PART, 16, keep)
    for copy in first + second + third:
        copy.wait_send()


def sum_scratch():
    return [pltpu.VMEM((HALF, WIDTH), F32)] * 5 + [pltpu.SemaphoreType.DMA] + [
        pltpu.SemaphoreType.DMA((PARTS,))
    ] * 6


def attention_sum(part, tokens, gain):
    vmem = pl.BlockSpec(memory_space=pltpu.VMEM)
    x1, h2 = pl.pallas_call(
        start_norm_kernel,
        out_shape=(
            jax.ShapeDtypeStruct((HALF, WIDTH), F32),
            jax.ShapeDtypeStruct((2, HALF, WIDTH), BF16),
        ),
        in_specs=[pl.BlockSpec(memory_space=pl.ANY), vmem, vmem],
        out_specs=(vmem, vmem),
        scratch_shapes=sum_scratch(),
        compiler_params=pltpu.CompilerParams(
            collective_id=1, has_side_effects=True, vmem_limit_bytes=40 * MIB
        ),
        name="attention_sum",
    )(part.reshape(2, HALF, WIDTH), tokens.reshape(2, HALF, WIDTH), gain.reshape(1, WIDTH))
    return x1, h2.reshape(TOK, WIDTH)


def back_norm_kernel(
    part, x1, upstream, gain, dx1_out, da_out, dg_out, own, near, far, back, fin, sems, near_s, near_r, far_s, far_r, back_s, back_r
):
    x, y, z, core = place()
    mate = device(x, y, z, 1 - core)
    across = device(x, y, lax.rem(z + 2, 4), core)
    greet([mate, across])
    load = pltpu.make_async_copy(part.at[core], own, sems)
    load.start()
    first, second, third = [], [], []
    for j in range(PARTS):
        rows = pl.ds(j * PART, PART)
        copy = remote(part.at[1 - core, rows], near.at[rows], near_s.at[j], near_r.at[j], mate)
        copy.start()
        first.append(copy)
    dg_out[...] = jnp.zeros((8, WIDTH), F32)
    load.wait()
    for j in range(PARTS):
        rows = pl.ds(j * PART, PART)
        first[j].wait_recv()

        def add(r, j=j):
            r = pl.ds(r.start + j * PART, r.size)
            own[r] = own[r] + near[r]

        by_rows(PART, 16, add)
        copy = remote(own.at[rows], far.at[rows], far_s.at[j], far_r.at[j], across)
        copy.start()
        second.append(copy)
    for j in range(PARTS):
        rows = pl.ds(j * PART, PART)
        second[j].wait_recv()

        def norm(r, j=j):
            r = pl.ds(pl.multiple_of(r.start + j * PART, 16), r.size)
            value = x1[r]
            total = own[r] + far[r]
            inverse = lax.rsqrt(jnp.mean(value * value, axis=-1, keepdims=True) + EPSILON)
            scaled = total * gain[...]
            grad = (
                upstream[core, r].astype(F32)
                + inverse * scaled
                - value * inverse**3 * jnp.mean(scaled * value, axis=-1, keepdims=True)
            )
            dg = total * value * inverse
            dg_out[...] += dg[0:8] + dg[8:16]
            low = grad.astype(BF16)
            dx1_out[r] = grad
            da_out[core, r] = low
            fin[r] = low.astype(F32)

        by_rows(PART, 16, norm)
        copy = remote(fin.at[rows], back.at[rows], back_s.at[j], back_r.at[j], mate)
        copy.start()
        third.append(copy)
    for j in range(PARTS):
        third[j].wait_recv()

        def keep(r, j=j):
            r = pl.ds(pl.multiple_of(r.start + j * PART, 16), r.size)
            da_out[1 - core, r] = back[r].astype(BF16)

        by_rows(PART, 16, keep)
    for copy in first + second + third:
        copy.wait_send()


def hidden_sum(part, x1, cotangent, gain):
    vmem = pl.BlockSpec(memory_space=pltpu.VMEM)
    dx1, da, dg = pl.pallas_call(
        back_norm_kernel,
        out_shape=(
            jax.ShapeDtypeStruct((HALF, WIDTH), F32),
            jax.ShapeDtypeStruct((2, HALF, WIDTH), BF16),
            jax.ShapeDtypeStruct((8, WIDTH), F32),
        ),
        in_specs=[pl.BlockSpec(memory_space=pl.ANY), vmem, vmem, vmem],
        out_specs=(vmem, vmem, vmem),
        scratch_shapes=sum_scratch(),
        compiler_params=pltpu.CompilerParams(
            collective_id=2, has_side_effects=True, vmem_limit_bytes=40 * MIB
        ),
        name="hidden_sum",
    )(part.reshape(2, HALF, WIDTH), x1, cotangent.reshape(2, HALF, WIDTH), gain.reshape(1, WIDTH))
    return dx1, da.reshape(TOK, WIDTH), dg


CMAX = 896
CHUNKS = (
    (0, 0, 0, 896, 0),
    (0, 0, 896, 896, 0),
    (0, 0, 1792, 896, 0),
    (0, 0, 2688, 768, 0),
    (1, 1, 0, 640, 1),
    (2, 2, 0, 384, 2),
    (3, 3, 0, 896, 3),
    (3, 3, 896, 896, 3),
)
WIDTHS = (3456, 640, 384, 1792)
XP, XM, YP, YM = range(4)
OPPOSITE = (XM, XP, YM, YP)


def scatter_kernel(*refs):
    lefts, rights, refs = refs[:4], refs[4:8], refs[8:]
    ffn_part, dh1_part, x1, dx1, tokens, gain, small_in, refs = *refs[:7], refs[7:]
    grads, block_out, grad_tokens, small_out, refs = refs[:4], refs[4], refs[5], refs[6], refs[7:]
    left_buf, right_buf, product, got, passed, got2, keep, got3, refs = *refs[:8], refs[8:]
    sum_own, sum_near, sum_far, sum_back, refs = *refs[:4], refs[4:]
    small, small_got, refs = refs[0], refs[1], refs[2:]
    left_sem, right_sem, s1, r1, s2, r2, s3, r3, credit, credit2, credit3, load_sem, sum_s, sum_r, small_s, small_r = refs

    x, y, z, core = place()
    around = (
        device(lax.rem(x + 1, 4), y, z, core),
        device(lax.rem(x + 3, 4), y, z, core),
        device(x, lax.rem(y + 1, 4), z, core),
        device(x, lax.rem(y + 3, 4), z, core),
    )
    z_lo = lax.rem(z, 2)
    beside = device(x, y, z + 1 - 2 * z_lo, core)
    mate = device(x, y, z, 1 - core)
    across = device(x, y, lax.rem(z + 2, 4), core)
    ring = (
        [device(lax.rem(x + i, 4), y, z, core) for i in (1, 2, 3)],
        [device(x, lax.rem(y + i, 4), z, core) for i in (1, 2, 3)],
        [device(x, y, lax.rem(z + i, 4), core) for i in (1, 2, 3)],
        [mate],
    )
    greet([one for group in ring for one in group])

    count = len(CHUNKS)
    place1, place2 = (x, y), (y, x)
    forward1, backward1 = (around[XP], around[YP]), (around[XM], around[YM])
    forward2, backward2 = (around[YP], around[XP]), (around[YM], around[XM])

    left_order = []
    for chunk in CHUNKS:
        if chunk[0] not in left_order:
            left_order.append(chunk[0])
    left_copies = [
        pltpu.make_async_copy(lefts[which], left_buf.at[i % 2], left_sem.at[i % 2])
        for i, which in enumerate(left_order)
    ]
    right_copies = [
        pltpu.make_async_copy(
            rights[chunk[1]].at[:, pl.ds(chunk[2], chunk[3])],
            right_buf.at[k % 2, :, pl.ds(0, chunk[3])],
            right_sem.at[k % 2],
        )
        for k, chunk in enumerate(CHUNKS)
    ]
    left_at = [left_order.index(chunk[0]) for chunk in CHUNKS]

    first, second, third = [], [], []
    for k, chunk in enumerate(CHUNKS):
        slot, cols = k % 2, pl.ds(0, chunk[3])
        per1, per2, per3 = [], [], []
        for o in range(2):
            far_block = lax.rem(place1[o] + 2, 4)
            after, before = lax.rem(place1[o] + 1, 4), lax.rem(place1[o] + 3, 4)
            top, low = pl.ds(0, 96), pl.ds(96, 96)
            plan = (
                (far_block, top, forward1[o]),
                (far_block, low, backward1[o]),
                (after, low, forward1[o]),
                (before, top, backward1[o]),
                (after, top, forward1[o]),
                (before, low, backward1[o]),
            )
            per1.append(
                [
                    remote(
                        product.at[slot, o, block, rows, cols],
                        got.at[slot, o, i, :, cols],
                        s1.at[slot, o, i],
                        r1.at[slot, o, i],
                        partner,
                    )
                    for i, (block, rows, partner) in enumerate(plan)
                ]
            )
            far_block = lax.rem(place2[o] + 2, 4)
            after, before = lax.rem(place2[o] + 1, 4), lax.rem(place2[o] + 3, 4)
            plan = (
                (far_block, 0, forward2[o]),
                (far_block, 1, backward2[o]),
                (after, 1, forward2[o]),
                (before, 0, backward2[o]),
                (after, 0, forward2[o]),
                (before, 1, backward2[o]),
            )
            per2.append(
                [
                    remote(
                        passed.at[slot, o, block, half, :, cols],
                        got2.at[slot, o, i, :, cols],
                        s2.at[slot, o, i],
                        r2.at[slot, o, i],
                        partner,
                    )
                    for i, (block, half, partner) in enumerate(plan)
                ]
            )
            per3.append(
                remote(
                    keep.at[slot, o, 1 - z_lo, :, cols],
                    got3.at[slot, o, :, cols],
                    s3.at[slot, o],
                    r3.at[slot, o],
                    beside,
                )
            )
        first.append(per1)
        second.append(per2)
        third.append(per3)

    def multiply(k):
        slot, width = k % 2, CHUNKS[k][3]
        right_copies[k].wait()
        if k == 0 or left_at[k] != left_at[k - 1]:
            left_copies[left_at[k]].wait()
        if k + 1 < count:
            right_copies[k + 1].start()
        if (k == 0 or left_at[k] != left_at[k - 1]) and left_at[k] + 1 < len(left_order):
            left_copies[left_at[k] + 1].start()
        if k >= 2:
            for o in range(2):
                for copy in first[k - 2][o]:
                    copy.wait_send()

        def block(b, carry):
            rows = pl.ds(pl.multiple_of(b * 384, 384), 384)
            for at in range(0, width, 256):
                size = min(256, width - at)
                cols = pl.ds(at, size)
                tile = jnp.dot(
                    left_buf[left_at[k] % 2, rows, :],
                    right_buf[slot, :, cols],
                    preferred_element_type=F32,
                )
                for q in range(8):
                    product[slot, 0, b, pl.ds(24 * q, 24), cols] = tile[48 * q : 48 * q + 24]
                    to = pl.ds(pl.multiple_of(48 * b + 24 * (q % 2), 24), 24)
                    product[slot, 1, q // 2, to, cols] = tile[48 * q + 24 : 48 * q + 48]
            return carry

        lax.fori_loop(0, 4, block, 0)
        if k >= 2:
            for d in range(4):
                pl.semaphore_wait(credit.at[d], 1)
        for o in range(2):
            for i in range(4):
                first[k][o][i].start()

    def relay(k):
        slot, width = k % 2, CHUNKS[k][3]
        cols = pl.ds(0, width)
        for o in range(2):
            for i, shift, base in ((0, 1, 0), (1, 3, 96)):
                first[k][o][i].wait_recv()
                b = lax.rem(place1[o] + shift, 4)

                def add(r, o=o, i=i, b=b, base=base):
                    to = pl.ds(pl.multiple_of(r.start + base, 8), r.size)
                    product[slot, o, b, to, cols] = (
                        product[slot, o, b, to, cols] + got[slot, o, i, r, cols]
                    )

                by_rows(96, 8, add)
                first[k][o][4 + i].start()

    def turn(k):
        slot, width = k % 2, CHUNKS[k][3]
        cols = pl.ds(0, width)
        for o in range(2):
            for base, i, j in ((0, 3, 4), (96, 2, 5)):
                first[k][o][i].wait_recv()
                first[k][o][j].wait_recv()
            b = place1[o]
            for q in range(4):
                for h in range(2):
                    row = 48 * q + 24 * h
                    i, j, at = (3, 4, row) if row < 96 else (2, 5, row - 96)

                    def add(r, o=o, b=b, q=q, h=h, row=row, i=i, j=j, at=at):
                        mine = pl.ds(pl.multiple_of(r.start + row, 8), r.size)
                        theirs = pl.ds(pl.multiple_of(r.start + at, 8), r.size)
                        passed[slot, o, q, h, r, cols] = (
                            product[slot, o, b, mine, cols]
                            + got[slot, o, i, theirs, cols]
                            + got[slot, o, j, theirs, cols]
                        )

                    by_rows(24, 8, add)
            if k >= 2:
                for d in ((YP, YM), (XP, XM))[o]:
                    pl.semaphore_wait(credit2.at[d], 1)
            for i in range(4):
                second[k][o][i].start()
        if k + 2 < count:
            for d in range(4):
                pl.semaphore_signal(
                    credit.at[OPPOSITE[d]], inc=1, device_id=around[d], device_id_type=MESH
                )

    def relay2(k):
        slot, width = k % 2, CHUNKS[k][3]
        cols = pl.ds(0, width)
        for o in range(2):
            for i, shift in ((0, 1), (1, 3)):
                second[k][o][i].wait_recv()
                b = lax.rem(place2[o] + shift, 4)
                passed[slot, o, b, i, :, cols] = (
                    passed[slot, o, b, i, :, cols] + got2[slot, o, i, :, cols]
                )
                second[k][o][4 + i].start()

    def turn2(k):
        slot, width = k % 2, CHUNKS[k][3]
        cols = pl.ds(0, width)
        for o in range(2):
            b = place2[o]
            for h, i, j in ((0, 3, 4), (1, 2, 5)):
                second[k][o][i].wait_recv()
                second[k][o][j].wait_recv()
                keep[slot, o, h, :, cols] = (
                    passed[slot, o, b, h, :, cols]
                    + got2[slot, o, i, :, cols]
                    + got2[slot, o, j, :, cols]
                )
        if k >= 2:
            pl.semaphore_wait(credit3, 1)
        for o in range(2):
            third[k][o].start()
        if k + 2 < count:
            for d in range(4):
                pl.semaphore_signal(
                    credit2.at[OPPOSITE[d]], inc=1, device_id=around[d], device_id_type=MESH
                )
        for o in range(2):
            for copy in second[k][o]:
                copy.wait_send()

    def finish(k):
        slot, (_, _, start, width, which) = k % 2, CHUNKS[k]
        cols = pl.ds(0, width)
        for o in range(2):
            third[k][o].wait_recv()
            grads[which][pl.ds(24 * o, 24), pl.ds(start, width)] = (
                keep[slot, o, z_lo, :, cols] + got3[slot, o, :, cols]
            )
            third[k][o].wait_send()
        if k + 2 < count:
            pl.semaphore_signal(credit3, inc=1, device_id=beside, device_id_type=MESH)

    parts = (dh1_part, ffn_part)
    loads = [pltpu.make_async_copy(parts[a].at[core], sum_own.at[a], load_sem.at[a]) for a in range(2)]
    near = [
        remote(parts[a].at[1 - core], sum_near.at[a], sum_s.at[a, 0], sum_r.at[a, 0], mate)
        for a in range(2)
    ]
    far = [
        remote(sum_own.at[a], sum_far.at[a], sum_s.at[a, 1], sum_r.at[a, 1], across)
        for a in range(2)
    ]
    back = [
        remote(sum_near.at[a], sum_back.at[a], sum_s.at[a, 2], sum_r.at[a, 2], mate)
        for a in range(2)
    ]

    def sum_begin(a):
        loads[a].start()
        near[a].start()

    def sum_cross(a):
        loads[a].wait()
        near[a].wait_recv()

        def add(r):
            sum_own[a, r] = sum_own[a, r] + sum_near[a, r]

        by_rows(HALF, 16, add)
        far[a].start()

    def tokens_end():
        far[0].wait_recv()
        small[0, pl.ds(24, 8), :] = jnp.zeros((8, 128), F32)

        def norm(r, acc):
            value = tokens[core, r].astype(F32)
            total = sum_own[0, r] + sum_far[0, r]
            inverse = lax.rsqrt(jnp.mean(value * value, axis=-1, keepdims=True) + EPSILON)
            scaled = total * gain[...]
            grad = (
                dx1[r]
                + inverse * scaled
                - value * inverse**3 * jnp.mean(scaled * value, axis=-1, keepdims=True)
            )
            dg = total * value * inverse
            low = grad.astype(BF16)
            grad_tokens[core, r] = low
            sum_near[0, r] = low.astype(F32)
            return acc + dg[0:8] + dg[8:16]

        def body(i, acc):
            return norm(pl.ds(pl.multiple_of(i * 16, 16), 16), acc)

        acc = lax.fori_loop(0, HALF // 16, body, jnp.zeros((8, WIDTH), F32))
        back[0].start()
        row = jnp.sum(acc, axis=0, keepdims=True) * 0.5
        for i in range(12):
            small[0, pl.ds(1 + i, 1), :] = row[:, 128 * i : 128 * i + 128]
        small[0, pl.ds(0, 1), :] = small_in[pl.ds(0, 1), :]
        for i in range(13, 32):
            small[0, pl.ds(i, 1), :] = small_in[pl.ds(i, 1), :]

    def out_end():
        far[1].wait_recv()

        def add(r):
            low = (x1[r] + (sum_own[1, r] + sum_far[1, r])).astype(BF16)
            block_out[core, r] = low
            sum_near[1, r] = low.astype(F32)

        by_rows(HALF, 16, add)
        back[1].start()

    def sum_end(a):
        result = (grad_tokens, block_out)[a]
        back[a].wait_recv()

        def add(r):
            result[1 - core, r] = sum_back[a, r].astype(BF16)

        by_rows(HALF, 16, add)
        for copy in (near[a], far[a], back[a]):
            copy.wait_send()

    spots = (x, y, z, core)
    small_copies = []
    for p in range(4):
        small_copies.append(
            [
                remote(
                    small.at[p],
                    small_got.at[p, spots[p]],
                    small_s.at[p, i],
                    small_r.at[p, i],
                    partner,
                )
                for i, partner in enumerate(ring[p])
            ]
        )

    def small_begin(p):
        for copy in small_copies[p]:
            copy.start()
        small_got[p, spots[p]] = small[p]

    def small_end(p):
        for copy in small_copies[p]:
            copy.wait_recv()
        total = small_got[p, 0] + small_got[p, 1]
        if p < 3:
            total = total + small_got[p, 2] + small_got[p, 3]
            small[p + 1] = total
        else:
            small_out[...] = total
        for copy in small_copies[p]:
            copy.wait_send()

    jobs = {
        0: [lambda: sum_begin(0)],
        1: [lambda: sum_cross(0), lambda: sum_begin(1)],
        3: [tokens_end, lambda: sum_cross(1), lambda: small_begin(0)],
        4: [lambda: sum_end(0), lambda: small_end(0), lambda: small_begin(1)],
        5: [lambda: small_end(1), lambda: small_begin(2), out_end],
        6: [lambda: small_end(2), lambda: small_begin(3), lambda: sum_end(1)],
        7: [lambda: small_end(3)],
    }

    left_copies[0].start()
    right_copies[0].start()
    for k in range(count + 3):
        if k < count:
            multiply(k)
        for job in jobs.get(k, ()):
            job()
        if 0 <= k - 1 < count:
            turn(k - 1)
        if k < count:
            relay(k)
        if 0 <= k - 2 < count:
            turn2(k - 2)
        if 0 <= k - 1 < count:
            relay2(k - 1)
        if 0 <= k - 3 < count:
            finish(k - 3)
    for k in (count - 2, count - 1):
        for o in range(2):
            for copy in first[k][o]:
                copy.wait_send()


def scatter(lefts, rights, ffn_part, dh1_part, x1, dx1, tokens, gain, small_in):
    vmem = pl.BlockSpec(memory_space=pltpu.VMEM)
    anywhere = pl.BlockSpec(memory_space=pl.ANY)
    dma = pltpu.SemaphoreType.DMA
    outs = pl.pallas_call(
        scatter_kernel,
        out_shape=tuple(jax.ShapeDtypeStruct((48, width), F32) for width in WIDTHS)
        + (
            jax.ShapeDtypeStruct((2, HALF, WIDTH), BF16),
            jax.ShapeDtypeStruct((2, HALF, WIDTH), BF16),
            jax.ShapeDtypeStruct((32, 128), F32),
        ),
        in_specs=[anywhere] * 10 + [vmem] * 5,
        out_specs=(vmem,) * 7,
        scratch_shapes=[
            pltpu.VMEM((2, WIDTH, TOK), BF16),
            pltpu.VMEM((2, TOK, CMAX), BF16),
            pltpu.VMEM((2, 2, 4, 192, CMAX), F32),
            pltpu.VMEM((2, 2, 6, 96, CMAX), F32),
            pltpu.VMEM((2, 2, 4, 2, 24, CMAX), F32),
            pltpu.VMEM((2, 2, 6, 24, CMAX), F32),
            pltpu.VMEM((2, 2, 2, 24, CMAX), F32),
            pltpu.VMEM((2, 2, 24, CMAX), F32),
            pltpu.VMEM((2, HALF, WIDTH), F32),
            pltpu.VMEM((2, HALF, WIDTH), F32),
            pltpu.VMEM((2, HALF, WIDTH), F32),
            pltpu.VMEM((2, HALF, WIDTH), F32),
            pltpu.VMEM((4, 32, 128), F32),
            pltpu.VMEM((4, 4, 32, 128), F32),
            dma((2,)),
            dma((2,)),
            dma((2, 2, 6)),
            dma((2, 2, 6)),
            dma((2, 2, 6)),
            dma((2, 2, 6)),
            dma((2, 2)),
            dma((2, 2)),
            pltpu.SemaphoreType.REGULAR((4,)),
            pltpu.SemaphoreType.REGULAR((4,)),
            pltpu.SemaphoreType.REGULAR,
            dma((2,)),
            dma((2, 3)),
            dma((2, 3)),
            dma((4, 3)),
            dma((4, 3)),
        ],
        compiler_params=pltpu.CompilerParams(
            collective_id=0, has_side_effects=True, vmem_limit_bytes=60 * MIB
        ),
        name="scatter",
    )(
        *lefts,
        *rights,
        ffn_part.reshape(2, HALF, WIDTH),
        dh1_part.reshape(2, HALF, WIDTH),
        x1,
        dx1,
        tokens.reshape(2, HALF, WIDTH),
        gain.reshape(1, WIDTH),
        small_in,
    )
    return outs


def per_device(
    tokens,
    segments,
    norm_one,
    w_query,
    key_projection,
    value_projection,
    w_out,
    q_gain,
    k_gain,
    norm_two,
    w_gate,
    w_up,
    w_down,
    cotangent,
):
    sequence_count, sequence_length = segments.shape
    token_count = tokens.shape[0]
    heads_local = w_query.shape[1] // HEAD_SIZE
    groups_local = key_projection.shape[1] // HEAD_SIZE
    group_count = QUERY_HEADS // KEY_VALUE_HEADS
    scale = HEAD_SIZE ** (-0.5)
    cosine_table, sine_table, allowed = rope_tables(segments)
    cosine_table = cosine_table[:, :, None, :]
    sine_table = sine_table[:, :, None, :]
    mask_full = allowed[:, None, None]
    tokens_f = tokens.astype(jnp.float32)
    first_hidden, inv_one = norm_rows(tokens_f, norm_one)
    hidden_one_low = first_hidden.astype(jnp.bfloat16)
    query_unrotated = jnp.dot(hidden_one_low, w_query, preferred_element_type=jnp.float32).reshape(
        sequence_count, sequence_length, heads_local, HEAD_SIZE
    )
    key_unrotated = jnp.dot(
        hidden_one_low, key_projection, preferred_element_type=jnp.float32
    ).reshape(sequence_count, sequence_length, groups_local, HEAD_SIZE)
    value_low = (
        jnp.dot(hidden_one_low, value_projection, preferred_element_type=jnp.float32)
        .astype(jnp.bfloat16)
        .reshape(sequence_count, sequence_length, groups_local, HEAD_SIZE)
    )
    query_norm, query_inv = norm_rows(query_unrotated, q_gain)
    key_norm, key_inv = norm_rows(key_unrotated, k_gain)
    query_low = (
        apply_rotary(query_norm, cosine_table, sine_table)
        .astype(jnp.bfloat16)
        .reshape(sequence_count, sequence_length, groups_local, group_count, HEAD_SIZE)
    )
    key_low = apply_rotary(key_norm, cosine_table, sine_table).astype(jnp.bfloat16)
    scores = (
        jnp.einsum("sqhgd,skhd->shgqk", query_low, key_low, preferred_element_type=jnp.float32)
        * scale
    )
    scores = jnp.where(mask_full, scores, -1e30)
    highest = jnp.max(scores, axis=-1, keepdims=True)
    expo_scores = jnp.exp(scores - highest)
    probs = expo_scores / jnp.sum(expo_scores, axis=-1, keepdims=True)
    probs_low = probs.astype(jnp.bfloat16)
    mixed = jnp.einsum(
        "shgqk,skhd->sqhgd", probs_low, value_low, preferred_element_type=jnp.float32
    )
    mixed_low = mixed.reshape(token_count, heads_local * HEAD_SIZE).astype(jnp.bfloat16)
    attn_part = jnp.dot(mixed_low, w_out, preferred_element_type=jnp.float32)
    x1, hidden_two_low = attention_sum(attn_part, tokens, norm_two)
    gate = jnp.dot(hidden_two_low, w_gate, preferred_element_type=jnp.float32)
    upper = jnp.dot(hidden_two_low, w_up, preferred_element_type=jnp.float32)
    sigmoid_gate = jax.nn.sigmoid(gate)
    silu_gate = gate * sigmoid_gate
    activ_low = (silu_gate * upper).astype(jnp.bfloat16)
    ffn_part = jnp.dot(activ_low, w_down, preferred_element_type=jnp.float32)
    grad_activ = jnp.einsum("td,fd->tf", cotangent, w_down, preferred_element_type=jnp.float32)
    grad_gate_in = (grad_activ * upper * sigmoid_gate * (1.0 + gate * (1.0 - sigmoid_gate))).astype(
        jnp.bfloat16
    )
    grad_up_in = (grad_activ * silu_gate).astype(jnp.bfloat16)
    hidden_two_part = jnp.einsum(
        "tf,df->td", grad_gate_in, w_gate, preferred_element_type=jnp.float32
    ) + jnp.einsum("tf,df->td", grad_up_in, w_up, preferred_element_type=jnp.float32)
    dx1, grad_attn_low, norm_two_part = hidden_sum(hidden_two_part, x1, cotangent, norm_two)
    grad_mixed = jnp.einsum("td,ad->ta", grad_attn_low, w_out, preferred_element_type=jnp.float32)
    grad_mixed_low = grad_mixed.astype(jnp.bfloat16).reshape(
        sequence_count, sequence_length, groups_local, group_count, HEAD_SIZE
    )
    grad_probs = jnp.einsum(
        "sqhgd,skhd->shgqk", grad_mixed_low, value_low, preferred_element_type=jnp.float32
    )
    grad_values = jnp.einsum(
        "shgqk,sqhgd->skhd", probs_low, grad_mixed_low, preferred_element_type=jnp.float32
    )
    grad_values_low = grad_values.reshape(token_count, groups_local * HEAD_SIZE).astype(
        jnp.bfloat16
    )
    grad_scores = probs * (grad_probs - jnp.sum(probs * grad_probs, axis=-1, keepdims=True))
    grad_scores_low = grad_scores.astype(jnp.bfloat16)
    grad_query_rot = (
        jnp.einsum(
            "shgqk,skhd->sqhgd", grad_scores_low, key_low, preferred_element_type=jnp.float32
        )
        * scale
    )
    grad_key_rot = (
        jnp.einsum(
            "shgqk,sqhgd->skhd", grad_scores_low, query_low, preferred_element_type=jnp.float32
        )
        * scale
    )
    grad_query_norm = rotate_back(
        grad_query_rot.reshape(sequence_count, sequence_length, heads_local, HEAD_SIZE),
        cosine_table,
        sine_table,
    )
    grad_key_norm = rotate_back(grad_key_rot, cosine_table, sine_table)
    grad_query_raw, grad_q_part = norm_back(query_unrotated, query_inv, q_gain, grad_query_norm)
    grad_key_raw, grad_k_part = norm_back(key_unrotated, key_inv, k_gain, grad_key_norm)
    grad_query_low = grad_query_raw.reshape(token_count, heads_local * HEAD_SIZE).astype(
        jnp.bfloat16
    )
    grad_key_low = grad_key_raw.reshape(token_count, groups_local * HEAD_SIZE).astype(jnp.bfloat16)
    hidden_one_part = (
        jnp.einsum("tc,dc->td", grad_query_low, w_query, preferred_element_type=jnp.float32)
        + jnp.einsum("tc,dc->td", grad_key_low, key_projection, preferred_element_type=jnp.float32)
        + jnp.einsum(
            "tc,dc->td", grad_values_low, value_projection, preferred_element_type=jnp.float32
        )
    )
    small_in = jnp.concatenate(
        [
            jnp.concatenate([grad_q_part, grad_k_part]).reshape(1, 128),
            jnp.zeros((12, 128), F32),
            (jnp.sum(norm_two_part, axis=0) * 0.5).reshape(12, 128),
            jnp.zeros((7, 128), F32),
        ],
        axis=0,
    )
    lefts = (hidden_two_low.T, hidden_one_low.T, grad_attn_low.T, cotangent.T)
    rights = (
        jnp.concatenate([grad_gate_in, grad_up_in], axis=1),
        jnp.concatenate([grad_query_low, grad_key_low, grad_values_low], axis=1),
        mixed_low,
        jnp.pad(activ_low, ((0, 0), (0, 64))),
    )
    gate_up, qkv, out, down, block_out, grad_tokens, small = scatter(
        lefts, rights, ffn_part, hidden_one_part, x1, dx1, tokens, norm_one, small_in
    )
    norms = lax.dynamic_slice_in_dim(
        small[1:25].reshape(2, WIDTH), lax.axis_index("dp") * 48, 48, axis=1
    )
    return (
        block_out.reshape(TOK, WIDTH),
        grad_tokens.reshape(TOK, WIDTH),
        norms[0],
        qkv[:, :384],
        qkv[:, 384:512],
        qkv[:, 512:640],
        out.T,
        small[0, :64],
        small[0, 64:],
        norms[1],
        gate_up[:, :FFL],
        gate_up[:, FFL:],
        down[:, :FFL].T,
    )


def solution(mesh):
    placed = (
        P("dp", None),
        P("dp", None),
        P(),
        P(None, "tensor"),
        P(None, "tensor"),
        P(None, "tensor"),
        P("tensor", None),
        P(),
        P(),
        P(),
        P(None, "tensor"),
        P(None, "tensor"),
        P("tensor", None),
        P("dp", None),
    )
    return jax.shard_map(
        per_device,
        mesh=mesh,
        in_specs=placed,
        out_specs=(
            P("dp", None),
            P("dp", None),
            P("dp"),
            P("dp", "tensor"),
            P("dp", "tensor"),
            P("dp", "tensor"),
            P("tensor", "dp"),
            P(),
            P(),
            P("dp"),
            P("dp", "tensor"),
            P("dp", "tensor"),
            P("tensor", "dp"),
        ),
        check_vma=False,
    )
```

```python
import jax
import jax.numpy as jnp
from jax import lax
from jax.experimental import pallas as pl
from jax.experimental.pallas import tpu as pltpu
from jax.sharding import PartitionSpec as P

QUERY_HEADS = 24
KEY_VALUE_HEADS = 8
HEAD_SIZE = 64


EPSILON = 1e-05
THETA = 1000000.0


def rope_tables(segments):
    sequence_count, sequence_length = segments.shape
    index_row = jnp.arange(sequence_length, dtype=jnp.int32)[None, :]
    change = jnp.concatenate(
        [jnp.ones((sequence_count, 1), jnp.bool_), segments[:, 1:] != segments[:, :-1]], axis=1
    )
    starts = lax.cummax(jnp.where(change, index_row, 0), axis=1)
    position = (index_row - starts).astype(jnp.float32)
    frequency = THETA ** (-jnp.arange(HEAD_SIZE // 2, dtype=jnp.float32) * 2.0 / HEAD_SIZE)
    angles = position[:, :, None] * frequency
    allowed = (segments[:, :, None] == segments[:, None, :]) & (
        index_row[:, :, None] >= index_row[:, None, :]
    )
    return (jnp.cos(angles), jnp.sin(angles), allowed)


def starts_of(segments):
    row = segments[0]
    return jnp.sum(row[None, :] < row[:, None], axis=1, dtype=jnp.int32).reshape(-1, 1)


def lane_tables(cosine, sine):
    none = jnp.zeros_like(sine)
    return (
        jnp.concatenate([cosine] * 4, axis=1),
        jnp.concatenate([-sine, none] * 2, axis=1),
        jnp.concatenate([none, sine] * 2, axis=1),
    )


def apply_rotary(values, cosine_table, sine_table):
    first, second = jnp.split(values, 2, axis=-1)
    return jnp.concatenate(
        [first * cosine_table - second * sine_table, second * cosine_table + first * sine_table],
        axis=-1,
    )


def norm_rows(values, gain):
    inverse = lax.rsqrt(jnp.mean(values * values, axis=-1, keepdims=True) + EPSILON)
    return (values * inverse * gain, inverse)


MESH = pl.DeviceIdType.MESH
F32 = jnp.float32
BF16 = jnp.bfloat16
WIDTH = 1536
TOK = 512
HALF = 256
FFL = 1728
MIB = 1 << 20


def place():
    dp = lax.axis_index("dp")
    tensor = lax.axis_index("tensor")
    x = lax.div(dp, 8)
    y = lax.rem(lax.div(dp, 2), 4)
    z = lax.div(tensor, 2) * 2 + lax.rem(dp, 2)
    return x, y, z, lax.rem(tensor, 2)


def device(x, y, z, core):
    return (x * 8 + y * 2 + lax.rem(z, 2), lax.div(z, 2) * 2 + core)


def greet(partners):
    barrier = pltpu.get_barrier_semaphore()
    for partner in partners:
        pl.semaphore_signal(barrier, inc=1, device_id=partner, device_id_type=MESH)
    pl.semaphore_wait(barrier, len(partners))


def remote(source, target, send_sem, recv_sem, partner):
    return pltpu.make_async_remote_copy(
        src_ref=source,
        dst_ref=target,
        send_sem=send_sem,
        recv_sem=recv_sem,
        device_id=partner,
        device_id_type=MESH,
    )


def by_rows(count, step, work):
    def body(i, carry):
        work(pl.ds(pl.multiple_of(i * step, step), step))
        return carry

    lax.fori_loop(0, count // step, body, 0)


PARTS = 4
PART = HALF // PARTS


def start_norm_kernel(
    part, tokens, gain, x1_out, h2_out, own, near, far, back, fin, sems, near_s, near_r, far_s, far_r, back_s, back_r
):
    x, y, z, core = place()
    mate = device(x, y, z, 1 - core)
    across = device(x, y, lax.rem(z + 2, 4), core)
    greet([mate, across])
    load = pltpu.make_async_copy(part.at[core], own, sems)
    load.start()
    first, second, third = [], [], []
    for j in range(PARTS):
        rows = pl.ds(j * PART, PART)
        copy = remote(part.at[1 - core, rows], near.at[rows], near_s.at[j], near_r.at[j], mate)
        copy.start()
        first.append(copy)
    load.wait()
    for j in range(PARTS):
        rows = pl.ds(j * PART, PART)
        first[j].wait_recv()

        def add(r, j=j):
            r = pl.ds(r.start + j * PART, r.size)
            own[r] = own[r] + near[r]

        by_rows(PART, 16, add)
        copy = remote(own.at[rows], far.at[rows], far_s.at[j], far_r.at[j], across)
        copy.start()
        second.append(copy)
    for j in range(PARTS):
        rows = pl.ds(j * PART, PART)
        second[j].wait_recv()

        def norm(r, j=j):
            r = pl.ds(pl.multiple_of(r.start + j * PART, 16), r.size)
            value = tokens[core, r].astype(F32) + (own[r] + far[r])
            inverse = lax.rsqrt(jnp.mean(value * value, axis=-1, keepdims=True) + EPSILON)
            low = (value * inverse * gain[...]).astype(BF16)
            x1_out[r] = value
            h2_out[core, r] = low
            fin[r] = low.astype(F32)

        by_rows(PART, 16, norm)
        copy = remote(fin.at[rows], back.at[rows], back_s.at[j], back_r.at[j], mate)
        copy.start()
        third.append(copy)
    for j in range(PARTS):
        third[j].wait_recv()

        def keep(r, j=j):
            r = pl.ds(pl.multiple_of(r.start + j * PART, 16), r.size)
            h2_out[1 - core, r] = back[r].astype(BF16)

        by_rows(PART, 16, keep)
    for copy in first + second + third:
        copy.wait_send()


def sum_scratch():
    return [pltpu.VMEM((HALF, WIDTH), F32)] * 5 + [pltpu.SemaphoreType.DMA] + [
        pltpu.SemaphoreType.DMA((PARTS,))
    ] * 6


def attention_sum(part, tokens, gain):
    vmem = pl.BlockSpec(memory_space=pltpu.VMEM)
    x1, h2 = pl.pallas_call(
        start_norm_kernel,
        out_shape=(
            jax.ShapeDtypeStruct((HALF, WIDTH), F32),
            jax.ShapeDtypeStruct((2, HALF, WIDTH), BF16),
        ),
        in_specs=[pl.BlockSpec(memory_space=pl.ANY), vmem, vmem],
        out_specs=(vmem, vmem),
        scratch_shapes=sum_scratch(),
        compiler_params=pltpu.CompilerParams(
            collective_id=1, has_side_effects=True, vmem_limit_bytes=40 * MIB
        ),
        name="attention_sum",
    )(part.reshape(2, HALF, WIDTH), tokens.reshape(2, HALF, WIDTH), gain.reshape(1, WIDTH))
    return x1, h2.reshape(TOK, WIDTH)


CMAX = 640
H2, COT, H1, DA = range(4)
GU, ACT, QKV, MIX = range(4)
CHUNKS = (
    (H2, GU, 0, 640),
    (H2, GU, 640, 640),
    (H2, GU, 1280, 640),
    (H2, GU, 1920, 512),
    (H2, GU, 2432, 512),
    (H2, GU, 2944, 512),
    (COT, ACT, 0, 640),
    (COT, ACT, 640, 640),
    (COT, ACT, 1280, 512),
    (H1, QKV, 0, 640),
    (DA, MIX, 0, 384),
)
WIDTHS = (3456, 1792, 640, 384)
XP, XM, YP, YM = range(4)
OPPOSITE = (XM, XP, YM, YP)
SCALE = HEAD_SIZE ** (-0.5)
HIGHEST = lax.Precision.HIGHEST


def dot_nt(left, right):
    return lax.dot_general(left, right, (((1,), (1,)), ((), ())), preferred_element_type=F32)


def dot_tn(left, right):
    return lax.dot_general(left, right, (((0,), (0,)), ((), ())), preferred_element_type=F32)


def head_mean(values):
    row = lax.broadcasted_iota(jnp.int32, (128, 128), 0)
    col = lax.broadcasted_iota(jnp.int32, (128, 128), 1)
    same = jnp.where((row < 64) == (col < 64), 1.0 / 64, 0.0)
    return jnp.concatenate(
        [
            jnp.dot(
                values[:, at : at + 128], same, precision=HIGHEST, preferred_element_type=F32
            )
            for at in range(0, values.shape[1], 128)
        ],
        axis=1,
    )


def turned(values, cos, sin_a, sin_b, sign):
    width = values.shape[1]
    copies = width // 128
    cos, sin_a, sin_b = (jnp.concatenate([t] * copies, axis=1) for t in (cos, sin_a, sin_b))
    ahead = pltpu.roll(values, width - 32, 1)
    behind = pltpu.roll(values, 32, 1)
    return values * cos + sign * (ahead * sin_a + behind * sin_b)


def backward_kernel(*refs):
    h2, cot, h1, gu, act, dh2_part, ffn_part, tokens, refs = *refs[:8], refs[8:]
    x1, gain1, gain2, q_gain, k_gain, qraw, kraw, vals, mixed, refs = *refs[:9], refs[9:]
    cos, sin_a, sin_b, begin, w_out, w_q, w_k, w_v, refs = *refs[:8], refs[8:]
    grads, block_out, grad_tokens, small_out, refs = refs[:4], refs[4], refs[5], refs[6], refs[7:]
    left_raw, left_t, right_buf, product, got, passed, got2, keep, got3, refs = *refs[:9], refs[9:]
    sum_own, sum_near, sum_far, sum_back, dh1_other, refs = *refs[:5], refs[5:]
    small, small_got, dx1, da, cot_own, tok_own, refs = *refs[:6], refs[6:]
    qr, kr, dmixed, dqr, dk_t, dv_t, dqkv, gain_acc, refs = *refs[:8], refs[8:]
    left_sem, right_sem, s1, r1, s2, r2, s3, r3, credit, credit2, credit3, refs = *refs[:11], refs[11:]
    load_sem, sum_s, sum_r, free, small_s, small_r = refs

    x, y, z, core = place()
    around = (
        device(lax.rem(x + 1, 4), y, z, core),
        device(lax.rem(x + 3, 4), y, z, core),
        device(x, lax.rem(y + 1, 4), z, core),
        device(x, lax.rem(y + 3, 4), z, core),
    )
    z_lo = lax.rem(z, 2)
    beside = device(x, y, z + 1 - 2 * z_lo, core)
    mate = device(x, y, z, 1 - core)
    across = device(x, y, lax.rem(z + 2, 4), core)
    ring = (
        [device(lax.rem(x + i, 4), y, z, core) for i in (1, 2, 3)],
        [device(x, lax.rem(y + i, 4), z, core) for i in (1, 2, 3)],
        [device(x, y, lax.rem(z + i, 4), core) for i in (1, 2, 3)],
        [mate],
    )
    greet([one for group in ring for one in group])

    count = len(CHUNKS)
    place1, place2 = (x, y), (y, x)
    forward1, backward1 = (around[XP], around[YP]), (around[XM], around[YM])
    forward2, backward2 = (around[YP], around[XP]), (around[YM], around[XM])

    left_copies = {
        which: pltpu.make_async_copy(source, left_raw, left_sem)
        for which, source in ((H2, h2), (COT, cot), (H1, h1))
    }
    right_copies = {
        k: pltpu.make_async_copy(
            (gu, act)[chunk[1]].at[:, pl.ds(chunk[2], chunk[3])],
            right_buf.at[k % 2, :, pl.ds(0, chunk[3])],
            right_sem.at[k % 2],
        )
        for k, chunk in enumerate(CHUNKS)
        if chunk[1] in (GU, ACT)
    }

    def new_left(k):
        return k == 0 or CHUNKS[k][0] != CHUNKS[k - 1][0]

    first, second, third = [], [], []
    for k, chunk in enumerate(CHUNKS):
        slot, cols = k % 2, pl.ds(0, chunk[3])
        per1, per2, per3 = [], [], []
        for o in range(2):
            far_block = lax.rem(place1[o] + 2, 4)
            after, before = lax.rem(place1[o] + 1, 4), lax.rem(place1[o] + 3, 4)
            top, low = pl.ds(0, 96), pl.ds(96, 96)
            plan = (
                (far_block, top, forward1[o]),
                (far_block, low, backward1[o]),
                (after, low, forward1[o]),
                (before, top, backward1[o]),
                (after, top, forward1[o]),
                (before, low, backward1[o]),
            )
            per1.append(
                [
                    remote(
                        product.at[slot, o, block, rows, cols],
                        got.at[slot, o, i, :, cols],
                        s1.at[slot, o, i],
                        r1.at[slot, o, i],
                        partner,
                    )
                    for i, (block, rows, partner) in enumerate(plan)
                ]
            )
            far_block = lax.rem(place2[o] + 2, 4)
            after, before = lax.rem(place2[o] + 1, 4), lax.rem(place2[o] + 3, 4)
            plan = (
                (far_block, 0, forward2[o]),
                (far_block, 1, backward2[o]),
                (after, 1, forward2[o]),
                (before, 0, backward2[o]),
                (after, 0, forward2[o]),
                (before, 1, backward2[o]),
            )
            per2.append(
                [
                    remote(
                        passed.at[slot, o, block, half, :, cols],
                        got2.at[slot, o, i, :, cols],
                        s2.at[slot, o, i],
                        r2.at[slot, o, i],
                        partner,
                    )
                    for i, (block, half, partner) in enumerate(plan)
                ]
            )
            per3.append(
                remote(
                    keep.at[slot, o, 1 - z_lo, :, cols],
                    got3.at[slot, o, :, cols],
                    s3.at[slot, o],
                    r3.at[slot, o],
                    beside,
                )
            )
        first.append(per1)
        second.append(per2)
        third.append(per3)

    def multiply(k):
        slot, (left, right, _, width) = k % 2, CHUNKS[k]
        if new_left(k):
            if left == DA:
                for half in range(2):
                    for at in range(0, WIDTH, 384):
                        left_t[pl.ds(at, 384), pl.ds(HALF * half, HALF)] = da[
                            half, :, pl.ds(at, 384)
                        ].T
            else:
                left_copies[left].wait()
                for at in range(0, WIDTH, 384):
                    left_t[pl.ds(at, 384), :] = left_raw[:, pl.ds(at, 384)].T
                if left in (H2, COT):
                    left_copies[(COT, H1)[left]].start()
        if k + 1 in right_copies:
            right_copies[k + 1].start()
        if k in right_copies:
            right_copies[k].wait()
        if k >= 2:
            for o in range(2):
                for copy in first[k - 2][o]:
                    copy.wait_send()

        def block(b, carry):
            rows = pl.ds(pl.multiple_of(b * 384, 384), 384)
            for at in range(0, width, 256):
                size = min(256, width - at)
                cols = pl.ds(at, size)
                if right == QKV:
                    operand = dqkv[:, cols]
                elif right == MIX:
                    operand = mixed[:, cols]
                else:
                    operand = right_buf[slot, :, cols]
                tile = jnp.dot(left_t[rows, :], operand, preferred_element_type=F32)
                for q in range(8):
                    product[slot, 0, b, pl.ds(24 * q, 24), cols] = tile[48 * q : 48 * q + 24]
                    to = pl.ds(pl.multiple_of(48 * b + 24 * (q % 2), 24), 24)
                    product[slot, 1, q // 2, to, cols] = tile[48 * q + 24 : 48 * q + 48]
            return carry

        lax.fori_loop(0, 4, block, 0)
        if k >= 2:
            for d in range(4):
                pl.semaphore_wait(credit.at[d], 1)
        for i in range(4):
            for o in range(2):
                first[k][o][i].start()

    def relay(k):
        slot, width = k % 2, CHUNKS[k][3]
        cols = pl.ds(0, width)
        for i, shift, base in ((0, 1, 0), (1, 3, 96)):
            for o in range(2):
                first[k][o][i].wait_recv()
                b = lax.rem(place1[o] + shift, 4)

                def add(r, o=o, i=i, b=b, base=base):
                    to = pl.ds(pl.multiple_of(r.start + base, 8), r.size)
                    product[slot, o, b, to, cols] = (
                        product[slot, o, b, to, cols] + got[slot, o, i, r, cols]
                    )

                by_rows(96, 24, add)
                first[k][o][4 + i].start()

    def turn(k):
        slot, width = k % 2, CHUNKS[k][3]
        cols = pl.ds(0, width)
        for o in range(2):
            for i in range(2, 6):
                first[k][o][i].wait_recv()
            b = place1[o]

            def add(q, carry, o=o, b=b):
                for h in range(2):
                    for half, i, j in ((0, 3, 4), (1, 2, 5)):
                        mine = pl.ds(pl.multiple_of(96 * half + 48 * q + 24 * h, 8), 24)
                        theirs = pl.ds(pl.multiple_of(48 * q + 24 * h, 8), 24)
                        passed[slot, o, 2 * half + q, h, :, cols] = (
                            product[slot, o, b, mine, cols]
                            + got[slot, o, i, theirs, cols]
                            + got[slot, o, j, theirs, cols]
                        )
                return carry

            lax.fori_loop(0, 2, add, 0)
            if k >= 2:
                for d in ((YP, YM), (XP, XM))[o]:
                    pl.semaphore_wait(credit2.at[d], 1)
            for i in range(4):
                second[k][o][i].start()
        if k + 2 < count:
            for d in range(4):
                pl.semaphore_signal(
                    credit.at[OPPOSITE[d]], inc=1, device_id=around[d], device_id_type=MESH
                )

    def relay2(k):
        slot, width = k % 2, CHUNKS[k][3]
        cols = pl.ds(0, width)
        for o in range(2):
            for i, shift in ((0, 1), (1, 3)):
                second[k][o][i].wait_recv()
                b = lax.rem(place2[o] + shift, 4)
                passed[slot, o, b, i, :, cols] = (
                    passed[slot, o, b, i, :, cols] + got2[slot, o, i, :, cols]
                )
                second[k][o][4 + i].start()

    def turn2(k):
        slot, width = k % 2, CHUNKS[k][3]
        cols = pl.ds(0, width)
        for o in range(2):
            b = place2[o]
            for h, i, j in ((0, 3, 4), (1, 2, 5)):
                second[k][o][i].wait_recv()
                second[k][o][j].wait_recv()
                keep[slot, o, h, :, cols] = (
                    passed[slot, o, b, h, :, cols]
                    + got2[slot, o, i, :, cols]
                    + got2[slot, o, j, :, cols]
                )
        if k >= 2:
            pl.semaphore_wait(credit3, 1)
        for o in range(2):
            third[k][o].start()
        if k + 2 < count:
            for d in range(4):
                pl.semaphore_signal(
                    credit2.at[OPPOSITE[d]], inc=1, device_id=around[d], device_id_type=MESH
                )
        for o in range(2):
            for copy in second[k][o]:
                copy.wait_send()

    def finish(k):
        slot, (_, which, start, width) = k % 2, CHUNKS[k]
        cols = pl.ds(0, width)
        for o in range(2):
            third[k][o].wait_recv()
            grads[which][pl.ds(24 * o, 24), pl.ds(start, width)] = (
                keep[slot, o, z_lo, :, cols] + got3[slot, o, :, cols]
            )
            third[k][o].wait_send()
        if k + 2 < count:
            pl.semaphore_signal(credit3, inc=1, device_id=beside, device_id_type=MESH)

    sets = (0, 1, 0)
    sources = (dh2_part.at[1 - core], ffn_part.at[1 - core], dh1_other)
    loads = [
        pltpu.make_async_copy((dh2_part, ffn_part)[a].at[core], sum_own.at[a], load_sem.at[a])
        for a in range(2)
    ]
    near = [
        remote(sources[a], sum_near.at[sets[a]], sum_s.at[a, 0], sum_r.at[a, 0], mate)
        for a in range(3)
    ]
    far = [
        remote(sum_own.at[sets[a]], sum_far.at[sets[a]], sum_s.at[a, 1], sum_r.at[a, 1], across)
        for a in range(3)
    ]
    back = [
        remote(sum_near.at[sets[a]], sum_back.at[sets[a]], sum_s.at[a, 2], sum_r.at[a, 2], mate)
        for a in range(3)
    ]
    side_loads = [
        pltpu.make_async_copy(cot.at[pl.ds(core * HALF, HALF)], cot_own, load_sem.at[2]),
        pltpu.make_async_copy(tokens.at[pl.ds(core * HALF, HALF)], tok_own, load_sem.at[3]),
    ]

    def sum_begin(a):
        loads[a].start()
        near[a].start()

    def sum_cross(a):
        if a < 2:
            loads[a].wait()
        near[a].wait_recv()
        at = sets[a]

        def add(r):
            sum_own[at, r] = sum_own[at, r] + sum_near[at, r]

        by_rows(HALF, 16, add)
        if a == 2:
            pl.semaphore_wait(free.at[1], 1)
        far[a].start()

    def norm_row(row, at):
        for i in range(12):
            small[0, pl.ds(at + i, 1), :] = row[:, 128 * i : 128 * i + 128]

    def hidden_end():
        side_loads[0].wait()
        far[0].wait_recv()

        def body(i, acc):
            r = pl.ds(pl.multiple_of(i * 16, 16), 16)
            value = x1[r]
            total = sum_own[0, r] + sum_far[0, r]
            inverse = lax.rsqrt(jnp.mean(value * value, axis=-1, keepdims=True) + EPSILON)
            scaled = total * gain2[...]
            grad = (
                cot_own[r].astype(F32)
                + inverse * scaled
                - value * inverse**3 * jnp.mean(scaled * value, axis=-1, keepdims=True)
            )
            dg = total * value * inverse
            low = grad.astype(BF16)
            dx1[r] = grad
            da[core, r] = low
            sum_near[0, r] = low.astype(F32)
            return acc + dg[0:8] + dg[8:16]

        acc = lax.fori_loop(0, HALF // 16, body, jnp.zeros((8, WIDTH), F32))
        back[0].start()
        small[0, pl.ds(24, 8), :] = jnp.zeros((8, 128), F32)
        norm_row(jnp.sum(acc, axis=0, keepdims=True) * 0.5, 13)

    def sum_close(a):
        for copy in (near[a], far[a], back[a]):
            copy.wait_send()

    def hidden_take():
        back[0].wait_recv()

        def put(r):
            da[1 - core, r] = sum_back[0, r].astype(BF16)

        by_rows(HALF, 16, put)
        sum_close(0)
        pl.semaphore_signal(free.at[0], inc=1, device_id=mate, device_id_type=MESH)
        pl.semaphore_signal(free.at[1], inc=1, device_id=across, device_id_type=MESH)

    def out_end():
        far[1].wait_recv()

        def add(r):
            low = (x1[r] + (sum_own[1, r] + sum_far[1, r])).astype(BF16)
            block_out[core, r] = low
            sum_near[1, r] = low.astype(F32)

        by_rows(HALF, 16, add)
        back[1].start()

    def out_take():
        back[1].wait_recv()

        def put(r):
            block_out[1 - core, r] = sum_back[1, r].astype(BF16)

        by_rows(HALF, 16, put)
        sum_close(1)

    def tokens_end():
        side_loads[1].wait()
        far[2].wait_recv()

        def body(i, acc):
            r = pl.ds(pl.multiple_of(i * 16, 16), 16)
            value = tok_own[r].astype(F32)
            total = sum_own[0, r] + sum_far[0, r]
            inverse = lax.rsqrt(jnp.mean(value * value, axis=-1, keepdims=True) + EPSILON)
            scaled = total * gain1[...]
            grad = (
                dx1[r]
                + inverse * scaled
                - value * inverse**3 * jnp.mean(scaled * value, axis=-1, keepdims=True)
            )
            dg = total * value * inverse
            low = grad.astype(BF16)
            grad_tokens[core, r] = low
            sum_near[0, r] = low.astype(F32)
            return acc + dg[0:8] + dg[8:16]

        acc = lax.fori_loop(0, HALF // 16, body, jnp.zeros((8, WIDTH), F32))
        back[2].start()
        norm_row(jnp.sum(acc, axis=0, keepdims=True) * 0.5, 1)
        row = gain_acc[...]
        heads = row[:, 0:128] + row[:, 128:256] + row[:, 256:384]
        heads = heads + pltpu.roll(heads, 64, 1)
        groups = row[:, 384:512] + pltpu.roll(row[:, 384:512], 64, 1)
        lane = lax.broadcasted_iota(jnp.int32, (8, 128), 1)
        both = jnp.where(lane < 64, heads, groups)
        small[0, pl.ds(0, 1), :] = jnp.sum(both, axis=0, keepdims=True)

    def tokens_take():
        back[2].wait_recv()

        def put(r):
            grad_tokens[1 - core, r] = sum_back[0, r].astype(BF16)

        by_rows(HALF, 16, put)
        sum_close(2)

    def tables(r):
        return cos[r], sin_a[r], sin_b[r]

    def rotate(r):
        for raw, gain, result in ((qraw, q_gain, qr), (kraw, k_gain, kr)):
            value = raw[r]
            inverse = lax.rsqrt(head_mean(value * value) + EPSILON)
            result[r] = turned(value * inverse * gain[...], *tables(r), 1.0).astype(BF16)

    def mix_back():
        for half in range(2):
            rows = pl.ds(HALF * half, HALF)
            dmixed[rows] = dot_nt(da[half], w_out[...]).astype(BF16)
        dk_t[...] = jnp.zeros((128, TOK), F32)
        dv_t[...] = jnp.zeros((128, TOK), F32)

    def head_back(head):
        group = head // 3
        lanes, glanes = pl.ds(64 * head, 64), pl.ds(64 * group, 64)
        for half in range(2):
            rows, keys = pl.ds(HALF * half, HALF), pl.ds(0, HALF * (half + 1))
            shape = (HALF, HALF * (half + 1))
            q, up = qr[rows, lanes], dmixed[rows, lanes]
            k, v = kr[keys, glanes], vals[keys, glanes]
            row = lax.broadcasted_iota(jnp.int32, shape, 0) + HALF * half
            col = lax.broadcasted_iota(jnp.int32, shape, 1)
            allowed = (col <= row) & (col >= begin[rows])
            scores = jnp.where(allowed, dot_nt(q, k) * SCALE, -1e30)
            expo = jnp.exp(scores - jnp.max(scores, axis=-1, keepdims=True))
            probs = expo / jnp.sum(expo, axis=-1, keepdims=True)
            dprobs = dot_nt(up, v)
            dscores = probs * (dprobs - jnp.sum(probs * dprobs, axis=-1, keepdims=True))
            dscores = dscores.astype(BF16)
            dqr[rows, lanes] = jnp.dot(dscores, k, preferred_element_type=F32) * SCALE
            dk_t[glanes, keys] += dot_tn(q, dscores) * SCALE
            dv_t[glanes, keys] += dot_tn(up, probs.astype(BF16))

    def raw_back():
        dkr = dk_t[...].T
        dqkv[:, pl.ds(512, 128)] = dv_t[...].T.astype(BF16)
        for i in range(4):
            r = pl.ds(128 * i, 128)
            for raw, gain, up, at in (
                (qraw, q_gain, dqr[r], 0),
                (kraw, k_gain, dkr[128 * i : 128 * i + 128], 384),
            ):
                width = up.shape[1]
                value = raw[r]
                up = turned(up, *tables(r), -1.0)
                inverse = lax.rsqrt(head_mean(value * value) + EPSILON)
                scaled = up * gain[...]
                grad = inverse * scaled - value * inverse**3 * head_mean(scaled * value)
                dqkv[r, pl.ds(at, width)] = grad.astype(BF16)
                part = jnp.sum((up * value * inverse).reshape(16, 8, width), axis=0)
                if i == 0:
                    gain_acc[:, pl.ds(at, width)] = part
                else:
                    gain_acc[:, pl.ds(at, width)] += part

    def hidden_back(half):
        rows = pl.ds(pl.multiple_of(half * HALF, HALF), HALF)
        return (
            dot_nt(dqkv[rows, pl.ds(0, 384)], w_q[...])
            + dot_nt(dqkv[rows, pl.ds(384, 128)], w_k[...])
            + dot_nt(dqkv[rows, pl.ds(512, 128)], w_v[...])
        )

    def first_begin():
        dh1_other[...] = hidden_back(1 - core)
        pl.semaphore_wait(free.at[0], 1)
        near[2].start()
        sum_own[0] = hidden_back(core)

    spots = (x, y, z, core)
    small_copies = [
        [
            remote(
                small.at[p],
                small_got.at[p, spots[p]],
                small_s.at[p, i],
                small_r.at[p, i],
                partner,
            )
            for i, partner in enumerate(ring[p])
        ]
        for p in range(4)
    ]

    def small_begin(p):
        for copy in small_copies[p]:
            copy.start()
        small_got[p, spots[p]] = small[p]

    def small_end(p):
        for copy in small_copies[p]:
            copy.wait_recv()
        total = small_got[p, 0] + small_got[p, 1]
        if p < 3:
            total = total + small_got[p, 2] + small_got[p, 3]
            small[p + 1] = total
        else:
            small_out[...] = total
        for copy in small_copies[p]:
            copy.wait_send()

    jobs = {
        (0, 0): [lambda: by_rows(TOK, 128, rotate), lambda: sum_cross(0)],
        (1, 0): [lambda: sum_begin(1)],
        (2, 0): [hidden_end],
        (2, 1): [lambda: sum_cross(1)],
        (2, 2): [hidden_take],
        (3, 0): [mix_back, lambda: [head_back(h) for h in range(3)]],
        (3, 2): [lambda: [head_back(h) for h in range(3, 6)]],
        (3, 4): [raw_back],
        (4, 0): [first_begin],
        (4, 2): [lambda: sum_cross(2)],
        (4, 4): [out_end],
        (5, 0): [out_take],
        (7, 0): [tokens_end, lambda: small_begin(0)],
        (7, 2): [tokens_take, lambda: small_end(0), lambda: small_begin(1)],
        (8, 0): [lambda: small_end(1), lambda: small_begin(2)],
        (8, 2): [lambda: small_end(2), lambda: small_begin(3)],
        (9, 0): [lambda: small_end(3)],
    }

    left_copies[H2].start()
    right_copies[0].start()
    sum_begin(0)
    for copy in side_loads:
        copy.start()
    for k in range(count + 3):
        steps = (
            (multiply, k),
            (turn, k - 1),
            (relay, k),
            (turn2, k - 2),
            (relay2, k - 1),
            (finish, k - 3),
        )
        for stage, (step, at) in enumerate(steps):
            if 0 <= at < count:
                step(at)
            for job in jobs.get((k, stage), ()):
                job()
    for k in (count - 2, count - 1):
        for o in range(2):
            for copy in first[k][o]:
                copy.wait_send()


def backward(anywhere_in, vmem_in):
    vmem = pl.BlockSpec(memory_space=pltpu.VMEM)
    anywhere = pl.BlockSpec(memory_space=pl.ANY)
    dma = pltpu.SemaphoreType.DMA
    regular = pltpu.SemaphoreType.REGULAR
    half = (HALF, WIDTH)
    return pl.pallas_call(
        backward_kernel,
        out_shape=tuple(jax.ShapeDtypeStruct((48, width), F32) for width in WIDTHS)
        + (
            jax.ShapeDtypeStruct((2, HALF, WIDTH), BF16),
            jax.ShapeDtypeStruct((2, HALF, WIDTH), BF16),
            jax.ShapeDtypeStruct((32, 128), F32),
        ),
        in_specs=[anywhere] * len(anywhere_in) + [vmem] * len(vmem_in),
        out_specs=(vmem,) * 7,
        scratch_shapes=[
            pltpu.VMEM((TOK, WIDTH), BF16),
            pltpu.VMEM((WIDTH, TOK), BF16),
            pltpu.VMEM((2, TOK, CMAX), BF16),
            pltpu.VMEM((2, 2, 4, 192, CMAX), F32),
            pltpu.VMEM((2, 2, 6, 96, CMAX), F32),
            pltpu.VMEM((2, 2, 4, 2, 24, CMAX), F32),
            pltpu.VMEM((2, 2, 6, 24, CMAX), F32),
            pltpu.VMEM((2, 2, 2, 24, CMAX), F32),
            pltpu.VMEM((2, 2, 24, CMAX), F32),
            pltpu.VMEM((2, *half), F32),
            pltpu.VMEM((2, *half), F32),
            pltpu.VMEM((2, *half), F32),
            pltpu.VMEM((2, *half), F32),
            pltpu.VMEM(half, F32),
            pltpu.VMEM((4, 32, 128), F32),
            pltpu.VMEM((4, 4, 32, 128), F32),
            pltpu.VMEM(half, F32),
            pltpu.VMEM((2, *half), BF16),
            pltpu.VMEM(half, BF16),
            pltpu.VMEM(half, BF16),
            pltpu.VMEM((TOK, 384), BF16),
            pltpu.VMEM((TOK, 128), BF16),
            pltpu.VMEM((TOK, 384), BF16),
            pltpu.VMEM((TOK, 384), F32),
            pltpu.VMEM((128, TOK), F32),
            pltpu.VMEM((128, TOK), F32),
            pltpu.VMEM((TOK, 640), BF16),
            pltpu.VMEM((8, 512), F32),
            dma,
            dma((2,)),
            dma((2, 2, 6)),
            dma((2, 2, 6)),
            dma((2, 2, 6)),
            dma((2, 2, 6)),
            dma((2, 2)),
            dma((2, 2)),
            regular((4,)),
            regular((4,)),
            regular,
            dma((4,)),
            dma((3, 3)),
            dma((3, 3)),
            regular((2,)),
            dma((4, 3)),
            dma((4, 3)),
        ],
        compiler_params=pltpu.CompilerParams(
            collective_id=0, has_side_effects=True, vmem_limit_bytes=62 * MIB
        ),
        name="backward",
    )(*anywhere_in, *vmem_in)


def per_device(
    tokens,
    segments,
    norm_one,
    w_query,
    key_projection,
    value_projection,
    w_out,
    q_gain,
    k_gain,
    norm_two,
    w_gate,
    w_up,
    w_down,
    cotangent,
):
    sequence_count, sequence_length = segments.shape
    token_count = tokens.shape[0]
    heads_local = w_query.shape[1] // HEAD_SIZE
    groups_local = key_projection.shape[1] // HEAD_SIZE
    group_count = QUERY_HEADS // KEY_VALUE_HEADS
    scale = HEAD_SIZE ** (-0.5)
    cosine_table, sine_table, allowed = rope_tables(segments)
    tables, begin = lane_tables(cosine_table[0], sine_table[0]), starts_of(segments)
    cosine_table = cosine_table[:, :, None, :]
    sine_table = sine_table[:, :, None, :]
    mask_full = allowed[:, None, None]
    tokens_f = tokens.astype(jnp.float32)
    first_hidden, inv_one = norm_rows(tokens_f, norm_one)
    hidden_one_low = first_hidden.astype(jnp.bfloat16)
    query_unrotated = jnp.dot(hidden_one_low, w_query, preferred_element_type=jnp.float32).reshape(
        sequence_count, sequence_length, heads_local, HEAD_SIZE
    )
    key_unrotated = jnp.dot(
        hidden_one_low, key_projection, preferred_element_type=jnp.float32
    ).reshape(sequence_count, sequence_length, groups_local, HEAD_SIZE)
    value_low = (
        jnp.dot(hidden_one_low, value_projection, preferred_element_type=jnp.float32)
        .astype(jnp.bfloat16)
        .reshape(sequence_count, sequence_length, groups_local, HEAD_SIZE)
    )
    query_norm, query_inv = norm_rows(query_unrotated, q_gain)
    key_norm, key_inv = norm_rows(key_unrotated, k_gain)
    query_low = (
        apply_rotary(query_norm, cosine_table, sine_table)
        .astype(jnp.bfloat16)
        .reshape(sequence_count, sequence_length, groups_local, group_count, HEAD_SIZE)
    )
    key_low = apply_rotary(key_norm, cosine_table, sine_table).astype(jnp.bfloat16)
    scores = (
        jnp.einsum("sqhgd,skhd->shgqk", query_low, key_low, preferred_element_type=jnp.float32)
        * scale
    )
    scores = jnp.where(mask_full, scores, -1e30)
    highest = jnp.max(scores, axis=-1, keepdims=True)
    expo_scores = jnp.exp(scores - highest)
    probs = expo_scores / jnp.sum(expo_scores, axis=-1, keepdims=True)
    probs_low = probs.astype(jnp.bfloat16)
    mixed = jnp.einsum(
        "shgqk,skhd->sqhgd", probs_low, value_low, preferred_element_type=jnp.float32
    )
    mixed_low = mixed.reshape(token_count, heads_local * HEAD_SIZE).astype(jnp.bfloat16)
    attn_part = jnp.dot(mixed_low, w_out, preferred_element_type=jnp.float32)
    x1, hidden_two_low = attention_sum(attn_part, tokens, norm_two)
    gate = jnp.dot(hidden_two_low, w_gate, preferred_element_type=jnp.float32)
    upper = jnp.dot(hidden_two_low, w_up, preferred_element_type=jnp.float32)
    sigmoid_gate = jax.nn.sigmoid(gate)
    silu_gate = gate * sigmoid_gate
    activ_low = (silu_gate * upper).astype(jnp.bfloat16)
    ffn_part = jnp.dot(activ_low, w_down, preferred_element_type=jnp.float32)
    grad_activ = jnp.einsum("td,fd->tf", cotangent, w_down, preferred_element_type=jnp.float32)
    grad_gate_in = (grad_activ * upper * sigmoid_gate * (1.0 + gate * (1.0 - sigmoid_gate))).astype(
        jnp.bfloat16
    )
    grad_up_in = (grad_activ * silu_gate).astype(jnp.bfloat16)
    hidden_two_part = jnp.einsum(
        "tf,df->td", grad_gate_in, w_gate, preferred_element_type=jnp.float32
    ) + jnp.einsum("tf,df->td", grad_up_in, w_up, preferred_element_type=jnp.float32)
    grads_in = jnp.concatenate([grad_gate_in, grad_up_in], axis=1)
    gate_up, down, qkv, out, block_out, grad_tokens, small = backward(
        (
            hidden_two_low,
            cotangent,
            hidden_one_low,
            grads_in,
            jnp.pad(activ_low, ((0, 0), (0, 64))),
            hidden_two_part.reshape(2, HALF, WIDTH),
            ffn_part.reshape(2, HALF, WIDTH),
            tokens,
        ),
        (
            x1,
            norm_one.reshape(1, WIDTH),
            norm_two.reshape(1, WIDTH),
            jnp.tile(q_gain, 6).reshape(1, 384),
            jnp.tile(k_gain, 2).reshape(1, 128),
            query_unrotated.reshape(TOK, 384),
            key_unrotated.reshape(TOK, 128),
            value_low.reshape(TOK, 128),
            mixed_low,
            *tables,
            begin,
            w_out,
            w_query,
            key_projection,
            value_projection,
        ),
    )
    norms = lax.dynamic_slice_in_dim(
        small[1:25].reshape(2, WIDTH), lax.axis_index("dp") * 48, 48, axis=1
    )
    return (
        block_out.reshape(TOK, WIDTH),
        grad_tokens.reshape(TOK, WIDTH),
        norms[0],
        qkv[:, :384],
        qkv[:, 384:512],
        qkv[:, 512:640],
        out.T,
        small[0, :64],
        small[0, 64:],
        norms[1],
        gate_up[:, :FFL],
        gate_up[:, FFL:],
        down[:, :FFL].T,
    )


def solution(mesh):
    placed = (
        P("dp", None),
        P("dp", None),
        P(),
        P(None, "tensor"),
        P(None, "tensor"),
        P(None, "tensor"),
        P("tensor", None),
        P(),
        P(),
        P(),
        P(None, "tensor"),
        P(None, "tensor"),
        P("tensor", None),
        P("dp", None),
    )
    return jax.shard_map(
        per_device,
        mesh=mesh,
        in_specs=placed,
        out_specs=(
            P("dp", None),
            P("dp", None),
            P("dp"),
            P("dp", "tensor"),
            P("dp", "tensor"),
            P("dp", "tensor"),
            P("tensor", "dp"),
            P(),
            P(),
            P("dp"),
            P("dp", "tensor"),
            P("dp", "tensor"),
            P("tensor", "dp"),
        ),
        check_vma=False,
    )
```

```python
import jax
import jax.numpy as jnp
from jax import lax
from jax.experimental import pallas as pl
from jax.experimental.pallas import tpu as pltpu
from jax.sharding import PartitionSpec as P

HEAD_SIZE = 64


EPSILON = 1e-05
THETA = 1000000.0


def starts_of(segments):
    row = segments[0]
    return jnp.sum(row[None, :] < row[:, None], axis=1, dtype=jnp.int32).reshape(-1, 1)


def lane_tables(begin):
    position = (jnp.arange(begin.shape[0], dtype=jnp.int32)[:, None] - begin).astype(jnp.float32)
    frequency = THETA ** (-jnp.arange(HEAD_SIZE // 2, dtype=jnp.float32) * 2.0 / HEAD_SIZE)
    angles = position * frequency
    cosine, sine = jnp.cos(angles), jnp.sin(angles)
    none = jnp.zeros_like(sine)
    return (
        jnp.concatenate([cosine] * 4, axis=1),
        jnp.concatenate([-sine, none] * 2, axis=1),
        jnp.concatenate([none, sine] * 2, axis=1),
    )


MESH = pl.DeviceIdType.MESH
F32 = jnp.float32
BF16 = jnp.bfloat16
WIDTH = 1536
TOK = 512
HALF = 256
FFL = 1728
MIB = 1 << 20
VMEM_MIB = 63


def place():
    dp = lax.axis_index("dp")
    tensor = lax.axis_index("tensor")
    x = lax.div(dp, 8)
    y = lax.rem(lax.div(dp, 2), 4)
    z = lax.div(tensor, 2) * 2 + lax.rem(dp, 2)
    return x, y, z, lax.rem(tensor, 2)


def device(x, y, z, core):
    return (x * 8 + y * 2 + lax.rem(z, 2), lax.div(z, 2) * 2 + core)


def greet(partners):
    barrier = pltpu.get_barrier_semaphore()
    for partner in partners:
        pl.semaphore_signal(barrier, inc=1, device_id=partner, device_id_type=MESH)
    pl.semaphore_wait(barrier, len(partners))


def remote(source, target, send_sem, recv_sem, partner):
    return pltpu.make_async_remote_copy(
        src_ref=source,
        dst_ref=target,
        send_sem=send_sem,
        recv_sem=recv_sem,
        device_id=partner,
        device_id_type=MESH,
    )


def by_rows(count, step, work):
    def body(i, carry):
        work(pl.ds(pl.multiple_of(i * step, step), step))
        return carry

    lax.fori_loop(0, count // step, body, 0)


CMAX = 512
COT, H2, H1, DA = range(4)
ACT, GU, QKV, MIX = range(4)
CHUNKS = (
    (COT, ACT, 0, 512),
    (COT, ACT, 512, 512),
    (COT, ACT, 1024, 512),
    (COT, ACT, 1536, 256),
    (H2, GU, 0, 512),
    (H2, GU, 512, 512),
    (H2, GU, 1024, 512),
    (H2, GU, 1536, 512),
    (H2, GU, 2048, 512),
    (H2, GU, 2560, 512),
    (H2, GU, 3072, 384),
    (H1, QKV, 0, 512),
    (H1, QKV, 512, 128),
    (DA, MIX, 0, 384),
)
COLUMNS = sum(chunk[3] for chunk in CHUNKS)
TILES = tuple((at, min(256, FFL - at)) for at in range(0, FFL, 256))
PAD = 1792
ATTN, DH2, DH1, FFN = range(4)
PIECES = 4
LATE = 4
XP, XM, YP, YM = range(4)
OPPOSITE = (XM, XP, YM, YP)
SCALE = HEAD_SIZE ** (-0.5)
HIGHEST = lax.Precision.HIGHEST


def dot_nt(left, right):
    return lax.dot_general(left, right, (((1,), (1,)), ((), ())), preferred_element_type=F32)


def dot_tn(left, right):
    return lax.dot_general(left, right, (((0,), (0,)), ((), ())), preferred_element_type=F32)


def head_mean(values):
    row = lax.broadcasted_iota(jnp.int32, (128, 128), 0)
    col = lax.broadcasted_iota(jnp.int32, (128, 128), 1)
    same = jnp.where((row < 64) == (col < 64), 1.0 / 64, 0.0)
    return jnp.concatenate(
        [
            jnp.dot(
                values[:, at : at + 128], same, precision=HIGHEST, preferred_element_type=F32
            )
            for at in range(0, values.shape[1], 128)
        ],
        axis=1,
    )


def turned(values, cos, sin_a, sin_b, sign):
    width = values.shape[1]
    copies = width // 128
    cos, sin_a, sin_b = (jnp.concatenate([t] * copies, axis=1) for t in (cos, sin_a, sin_b))
    ahead = pltpu.roll(values, width - 32, 1)
    behind = pltpu.roll(values, 32, 1)
    return values * cos + sign * (ahead * sin_a + behind * sin_b)


def block_kernel(*refs):
    tokens, cotangent, w_gate, w_up, w_down, refs = *refs[:5], refs[5:]
    gain1, gain2, q_gain, k_gain, cos, sin_a, sin_b, begin, refs = *refs[:8], refs[8:]
    w_out, w_q, w_k, w_v, refs = *refs[:4], refs[4:]
    block_out, grad_tokens, out_q, out_k, out_v, out_o, out_gate, out_up, out_down, small_out, refs = (
        *refs[:10],
        refs[10:],
    )
    tok, cot, h1, h2, da, left_t, refs = *refs[:6], refs[6:]
    product, got, passed, got2, keep, got3, refs = *refs[:6], refs[6:]
    halves, sum_near, sum_far, sum_back, x1, dx1, refs = *refs[:6], refs[6:]
    small, small_got, gain_acc, refs = *refs[:3], refs[3:]
    qraw, kraw, vals, mixed, qr, kr, dmixed, dqr, dk_t, dv_t, dqkv, refs = *refs[:11], refs[11:]
    act, gu, ffn, row_buf, refs = *refs[:4], refs[4:]
    s1, r1, s2, r2, s3, r3, credit, credit2, refs = *refs[:8], refs[8:]
    load_sem, row_sem, sum_s, sum_r, free, small_s, small_r, out_sem = refs

    x, y, z, core = place()
    around = (
        device(lax.rem(x + 1, 4), y, z, core),
        device(lax.rem(x + 3, 4), y, z, core),
        device(x, lax.rem(y + 1, 4), z, core),
        device(x, lax.rem(y + 3, 4), z, core),
    )
    z_lo = lax.rem(z, 2)
    beside = device(x, y, z + 1 - 2 * z_lo, core)
    mate = device(x, y, z, 1 - core)
    across = device(x, y, lax.rem(z + 2, 4), core)
    ring = (
        [device(lax.rem(x + i, 4), y, z, core) for i in (1, 2, 3)],
        [device(x, lax.rem(y + i, 4), z, core) for i in (1, 2, 3)],
        [device(x, y, lax.rem(z + i, 4), core) for i in (1, 2, 3)],
        [mate],
    )
    greet([one for group in ring for one in group])

    part, sum_own = halves.at[1 - core], halves.at[core]
    count = len(CHUNKS)
    place1, place2 = (x, y), (y, x)
    forward1, backward1 = (around[XP], around[YP]), (around[XM], around[YM])
    forward2, backward2 = (around[YP], around[XP]), (around[YM], around[XM])

    def new_left(k):
        return k == 0 or CHUNKS[k][0] != CHUNKS[k - 1][0]

    first, second, third = [], [], []
    starts = [sum(chunk[3] for chunk in CHUNKS[:k]) for k in range(count)]
    for k, chunk in enumerate(CHUNKS):
        slot, cols = k % 2, pl.ds(0, chunk[3])
        per1, per2, per3 = [], [], []
        for o in range(2):
            far_block = lax.rem(place1[o] + 2, 4)
            after, before = lax.rem(place1[o] + 1, 4), lax.rem(place1[o] + 3, 4)
            top, low = pl.ds(0, 96), pl.ds(96, 96)
            plan = (
                (far_block, top, forward1[o]),
                (far_block, low, backward1[o]),
                (after, low, forward1[o]),
                (before, top, backward1[o]),
                (after, top, forward1[o]),
                (before, low, backward1[o]),
            )
            per1.append(
                [
                    remote(
                        product.at[slot, o, block, rows, cols],
                        got.at[slot, o, i, :, cols],
                        s1.at[slot, o, i],
                        r1.at[slot, o, i],
                        partner,
                    )
                    for i, (block, rows, partner) in enumerate(plan)
                ]
            )
            far_block = lax.rem(place2[o] + 2, 4)
            after, before = lax.rem(place2[o] + 1, 4), lax.rem(place2[o] + 3, 4)
            plan = (
                (far_block, 0, forward2[o]),
                (far_block, 1, backward2[o]),
                (after, 1, forward2[o]),
                (before, 0, backward2[o]),
                (after, 0, forward2[o]),
                (before, 1, backward2[o]),
            )
            per2.append(
                [
                    remote(
                        passed.at[slot, o, block, half, :, cols],
                        got2.at[slot, o, i, :, cols],
                        s2.at[slot, o, i],
                        r2.at[slot, o, i],
                        partner,
                    )
                    for i, (block, half, partner) in enumerate(plan)
                ]
            )
            per3.append(
                remote(
                    keep.at[o, 1 - z_lo, :, pl.ds(starts[k], chunk[3])],
                    got3.at[o, :, pl.ds(starts[k], chunk[3])],
                    s3.at[k, o],
                    r3.at[k, o],
                    beside,
                )
            )
        first.append(per1)
        second.append(per2)
        third.append(per3)

    def multiply(k):
        slot, (left, right, start, width) = k % 2, CHUNKS[k]
        if new_left(k):
            source = (cot, h2, h1, da)[left]
            for half in range(2):
                for at in range(0, WIDTH, 384):
                    left_t[pl.ds(at, 384), pl.ds(HALF * half, HALF)] = source[
                        half, :, pl.ds(at, 384)
                    ].T
        if k >= 2:
            for o in range(2):
                for copy in first[k - 2][o]:
                    copy.wait_send()
        operand = (act, gu, dqkv, mixed)[right]

        def block(b, carry):
            rows = pl.ds(pl.multiple_of(b * 384, 384), 384)
            for at in range(0, width, 256):
                size = min(256, width - at)
                cols = pl.ds(at, size)
                tile = jnp.dot(
                    left_t[rows, :],
                    operand[:, pl.ds(start + at, size)],
                    preferred_element_type=F32,
                )
                for q in range(8):
                    product[slot, 0, b, pl.ds(24 * q, 24), cols] = tile[48 * q : 48 * q + 24]
                    to = pl.ds(pl.multiple_of(48 * b + 24 * (q % 2), 24), 24)
                    product[slot, 1, q // 2, to, cols] = tile[48 * q + 24 : 48 * q + 48]
            return carry

        lax.fori_loop(0, 4, block, 0)
        if k >= 2:
            for d in range(4):
                pl.semaphore_wait(credit.at[d], 1)
        for i in range(4):
            for o in range(2):
                first[k][o][i].start()

    def relay(k):
        slot, width = k % 2, CHUNKS[k][3]
        cols = pl.ds(0, width)
        for i, shift, base in ((0, 1, 0), (1, 3, 96)):
            for o in range(2):
                first[k][o][i].wait_recv()
                b = lax.rem(place1[o] + shift, 4)

                def add(r, o=o, i=i, b=b, base=base):
                    to = pl.ds(pl.multiple_of(r.start + base, 8), r.size)
                    product[slot, o, b, to, cols] = (
                        product[slot, o, b, to, cols] + got[slot, o, i, r, cols]
                    )

                by_rows(96, 24, add)
                first[k][o][4 + i].start()

    def turn(k):
        slot, width = k % 2, CHUNKS[k][3]
        cols = pl.ds(0, width)
        for o in range(2):
            for i in range(2, 6):
                first[k][o][i].wait_recv()
            b = place1[o]

            def add(q, carry, o=o, b=b):
                for h in range(2):
                    for half, i, j in ((0, 3, 4), (1, 2, 5)):
                        mine = pl.ds(pl.multiple_of(96 * half + 48 * q + 24 * h, 8), 24)
                        theirs = pl.ds(pl.multiple_of(48 * q + 24 * h, 8), 24)
                        passed[slot, o, 2 * half + q, h, :, cols] = (
                            product[slot, o, b, mine, cols]
                            + got[slot, o, i, theirs, cols]
                            + got[slot, o, j, theirs, cols]
                        )
                return carry

            lax.fori_loop(0, 2, add, 0)
            if k >= 2:
                for d in ((YP, YM), (XP, XM))[o]:
                    pl.semaphore_wait(credit2.at[d], 1)
            for i in range(4):
                second[k][o][i].start()
        if k + 2 < count:
            for d in range(4):
                pl.semaphore_signal(
                    credit.at[OPPOSITE[d]], inc=1, device_id=around[d], device_id_type=MESH
                )

    def relay2(k):
        slot, width = k % 2, CHUNKS[k][3]
        cols = pl.ds(0, width)
        for o in range(2):
            for i, shift in ((0, 1), (1, 3)):
                second[k][o][i].wait_recv()
                b = lax.rem(place2[o] + shift, 4)
                passed[slot, o, b, i, :, cols] = (
                    passed[slot, o, b, i, :, cols] + got2[slot, o, i, :, cols]
                )
                second[k][o][4 + i].start()

    def turn2(k):
        slot, width = k % 2, CHUNKS[k][3]
        cols = pl.ds(0, width)
        for o in range(2):
            b = place2[o]
            for h, i, j in ((0, 3, 4), (1, 2, 5)):
                second[k][o][i].wait_recv()
                second[k][o][j].wait_recv()
                keep[o, h, :, pl.ds(starts[k], width)] = (
                    passed[slot, o, b, h, :, cols]
                    + got2[slot, o, i, :, cols]
                    + got2[slot, o, j, :, cols]
                )
        for o in range(2):
            third[k][o].start()
        if k + 2 < count:
            for d in range(4):
                pl.semaphore_signal(
                    credit2.at[OPPOSITE[d]], inc=1, device_id=around[d], device_id_type=MESH
                )
        for o in range(2):
            for copy in second[k][o]:
                copy.wait_send()

    def finish(k):
        _, which, start, width = CHUNKS[k]
        cols = pl.ds(starts[k], width)
        for o in range(2):
            third[k][o].wait_recv()
            rows = pl.ds(24 * o, 24)
            value = keep[o, z_lo, :, cols] + got3[o, :, cols]
            outs, edges = {
                ACT: ((out_down,), (0, FFL)),
                GU: ((out_gate, out_up), (0, FFL, 2 * FFL)),
                QKV: ((out_q, out_k, out_v), (0, 384, 512, 640)),
                MIX: ((out_o,), (0, 384)),
            }[which]
            for out, low, high in zip(outs, edges[:-1], edges[1:]):
                low_at, high_at = max(low, start), min(high, start + width)
                if low_at < high_at:
                    out[rows, pl.ds(low_at - low, high_at - low_at)] = value[
                        :, low_at - start : high_at - start
                    ]
            third[k][o].wait_send()

    def sum_copies(a):
        pieces = PIECES if a == ATTN else 1
        size = HALF // pieces
        other, own = (ffn.at[1 - core], ffn.at[core]) if a == FFN else (part, sum_own)
        plan = ((other, sum_near, mate), (own, sum_far, across), (sum_near, sum_back, mate))
        return [
            [
                remote(
                    source.at[pl.ds(j * size, size)],
                    target.at[pl.ds(j * size, size)],
                    sum_s.at[a, i, j],
                    sum_r.at[a, i, j],
                    partner,
                )
                for j in range(pieces)
            ]
            for i, (source, target, partner) in enumerate(plan)
        ]

    near, far, back = zip(*[sum_copies(a) for a in range(4)])

    def sum_cross(a, j=0):
        near[a][j].wait_recv()
        size = HALF // len(near[a])
        own = ffn.at[core] if a == FFN else sum_own

        def add(r):
            r = pl.ds(pl.multiple_of(r.start + j * size, 16), r.size)
            own[r] = own[r] + sum_near[r]

        by_rows(size, 16, add)
        if a > 0 and j == 0:
            pl.semaphore_wait(free.at[1], 1)
        far[a][j].start()

    def sum_send(a, j=0):
        if a > 0:
            pl.semaphore_wait(free.at[0], 1)
        near[a][j].start()

    def sum_take(a, result, j=0):
        back[a][j].wait_recv()
        size = HALF // len(near[a])

        def put(r):
            r = pl.ds(pl.multiple_of(r.start + j * size, 16), r.size)
            result[1 - core, r] = sum_back[r].astype(BF16)

        by_rows(size, 16, put)
        if j + 1 == len(near[a]):
            for copy in near[a] + far[a] + back[a]:
                copy.wait_send()
            if a < 3:
                pl.semaphore_signal(free.at[0], inc=1, device_id=mate, device_id_type=MESH)
                pl.semaphore_signal(free.at[1], inc=1, device_id=across, device_id_type=MESH)

    def norm_row(row, at):
        for i in range(12):
            small[0, pl.ds(at + i, 1), :] = row[:, 128 * i : 128 * i + 128]

    token_load = pltpu.make_async_copy(tokens, tok, load_sem.at[0])
    cot_load = pltpu.make_async_copy(cotangent, cot, load_sem.at[1])

    def project():
        token_load.wait()

        def norm(i, carry):
            for half in range(2):
                r = pl.ds(pl.multiple_of(i * 16, 16), 16)
                value = tok[half, r].astype(F32)
                inverse = lax.rsqrt(jnp.mean(value * value, axis=-1, keepdims=True) + EPSILON)
                h1[half, r] = (value * inverse * gain1[...]).astype(BF16)
            return carry

        lax.fori_loop(0, HALF // 16, norm, 0)
        for half in range(2):
            rows = pl.ds(HALF * half, HALF)
            value = h1[half]
            qraw[rows] = jnp.dot(value, w_q[...], preferred_element_type=F32)
            kraw[rows] = jnp.dot(value, w_k[...], preferred_element_type=F32)
            vals[rows] = jnp.dot(value, w_v[...], preferred_element_type=F32).astype(BF16)

    def softmax(head, half):
        lanes, glanes = pl.ds(64 * head, 64), pl.ds(64 * (head // 3), 64)
        rows, keys = pl.ds(HALF * half, HALF), pl.ds(0, HALF * (half + 1))
        shape = (HALF, HALF * (half + 1))
        row = lax.broadcasted_iota(jnp.int32, shape, 0) + HALF * half
        col = lax.broadcasted_iota(jnp.int32, shape, 1)
        allowed = (col <= row) & (col >= begin[rows])
        scores = dot_nt(qr[rows, lanes], kr[keys, glanes]) * SCALE
        scores = jnp.where(allowed, scores, -1e30)
        expo = jnp.exp(scores - jnp.max(scores, axis=-1, keepdims=True))
        return expo / jnp.sum(expo, axis=-1, keepdims=True)

    def attend():
        for head in range(6):
            for half in range(2):
                keys = pl.ds(0, HALF * (half + 1))
                mixed[pl.ds(HALF * half, HALF), pl.ds(64 * head, 64)] = jnp.dot(
                    softmax(head, half).astype(BF16),
                    vals[keys, pl.ds(64 * (head // 3), 64)],
                    preferred_element_type=F32,
                ).astype(BF16)

    def attend_out():
        for at in range(0, WIDTH, 256):
            cols = pl.ds(at, 256)
            value = jnp.dot(mixed[...], w_out[:, cols], preferred_element_type=F32)
            halves[:, :, cols] = value.reshape(2, HALF, 256)
        for j in range(PIECES):
            sum_send(ATTN, j)

    def second_norm(j):
        far[ATTN][j].wait_recv()
        size = HALF // PIECES

        def norm(r):
            r = pl.ds(pl.multiple_of(r.start + j * size, 16), r.size)
            value = tok[core, r].astype(F32) + (sum_own[r] + sum_far[r])
            inverse = lax.rsqrt(jnp.mean(value * value, axis=-1, keepdims=True) + EPSILON)
            low = (value * inverse * gain2[...]).astype(BF16)
            x1[r] = value
            h2[core, r] = low
            sum_near[r] = low.astype(F32)

        by_rows(size, 16, norm)
        back[ATTN][j].start()

    def loads_of(t):
        at, size = TILES[t]
        return [
            pltpu.make_async_copy(
                weight.at[pl.ds(at, size), :],
                row_buf.at[i, pl.ds(256 * (t % 2), size), :],
                row_sem.at[t % 2, i],
            )
            for i, weight in enumerate((w_gate, w_up, w_down))
        ]

    tile_loads = [loads_of(t) for t in range(len(TILES))]

    def load_tile(t):
        for copy in tile_loads[t]:
            copy.start()

    def tile(t):
        at, size = TILES[t]
        cols, rows = pl.ds(at, size), pl.ds(256 * (t % 2), size)
        for copy in tile_loads[t]:
            copy.wait()
        gate, up, dact = (
            dot_nt(source[...].reshape(TOK, WIDTH), row_buf[i, rows, :])
            for i, source in enumerate((h2, h2, cot))
        )
        sigmoid = jax.nn.sigmoid(gate)
        silu = gate * sigmoid
        act[:, cols] = (silu * up).astype(BF16)
        gu[:, cols] = (dact * up * sigmoid * (1.0 + gate * (1.0 - sigmoid))).astype(BF16)
        gu[:, pl.ds(FFL + at, size)] = (dact * silu).astype(BF16)

    def tile_back(p):
        at = 512 * p
        size = min(512, FFL - at)
        inputs = (
            gu[:, pl.ds(at, size)],
            gu[:, pl.ds(FFL + at, size)],
            act[:, pl.ds(at, size)],
        )
        for to in range(0, WIDTH, 512):
            cols = pl.ds(to, 512)
            weights = [row_buf[i, pl.ds(0, size), cols] for i in range(3)]
            dh2, dh2_up, down = (
                jnp.dot(value, weight, preferred_element_type=F32).reshape(2, HALF, 512)
                for value, weight in zip(inputs, weights)
            )
            if p == 0:
                halves[:, :, cols] = dh2 + dh2_up
                ffn[:, :, cols] = down
            else:
                halves[:, :, cols] += dh2 + dh2_up
                ffn[:, :, cols] += down
        for t in range(2 * p + 2, min(2 * p + 4, len(TILES))):
            load_tile(t)

    def hidden_end():
        far[DH2][0].wait_recv()

        def body(i, acc):
            r = pl.ds(pl.multiple_of(i * 16, 16), 16)
            value = x1[r]
            total = sum_own[r] + sum_far[r]
            inverse = lax.rsqrt(jnp.mean(value * value, axis=-1, keepdims=True) + EPSILON)
            scaled = total * gain2[...]
            grad = (
                cot[core, r].astype(F32)
                + inverse * scaled
                - value * inverse**3 * jnp.mean(scaled * value, axis=-1, keepdims=True)
            )
            dg = total * value * inverse
            low = grad.astype(BF16)
            dx1[r] = grad
            da[core, r] = low
            sum_near[r] = low.astype(F32)
            return acc + dg[0:8] + dg[8:16]

        acc = lax.fori_loop(0, HALF // 16, body, jnp.zeros((8, WIDTH), F32))
        back[DH2][0].start()
        small[0, pl.ds(24, 8), :] = jnp.zeros((8, 128), F32)
        norm_row(jnp.sum(acc, axis=0, keepdims=True) * 0.5, 13)

    out_copy = pltpu.make_async_copy(h2, block_out, out_sem.at[0])
    tokens_copy = pltpu.make_async_copy(cot, grad_tokens, out_sem.at[1])

    def out_end():
        far[FFN][0].wait_recv()

        def add(r):
            low = (x1[r] + (ffn[core, r] + sum_far[r])).astype(BF16)
            h2[core, r] = low
            sum_near[r] = low.astype(F32)

        by_rows(HALF, 16, add)
        back[FFN][0].start()

    def out_take():
        sum_take(FFN, h2)
        out_copy.start()

    def tokens_end():
        far[DH1][0].wait_recv()

        def body(i, acc):
            r = pl.ds(pl.multiple_of(i * 16, 16), 16)
            value = tok[core, r].astype(F32)
            total = sum_own[r] + sum_far[r]
            inverse = lax.rsqrt(jnp.mean(value * value, axis=-1, keepdims=True) + EPSILON)
            scaled = total * gain1[...]
            grad = (
                dx1[r]
                + inverse * scaled
                - value * inverse**3 * jnp.mean(scaled * value, axis=-1, keepdims=True)
            )
            dg = total * value * inverse
            low = grad.astype(BF16)
            cot[core, r] = low
            sum_near[r] = low.astype(F32)
            return acc + dg[0:8] + dg[8:16]

        acc = lax.fori_loop(0, HALF // 16, body, jnp.zeros((8, WIDTH), F32))
        back[DH1][0].start()
        norm_row(jnp.sum(acc, axis=0, keepdims=True) * 0.5, 1)
        row = gain_acc[...]
        heads = row[:, 0:128] + row[:, 128:256] + row[:, 256:384]
        heads = heads + pltpu.roll(heads, 64, 1)
        groups = row[:, 384:512] + pltpu.roll(row[:, 384:512], 64, 1)
        lane = lax.broadcasted_iota(jnp.int32, (8, 128), 1)
        both = jnp.where(lane < 64, heads, groups)
        small[0, pl.ds(0, 1), :] = jnp.sum(both, axis=0, keepdims=True)

    def tokens_take():
        sum_take(DH1, cot)
        tokens_copy.start()

    def tables(r):
        return cos[r], sin_a[r], sin_b[r]

    def rotate(r):
        for raw, gain, result in ((qraw, q_gain, qr), (kraw, k_gain, kr)):
            value = raw[r]
            inverse = lax.rsqrt(head_mean(value * value) + EPSILON)
            result[r] = turned(value * inverse * gain[...], *tables(r), 1.0).astype(BF16)

    def mix_back():
        for half in range(2):
            rows = pl.ds(HALF * half, HALF)
            dmixed[rows] = dot_nt(da[half], w_out[...]).astype(BF16)
        dk_t[...] = jnp.zeros((128, TOK), F32)
        dv_t[...] = jnp.zeros((128, TOK), F32)

    def head_back(head):
        lanes, glanes = pl.ds(64 * head, 64), pl.ds(64 * (head // 3), 64)
        for half in range(2):
            rows, keys = pl.ds(HALF * half, HALF), pl.ds(0, HALF * (half + 1))
            q, up = qr[rows, lanes], dmixed[rows, lanes]
            probs = softmax(head, half)
            dprobs = dot_nt(up, vals[keys, glanes])
            dscores = probs * (dprobs - jnp.sum(probs * dprobs, axis=-1, keepdims=True))
            dscores = dscores.astype(BF16)
            dqr[rows, lanes] = (
                jnp.dot(dscores, kr[keys, glanes], preferred_element_type=F32) * SCALE
            )
            dk_t[glanes, keys] += dot_tn(q, dscores) * SCALE
            dv_t[glanes, keys] += dot_tn(up, probs.astype(BF16))

    def raw_back():
        dkr = dk_t[...].T
        dqkv[:, pl.ds(512, 128)] = dv_t[...].T.astype(BF16)
        for i in range(4):
            r = pl.ds(128 * i, 128)
            for raw, gain, up, at in (
                (qraw, q_gain, dqr[r], 0),
                (kraw, k_gain, dkr[128 * i : 128 * i + 128], 384),
            ):
                width = up.shape[1]
                value = raw[r]
                up = turned(up, *tables(r), -1.0)
                inverse = lax.rsqrt(head_mean(value * value) + EPSILON)
                scaled = up * gain[...]
                grad = inverse * scaled - value * inverse**3 * head_mean(scaled * value)
                dqkv[r, pl.ds(at, width)] = grad.astype(BF16)
                part = jnp.sum((up * value * inverse).reshape(16, 8, width), axis=0)
                if i == 0:
                    gain_acc[:, pl.ds(at, width)] = part
                else:
                    gain_acc[:, pl.ds(at, width)] += part

    def first_begin():
        for at in range(0, WIDTH, 256):
            rows = pl.ds(at, 256)
            value = (
                dot_nt(dqkv[:, pl.ds(0, 384)], w_q[rows, :])
                + dot_nt(dqkv[:, pl.ds(384, 128)], w_k[rows, :])
                + dot_nt(dqkv[:, pl.ds(512, 128)], w_v[rows, :])
            )
            halves[:, :, rows] = value.reshape(2, HALF, 256)
        sum_send(DH1)

    spots = (x, y, z, core)
    small_copies = [
        [
            remote(
                small.at[p],
                small_got.at[p, spots[p]],
                small_s.at[p, i],
                small_r.at[p, i],
                partner,
            )
            for i, partner in enumerate(ring[p])
        ]
        for p in range(4)
    ]

    def small_begin(p):
        for copy in small_copies[p]:
            copy.start()
        small_got[p, spots[p]] = small[p]

    def small_end(p):
        for copy in small_copies[p]:
            copy.wait_recv()
        total = small_got[p, 0] + small_got[p, 1]
        if p < 3:
            total = total + small_got[p, 2] + small_got[p, 3]
            small[p + 1] = total
        else:
            small_out[...] = total
        for copy in small_copies[p]:
            copy.wait_send()

    def each(work, *several):
        return lambda: [work(one) for one in several]

    jobs = {
        (0, 0): [each(tile_back, 0)],
        (0, 2): [each(tile, 2, 3)],
        (1, 0): [each(tile_back, 1)],
        (1, 2): [each(tile, 4, 5)],
        (2, 0): [each(tile_back, 2)],
        (2, 2): [each(tile, 6), each(tile_back, 3), each(sum_send, DH2)],
        (2, 4): [each(sum_cross, DH2)],
        (5, 0): [hidden_end],
        (5, 1): [lambda: sum_take(DH2, da)],
        (5, 2): [mix_back, each(head_back, 0, 1, 2)],
        (5, 4): [each(head_back, 3, 4, 5)],
        (6, 0): [raw_back, first_begin],
        (6, 2): [each(sum_cross, DH1)],
        (9, 0): [tokens_end, each(small_begin, 0)],
        (9, 1): [tokens_take, each(sum_send, FFN)],
        (9, 2): [each(small_end, 0), each(small_begin, 1)],
        (9, 4): [each(sum_cross, FFN)],
        (10, 0): [each(small_end, 1), each(small_begin, 2)],
        (10, 2): [each(small_end, 2), each(small_begin, 3)],
        (11, 0): [each(small_end, 3)],
        (12, 4): [out_end],
        (13, 0): [out_take],
    }

    token_load.start()
    cot_load.start()
    act[:, pl.ds(FFL, PAD - FFL)] = jnp.zeros((TOK, PAD - FFL), BF16)
    load_tile(0)
    load_tile(1)
    project()
    by_rows(TOK, 128, rotate)
    attend()
    attend_out()
    for j in range(PIECES):
        sum_cross(ATTN, j)
    for j in range(PIECES):
        second_norm(j)
    cot_load.wait()
    for j in range(PIECES):
        sum_take(ATTN, h2, j)
    tile(0)
    tile(1)
    for k in range(count + 2 + LATE):
        steps = (
            (multiply, k),
            (turn, k - 1),
            (relay, k),
            (turn2, k - 2),
            (relay2, k - 1),
            (finish, k - 2 - LATE),
        )
        for stage, (step, at) in enumerate(steps):
            if 0 <= at < count:
                step(at)
            for job in jobs.get((k, stage), ()):
                job()
    for k in (count - 2, count - 1):
        for o in range(2):
            for copy in first[k][o]:
                copy.wait_send()
    out_copy.wait()
    tokens_copy.wait()


def block(anywhere_in, vmem_in):
    vmem = pl.BlockSpec(memory_space=pltpu.VMEM)
    anywhere = pl.BlockSpec(memory_space=pl.ANY)
    dma = pltpu.SemaphoreType.DMA
    regular = pltpu.SemaphoreType.REGULAR
    half, rows = (HALF, WIDTH), (2, HALF, WIDTH)
    return pl.pallas_call(
        block_kernel,
        out_shape=(
            jax.ShapeDtypeStruct(rows, BF16),
            jax.ShapeDtypeStruct(rows, BF16),
            jax.ShapeDtypeStruct((48, 384), F32),
            jax.ShapeDtypeStruct((48, 128), F32),
            jax.ShapeDtypeStruct((48, 128), F32),
            jax.ShapeDtypeStruct((48, 384), F32),
            jax.ShapeDtypeStruct((48, FFL), F32),
            jax.ShapeDtypeStruct((48, FFL), F32),
            jax.ShapeDtypeStruct((48, FFL), F32),
            jax.ShapeDtypeStruct((32, 128), F32),
        ),
        in_specs=[anywhere] * len(anywhere_in) + [vmem] * len(vmem_in),
        out_specs=(anywhere,) * 2 + (vmem,) * 8,
        scratch_shapes=[
            pltpu.VMEM(rows, BF16),
            pltpu.VMEM(rows, BF16),
            pltpu.VMEM(rows, BF16),
            pltpu.VMEM(rows, BF16),
            pltpu.VMEM(rows, BF16),
            pltpu.VMEM((WIDTH, TOK), BF16),
            pltpu.VMEM((2, 2, 4, 192, CMAX), F32),
            pltpu.VMEM((2, 2, 6, 96, CMAX), F32),
            pltpu.VMEM((2, 2, 4, 2, 24, CMAX), F32),
            pltpu.VMEM((2, 2, 6, 24, CMAX), F32),
            pltpu.VMEM((2, 2, 24, COLUMNS), F32),
            pltpu.VMEM((2, 24, COLUMNS), F32),
            pltpu.VMEM((2, *half), F32),
            pltpu.VMEM(half, F32),
            pltpu.VMEM(half, F32),
            pltpu.VMEM(half, F32),
            pltpu.VMEM(half, F32),
            pltpu.VMEM(half, F32),
            pltpu.VMEM((4, 32, 128), F32),
            pltpu.VMEM((4, 4, 32, 128), F32),
            pltpu.VMEM((8, 512), F32),
            pltpu.VMEM((TOK, 384), F32),
            pltpu.VMEM((TOK, 128), F32),
            pltpu.VMEM((TOK, 128), BF16),
            pltpu.VMEM((TOK, 384), BF16),
            pltpu.VMEM((TOK, 384), BF16),
            pltpu.VMEM((TOK, 128), BF16),
            pltpu.VMEM((TOK, 384), BF16),
            pltpu.VMEM((TOK, 384), F32),
            pltpu.VMEM((128, TOK), F32),
            pltpu.VMEM((128, TOK), F32),
            pltpu.VMEM((TOK, 640), BF16),
            pltpu.VMEM((TOK, PAD), BF16),
            pltpu.VMEM((TOK, 2 * FFL), BF16),
            pltpu.VMEM((2, *half), F32),
            pltpu.VMEM((3, 512, WIDTH), BF16),
            dma((2, 2, 6)),
            dma((2, 2, 6)),
            dma((2, 2, 6)),
            dma((2, 2, 6)),
            dma((len(CHUNKS), 2)),
            dma((len(CHUNKS), 2)),
            regular((4,)),
            regular((4,)),
            dma((2,)),
            dma((2, 3)),
            dma((4, 3, PIECES)),
            dma((4, 3, PIECES)),
            regular((2,)),
            dma((4, 3)),
            dma((4, 3)),
            dma((2,)),
        ],
        compiler_params=pltpu.CompilerParams(
            collective_id=0, has_side_effects=True, vmem_limit_bytes=VMEM_MIB * MIB
        ),
        name="whole",
    )(*anywhere_in, *vmem_in)


def per_device(
    tokens,
    segments,
    norm_one,
    w_query,
    key_projection,
    value_projection,
    w_out,
    q_gain,
    k_gain,
    norm_two,
    w_gate,
    w_up,
    w_down,
    cotangent,
):
    begin = starts_of(segments)
    outs = block(
        (
            tokens.reshape(2, HALF, WIDTH),
            cotangent.reshape(2, HALF, WIDTH),
            w_gate.T,
            w_up.T,
            w_down,
        ),
        (
            norm_one.reshape(1, WIDTH),
            norm_two.reshape(1, WIDTH),
            jnp.tile(q_gain, 6).reshape(1, 384),
            jnp.tile(k_gain, 2).reshape(1, 128),
            *lane_tables(begin),
            begin,
            w_out,
            w_query,
            key_projection,
            value_projection,
        ),
    )
    block_out, grad_tokens, query, key, value, out, gate, upper, down, small = outs
    norms = lax.dynamic_slice_in_dim(
        small[1:25].reshape(2, WIDTH), lax.axis_index("dp") * 48, 48, axis=1
    )
    return (
        block_out.reshape(TOK, WIDTH),
        grad_tokens.reshape(TOK, WIDTH),
        norms[0],
        query,
        key,
        value,
        out.T,
        small[0, :64],
        small[0, 64:],
        norms[1],
        gate,
        upper,
        down.T,
    )


def solution(mesh):
    placed = (
        P("dp", None),
        P("dp", None),
        P(),
        P(None, "tensor"),
        P(None, "tensor"),
        P(None, "tensor"),
        P("tensor", None),
        P(),
        P(),
        P(),
        P(None, "tensor"),
        P(None, "tensor"),
        P("tensor", None),
        P("dp", None),
    )
    return jax.shard_map(
        per_device,
        mesh=mesh,
        in_specs=placed,
        out_specs=(
            P("dp", None),
            P("dp", None),
            P("dp"),
            P("dp", "tensor"),
            P("dp", "tensor"),
            P("dp", "tensor"),
            P("tensor", "dp"),
            P(),
            P(),
            P("dp"),
            P("dp", "tensor"),
            P("dp", "tensor"),
            P("tensor", "dp"),
        ),
        check_vma=False,
    )
```

```python
import jax
import jax.numpy as jnp
from jax import lax
from jax.experimental import pallas as pl
from jax.experimental.pallas import tpu as pltpu
from jax.sharding import PartitionSpec as P

HEAD_SIZE = 64


EPSILON = 1e-05
THETA = 1000000.0


def starts_of(segments):
    row = segments[0]
    return jnp.sum(row[None, :] < row[:, None], axis=1, dtype=jnp.int32).reshape(-1, 1)


def lane_tables(begin):
    position = (jnp.arange(begin.shape[0], dtype=jnp.int32)[:, None] - begin).astype(jnp.float32)
    frequency = THETA ** (-jnp.arange(HEAD_SIZE // 2, dtype=jnp.float32) * 2.0 / HEAD_SIZE)
    angles = position * frequency
    cosine, sine = jnp.cos(angles), jnp.sin(angles)
    none = jnp.zeros_like(sine)
    return (
        jnp.concatenate([cosine] * 4, axis=1),
        jnp.concatenate([-sine, none] * 2, axis=1),
        jnp.concatenate([none, sine] * 2, axis=1),
    )


MESH = pl.DeviceIdType.MESH
F32 = jnp.float32
BF16 = jnp.bfloat16
WIDTH = 1536
TOK = 512
HALF = 256
FFL = 1728
MIB = 1 << 20
VMEM_MIB = 63


def place():
    dp = lax.axis_index("dp")
    tensor = lax.axis_index("tensor")
    x = lax.div(dp, 8)
    y = lax.rem(lax.div(dp, 2), 4)
    z = lax.div(tensor, 2) * 2 + lax.rem(dp, 2)
    return x, y, z, lax.rem(tensor, 2)


def device(x, y, z, core):
    return (x * 8 + y * 2 + lax.rem(z, 2), lax.div(z, 2) * 2 + core)


def greet(partners):
    barrier = pltpu.get_barrier_semaphore()
    for partner in partners:
        pl.semaphore_signal(barrier, inc=1, device_id=partner, device_id_type=MESH)


def await_greetings(partners):
    pl.semaphore_wait(pltpu.get_barrier_semaphore(), len(partners))


def remote(source, target, send_sem, recv_sem, partner):
    return pltpu.make_async_remote_copy(
        src_ref=source,
        dst_ref=target,
        send_sem=send_sem,
        recv_sem=recv_sem,
        device_id=partner,
        device_id_type=MESH,
    )


def by_rows(count, step, work):
    def body(i, carry):
        work(pl.ds(pl.multiple_of(i * step, step), step))
        return carry

    lax.fori_loop(0, count // step, body, 0)


CMAX = 512
COT, H2, H1, DA = range(4)
ACT, GU, QKV, MIX = range(4)
CHUNKS = (
    (COT, ACT, 0, 512),
    (COT, ACT, 512, 512),
    (COT, ACT, 1024, 512),
    (COT, ACT, 1536, 256),
    (H2, GU, 0, 512),
    (H2, GU, 512, 512),
    (H2, GU, 1024, 512),
    (H2, GU, 1536, 512),
    (H2, GU, 2048, 512),
    (H2, GU, 2560, 512),
    (H2, GU, 3072, 384),
    (DA, MIX, 0, 384),
    (H1, QKV, 0, 384),
    (H1, QKV, 384, 256),
)
COLUMNS = sum(chunk[3] for chunk in CHUNKS)
TILES = tuple((at, min(256, FFL - at)) for at in range(0, FFL, 256))
PAD = 1792
ATTN, DH2, DH1, FFN = range(4)
PIECES = 4
LATE = 4
XP, XM, YP, YM = range(4)
OPPOSITE = (XM, XP, YM, YP)
SCALE = HEAD_SIZE ** (-0.5)
HIGHEST = lax.Precision.HIGHEST


def dot_nt(left, right):
    return lax.dot_general(left, right, (((1,), (1,)), ((), ())), preferred_element_type=F32)


def dot_tn(left, right):
    return lax.dot_general(left, right, (((0,), (0,)), ((), ())), preferred_element_type=F32)


def head_mean(values):
    row = lax.broadcasted_iota(jnp.int32, (128, 128), 0)
    col = lax.broadcasted_iota(jnp.int32, (128, 128), 1)
    same = jnp.where((row < 64) == (col < 64), 1.0 / 64, 0.0)
    return jnp.concatenate(
        [
            jnp.dot(
                values[:, at : at + 128], same, precision=HIGHEST, preferred_element_type=F32
            )
            for at in range(0, values.shape[1], 128)
        ],
        axis=1,
    )


def turned(values, cos, sin_a, sin_b, sign):
    width = values.shape[1]
    copies = width // 128
    cos, sin_a, sin_b = (jnp.concatenate([t] * copies, axis=1) for t in (cos, sin_a, sin_b))
    ahead = pltpu.roll(values, width - 32, 1)
    behind = pltpu.roll(values, 32, 1)
    return values * cos + sign * (ahead * sin_a + behind * sin_b)


def block_kernel(*refs):
    tokens, cotangent, w_gate, w_up, w_down, refs = *refs[:5], refs[5:]
    projections, refs = refs[:4], refs[4:]
    gain1, gain2, q_gain, k_gain, cos, sin_a, sin_b, begin, refs = *refs[:8], refs[8:]
    block_out, grad_tokens, out_q, out_k, out_v, out_o, out_gate, out_up, out_down, small_out, refs = (
        *refs[:10],
        refs[10:],
    )
    tok, cot, h1, h2, da, left_t, refs = *refs[:6], refs[6:]
    w_q, w_k, w_v, w_out, refs = *refs[:4], refs[4:]
    product, got, passed, got2, keep, got3, refs = *refs[:6], refs[6:]
    halves, sum_near, sum_far, sum_back, x1, dx1, refs = *refs[:6], refs[6:]
    small, small_got, gain_acc, refs = *refs[:3], refs[3:]
    qraw, kraw, vals, mixed, qr, kr, dmixed, dqr, dk_t, dv_t, dqkv, refs = *refs[:11], refs[11:]
    act, gu, ffn, row_buf, refs = *refs[:4], refs[4:]
    s1, r1, s2, r2, s3, r3, credit, credit2, refs = *refs[:8], refs[8:]
    load_sem, row_sem, sum_s, sum_r, free, small_s, small_r, out_sem = refs

    x, y, z, core = place()
    around = (
        device(lax.rem(x + 1, 4), y, z, core),
        device(lax.rem(x + 3, 4), y, z, core),
        device(x, lax.rem(y + 1, 4), z, core),
        device(x, lax.rem(y + 3, 4), z, core),
    )
    z_lo = lax.rem(z, 2)
    beside = device(x, y, z + 1 - 2 * z_lo, core)
    mate = device(x, y, z, 1 - core)
    across = device(x, y, lax.rem(z + 2, 4), core)
    ring = (
        [device(lax.rem(x + i, 4), y, z, core) for i in (1, 2, 3)],
        [device(x, lax.rem(y + i, 4), z, core) for i in (1, 2, 3)],
        [device(x, y, lax.rem(z + i, 4), core) for i in (1, 2, 3)],
        [mate],
    )
    partners = [one for group in ring for one in group]
    greet(partners)

    part, sum_own = halves.at[1 - core], halves.at[core]
    count = len(CHUNKS)
    place1, place2 = (x, y), (y, x)
    forward1, backward1 = (around[XP], around[YP]), (around[XM], around[YM])
    forward2, backward2 = (around[YP], around[XP]), (around[YM], around[XM])

    def new_left(k):
        return k == 0 or CHUNKS[k][0] != CHUNKS[k - 1][0]

    first, second, third = [], [], []
    starts = [sum(chunk[3] for chunk in CHUNKS[:k]) for k in range(count)]
    for k, chunk in enumerate(CHUNKS):
        slot, cols = k % 2, pl.ds(0, chunk[3])
        per1, per2, per3 = [], [], []
        for o in range(2):
            far_block = lax.rem(place1[o] + 2, 4)
            after, before = lax.rem(place1[o] + 1, 4), lax.rem(place1[o] + 3, 4)
            top, low = pl.ds(0, 96), pl.ds(96, 96)
            plan = (
                (far_block, top, forward1[o]),
                (far_block, low, backward1[o]),
                (after, low, forward1[o]),
                (before, top, backward1[o]),
                (after, top, forward1[o]),
                (before, low, backward1[o]),
            )
            per1.append(
                [
                    remote(
                        product.at[slot, o, block, rows, cols],
                        got.at[slot, o, i, :, cols],
                        s1.at[slot, o, i],
                        r1.at[slot, o, i],
                        partner,
                    )
                    for i, (block, rows, partner) in enumerate(plan)
                ]
            )
            far_block = lax.rem(place2[o] + 2, 4)
            after, before = lax.rem(place2[o] + 1, 4), lax.rem(place2[o] + 3, 4)
            plan = (
                (far_block, 0, forward2[o]),
                (far_block, 1, backward2[o]),
                (after, 1, forward2[o]),
                (before, 0, backward2[o]),
                (after, 0, forward2[o]),
                (before, 1, backward2[o]),
            )
            per2.append(
                [
                    remote(
                        passed.at[slot, o, block, half, :, cols],
                        got2.at[slot, o, i, :, cols],
                        s2.at[slot, o, i],
                        r2.at[slot, o, i],
                        partner,
                    )
                    for i, (block, half, partner) in enumerate(plan)
                ]
            )
            per3.append(
                remote(
                    keep.at[o, 1 - z_lo, :, pl.ds(starts[k], chunk[3])],
                    got3.at[o, :, pl.ds(starts[k], chunk[3])],
                    s3.at[k, o],
                    r3.at[k, o],
                    beside,
                )
            )
        first.append(per1)
        second.append(per2)
        third.append(per3)

    def multiply(k):
        slot, (left, right, start, width) = k % 2, CHUNKS[k]
        if new_left(k):
            source = (cot, h2, h1, da)[left]
            for half in range(2):
                for at in range(0, WIDTH, 384):
                    left_t[pl.ds(at, 384), pl.ds(HALF * half, HALF)] = source[
                        half, :, pl.ds(at, 384)
                    ].T
        if k >= 2:
            for o in range(2):
                for copy in first[k - 2][o]:
                    copy.wait_send()
        operand = (act, gu, dqkv, mixed)[right]

        def block(b, carry):
            rows = pl.ds(pl.multiple_of(b * 384, 384), 384)
            for at in range(0, width, 256):
                size = min(256, width - at)
                cols = pl.ds(at, size)
                tile = jnp.dot(
                    left_t[rows, :],
                    operand[:, pl.ds(start + at, size)],
                    preferred_element_type=F32,
                )
                for q in range(8):
                    product[slot, 0, b, pl.ds(24 * q, 24), cols] = tile[48 * q : 48 * q + 24]
                    to = pl.ds(pl.multiple_of(48 * b + 24 * (q % 2), 24), 24)
                    product[slot, 1, q // 2, to, cols] = tile[48 * q + 24 : 48 * q + 48]
            return carry

        lax.fori_loop(0, 4, block, 0)
        if k >= 2:
            for d in range(4):
                pl.semaphore_wait(credit.at[d], 1)
        for i in range(4):
            for o in range(2):
                first[k][o][i].start()

    def relay(k):
        slot, width = k % 2, CHUNKS[k][3]
        cols = pl.ds(0, width)
        for i, shift, base in ((0, 1, 0), (1, 3, 96)):
            for o in range(2):
                first[k][o][i].wait_recv()
                b = lax.rem(place1[o] + shift, 4)

                def add(r, o=o, i=i, b=b, base=base):
                    to = pl.ds(pl.multiple_of(r.start + base, 8), r.size)
                    product[slot, o, b, to, cols] = (
                        product[slot, o, b, to, cols] + got[slot, o, i, r, cols]
                    )

                by_rows(96, 24, add)
                first[k][o][4 + i].start()

    def turn(k):
        slot, width = k % 2, CHUNKS[k][3]
        cols = pl.ds(0, width)
        for o in range(2):
            for i in range(2, 6):
                first[k][o][i].wait_recv()
            b = place1[o]

            def add(q, carry, o=o, b=b):
                for h in range(2):
                    for half, i, j in ((0, 3, 4), (1, 2, 5)):
                        mine = pl.ds(pl.multiple_of(96 * half + 48 * q + 24 * h, 8), 24)
                        theirs = pl.ds(pl.multiple_of(48 * q + 24 * h, 8), 24)
                        passed[slot, o, 2 * half + q, h, :, cols] = (
                            product[slot, o, b, mine, cols]
                            + got[slot, o, i, theirs, cols]
                            + got[slot, o, j, theirs, cols]
                        )
                return carry

            lax.fori_loop(0, 2, add, 0)
            if k >= 2:
                for d in ((YP, YM), (XP, XM))[o]:
                    pl.semaphore_wait(credit2.at[d], 1)
            for i in range(4):
                second[k][o][i].start()
        if k + 2 < count:
            for d in range(4):
                pl.semaphore_signal(
                    credit.at[OPPOSITE[d]], inc=1, device_id=around[d], device_id_type=MESH
                )

    def relay2(k):
        slot, width = k % 2, CHUNKS[k][3]
        cols = pl.ds(0, width)
        for o in range(2):
            for i, shift in ((0, 1), (1, 3)):
                second[k][o][i].wait_recv()
                b = lax.rem(place2[o] + shift, 4)
                passed[slot, o, b, i, :, cols] = (
                    passed[slot, o, b, i, :, cols] + got2[slot, o, i, :, cols]
                )
                second[k][o][4 + i].start()

    def turn2(k):
        slot, width = k % 2, CHUNKS[k][3]
        cols = pl.ds(0, width)
        for o in range(2):
            b = place2[o]
            for h, i, j in ((0, 3, 4), (1, 2, 5)):
                second[k][o][i].wait_recv()
                second[k][o][j].wait_recv()
                keep[o, h, :, pl.ds(starts[k], width)] = (
                    passed[slot, o, b, h, :, cols]
                    + got2[slot, o, i, :, cols]
                    + got2[slot, o, j, :, cols]
                )
        for o in range(2):
            third[k][o].start()
        if k + 2 < count:
            for d in range(4):
                pl.semaphore_signal(
                    credit2.at[OPPOSITE[d]], inc=1, device_id=around[d], device_id_type=MESH
                )
        for o in range(2):
            for copy in second[k][o]:
                copy.wait_send()

    def finish(k):
        _, which, start, width = CHUNKS[k]
        cols = pl.ds(starts[k], width)
        for o in range(2):
            third[k][o].wait_recv()
            rows = pl.ds(24 * o, 24)
            value = keep[o, z_lo, :, cols] + got3[o, :, cols]
            outs, edges = {
                ACT: ((out_down,), (0, FFL)),
                GU: ((out_gate, out_up), (0, FFL, 2 * FFL)),
                QKV: ((out_q, out_k, out_v), (0, 384, 512, 640)),
                MIX: ((out_o,), (0, 384)),
            }[which]
            for out, low, high in zip(outs, edges[:-1], edges[1:]):
                low_at, high_at = max(low, start), min(high, start + width)
                if low_at < high_at:
                    out[rows, pl.ds(low_at - low, high_at - low_at)] = value[
                        :, low_at - start : high_at - start
                    ]
            third[k][o].wait_send()

    def sum_copies(a):
        pieces = PIECES if a == ATTN else 1
        size = HALF // pieces
        other, own = (ffn.at[1 - core], ffn.at[core]) if a == FFN else (part, sum_own)
        plan = ((other, sum_near, mate), (own, sum_far, across), (sum_near, sum_back, mate))
        return [
            [
                remote(
                    source.at[pl.ds(j * size, size)],
                    target.at[pl.ds(j * size, size)],
                    sum_s.at[a, i, j],
                    sum_r.at[a, i, j],
                    partner,
                )
                for j in range(pieces)
            ]
            for i, (source, target, partner) in enumerate(plan)
        ]

    near, far, back = zip(*[sum_copies(a) for a in range(4)])

    def sum_cross(a, j=0):
        near[a][j].wait_recv()
        size = HALF // len(near[a])
        own = ffn.at[core] if a == FFN else sum_own

        def add(r):
            r = pl.ds(pl.multiple_of(r.start + j * size, 16), r.size)
            own[r] = own[r] + sum_near[r]

        by_rows(size, 16, add)
        if a > 0 and j == 0:
            pl.semaphore_wait(free.at[1], 1)
        far[a][j].start()

    def sum_send(a, j=0):
        if a > 0:
            pl.semaphore_wait(free.at[0], 1)
        near[a][j].start()

    def sum_take(a, result, j=0):
        back[a][j].wait_recv()
        size = HALF // len(near[a])

        def put(r):
            r = pl.ds(pl.multiple_of(r.start + j * size, 16), r.size)
            result[1 - core, r] = sum_back[r].astype(BF16)

        by_rows(size, 16, put)
        if j + 1 == len(near[a]):
            for copy in near[a] + far[a] + back[a]:
                copy.wait_send()
            if a != DH1:
                pl.semaphore_signal(free.at[0], inc=1, device_id=mate, device_id_type=MESH)
                pl.semaphore_signal(free.at[1], inc=1, device_id=across, device_id_type=MESH)

    def norm_row(row, at):
        for i in range(12):
            small[0, pl.ds(at + i, 1), :] = row[:, 128 * i : 128 * i + 128]

    token_load = pltpu.make_async_copy(tokens, tok, load_sem.at[0])
    cot_load = pltpu.make_async_copy(cotangent, cot, load_sem.at[1])
    weight_loads = [
        pltpu.make_async_copy(source, target, load_sem.at[2 + i])
        for i, (source, target) in enumerate(zip(projections, (w_q, w_k, w_v, w_out)))
    ]

    def project():
        token_load.wait()

        def norm(i, carry):
            for half in range(2):
                r = pl.ds(pl.multiple_of(i * 16, 16), 16)
                value = tok[half, r].astype(F32)
                inverse = lax.rsqrt(jnp.mean(value * value, axis=-1, keepdims=True) + EPSILON)
                h1[half, r] = (value * inverse * gain1[...]).astype(BF16)
            return carry

        lax.fori_loop(0, HALF // 16, norm, 0)
        for copy in weight_loads:
            copy.wait()
        value = h1[...].reshape(TOK, WIDTH)
        qraw[...] = jnp.dot(value, w_q[...], preferred_element_type=F32)
        kraw[...] = jnp.dot(value, w_k[...], preferred_element_type=F32)
        vals[...] = jnp.dot(value, w_v[...], preferred_element_type=F32).astype(BF16)

    def softmax(head, start, size, end):
        lanes, glanes = pl.ds(64 * head, 64), pl.ds(64 * (head // 3), 64)
        rows, keys = pl.ds(start, size), pl.ds(0, end)
        row = lax.broadcasted_iota(jnp.int32, (size, end), 0) + start
        col = lax.broadcasted_iota(jnp.int32, (size, end), 1)
        allowed = (col <= row) & (col >= begin[rows])
        scores = dot_nt(qr[rows, lanes], kr[keys, glanes]) * SCALE
        expo = jnp.exp(jnp.where(allowed, scores, -1e30))
        return expo * (1.0 / jnp.sum(expo, axis=-1, keepdims=True))

    def attend(j):
        size = HALF // PIECES
        for half in range(2):
            start = HALF * half + size * j
            end = -(-(start + size) // 128) * 128
            rows = pl.ds(start, size)
            for head in range(6):
                mixed[rows, pl.ds(64 * head, 64)] = jnp.dot(
                    softmax(head, start, size, end).astype(BF16),
                    vals[pl.ds(0, end), pl.ds(64 * (head // 3), 64)],
                    preferred_element_type=F32,
                ).astype(BF16)
            halves[half, pl.ds(size * j, size), :] = jnp.dot(
                mixed[rows], w_out[...], preferred_element_type=F32
            )
        if j == 0:
            await_greetings(partners)
        sum_send(ATTN, j)

    def second_norm(j):
        far[ATTN][j].wait_recv()
        size = HALF // PIECES

        def norm(r):
            r = pl.ds(pl.multiple_of(r.start + j * size, 16), r.size)
            value = tok[core, r].astype(F32) + (sum_own[r] + sum_far[r])
            inverse = lax.rsqrt(jnp.mean(value * value, axis=-1, keepdims=True) + EPSILON)
            low = (value * inverse * gain2[...]).astype(BF16)
            x1[r] = value
            h2[core, r] = low
            sum_near[r] = low.astype(F32)

        by_rows(size, 16, norm)
        back[ATTN][j].start()

    def loads_of(t):
        at, size = TILES[t]
        return [
            pltpu.make_async_copy(
                weight.at[pl.ds(at, size), :],
                row_buf.at[i, pl.ds(256 * (t % 2), size), :],
                row_sem.at[t % 2, i],
            )
            for i, weight in enumerate((w_gate, w_up, w_down))
        ]

    tile_loads = [loads_of(t) for t in range(len(TILES))]

    def load_tile(t):
        for copy in tile_loads[t]:
            copy.start()

    def tile(t):
        at, size = TILES[t]
        cols, rows = pl.ds(at, size), pl.ds(256 * (t % 2), size)
        for copy in tile_loads[t]:
            copy.wait()
        gate, up, dact = (
            dot_nt(source[...].reshape(TOK, WIDTH), row_buf[i, rows, :])
            for i, source in enumerate((h2, h2, cot))
        )
        sigmoid = jax.nn.sigmoid(gate)
        silu = gate * sigmoid
        act[:, cols] = (silu * up).astype(BF16)
        gu[:, cols] = (dact * up * sigmoid * (1.0 + gate * (1.0 - sigmoid))).astype(BF16)
        gu[:, pl.ds(FFL + at, size)] = (dact * silu).astype(BF16)

    def tile_back(p):
        at = 512 * p
        size = min(512, FFL - at)
        inputs = (
            gu[:, pl.ds(at, size)],
            gu[:, pl.ds(FFL + at, size)],
            act[:, pl.ds(at, size)],
        )
        for to in range(0, WIDTH, 512):
            cols = pl.ds(to, 512)
            weights = [row_buf[i, pl.ds(0, size), cols] for i in range(3)]
            dh2, dh2_up, down = (
                jnp.dot(value, weight, preferred_element_type=F32).reshape(2, HALF, 512)
                for value, weight in zip(inputs, weights)
            )
            if p == 0:
                halves[:, :, cols] = dh2 + dh2_up
                ffn[:, :, cols] = down
            else:
                halves[:, :, cols] += dh2 + dh2_up
                ffn[:, :, cols] += down
        for t in range(2 * p + 2, min(2 * p + 4, len(TILES))):
            load_tile(t)

    def hidden_end():
        far[DH2][0].wait_recv()

        def body(i, acc):
            r = pl.ds(pl.multiple_of(i * 16, 16), 16)
            value = x1[r]
            total = sum_own[r] + sum_far[r]
            inverse = lax.rsqrt(jnp.mean(value * value, axis=-1, keepdims=True) + EPSILON)
            scaled = total * gain2[...]
            grad = (
                cot[core, r].astype(F32)
                + inverse * scaled
                - value * inverse**3 * jnp.mean(scaled * value, axis=-1, keepdims=True)
            )
            dg = total * value * inverse
            low = grad.astype(BF16)
            dx1[r] = grad
            da[core, r] = low
            sum_near[r] = low.astype(F32)
            return acc + dg[0:8] + dg[8:16]

        acc = lax.fori_loop(0, HALF // 16, body, jnp.zeros((8, WIDTH), F32))
        back[DH2][0].start()
        small[0, pl.ds(24, 8), :] = jnp.zeros((8, 128), F32)
        norm_row(jnp.sum(acc, axis=0, keepdims=True) * 0.5, 13)

    out_copy = pltpu.make_async_copy(h2, block_out, out_sem.at[0])
    tokens_copy = pltpu.make_async_copy(cot, grad_tokens, out_sem.at[1])

    def out_end():
        far[FFN][0].wait_recv()

        def add(r):
            low = (x1[r] + (ffn[core, r] + sum_far[r])).astype(BF16)
            h2[core, r] = low
            sum_near[r] = low.astype(F32)

        by_rows(HALF, 16, add)
        back[FFN][0].start()

    def out_take():
        sum_take(FFN, h2)
        out_copy.start()

    def tokens_end():
        far[DH1][0].wait_recv()

        def body(i, acc):
            r = pl.ds(pl.multiple_of(i * 16, 16), 16)
            value = tok[core, r].astype(F32)
            total = sum_own[r] + sum_far[r]
            inverse = lax.rsqrt(jnp.mean(value * value, axis=-1, keepdims=True) + EPSILON)
            scaled = total * gain1[...]
            grad = (
                dx1[r]
                + inverse * scaled
                - value * inverse**3 * jnp.mean(scaled * value, axis=-1, keepdims=True)
            )
            dg = total * value * inverse
            low = grad.astype(BF16)
            cot[core, r] = low
            sum_near[r] = low.astype(F32)
            return acc + dg[0:8] + dg[8:16]

        acc = lax.fori_loop(0, HALF // 16, body, jnp.zeros((8, WIDTH), F32))
        back[DH1][0].start()
        norm_row(jnp.sum(acc, axis=0, keepdims=True) * 0.5, 1)
        row = gain_acc[...]
        heads = row[:, 0:128] + row[:, 128:256] + row[:, 256:384]
        heads = heads + pltpu.roll(heads, 64, 1)
        groups = row[:, 384:512] + pltpu.roll(row[:, 384:512], 64, 1)
        lane = lax.broadcasted_iota(jnp.int32, (8, 128), 1)
        both = jnp.where(lane < 64, heads, groups)
        small[0, pl.ds(0, 1), :] = jnp.sum(both, axis=0, keepdims=True)

    def tokens_take():
        sum_take(DH1, cot)
        tokens_copy.start()

    def tables(r):
        return cos[r], sin_a[r], sin_b[r]

    def rotate(r):
        for raw, gain, result in ((qraw, q_gain, qr), (kraw, k_gain, kr)):
            value = raw[r]
            inverse = lax.rsqrt(head_mean(value * value) + EPSILON)
            result[r] = turned(value * inverse * gain[...], *tables(r), 1.0).astype(BF16)

    def mix_back():
        for half in range(2):
            rows = pl.ds(HALF * half, HALF)
            dmixed[rows] = dot_nt(da[half], w_out[...]).astype(BF16)
        dk_t[...] = jnp.zeros((128, TOK), F32)
        dv_t[...] = jnp.zeros((128, TOK), F32)

    def head_back(head):
        lanes, glanes = pl.ds(64 * head, 64), pl.ds(64 * (head // 3), 64)
        for half in range(2):
            rows, keys = pl.ds(HALF * half, HALF), pl.ds(0, HALF * (half + 1))
            q, up = qr[rows, lanes], dmixed[rows, lanes]
            probs = softmax(head, HALF * half, HALF, HALF * (half + 1))
            dprobs = dot_nt(up, vals[keys, glanes])
            dscores = probs * (dprobs - jnp.sum(probs * dprobs, axis=-1, keepdims=True))
            dscores = dscores.astype(BF16)
            dqr[rows, lanes] = (
                jnp.dot(dscores, kr[keys, glanes], preferred_element_type=F32) * SCALE
            )
            dk_t[glanes, keys] += dot_tn(q, dscores) * SCALE
            dv_t[glanes, keys] += dot_tn(up, probs.astype(BF16))

    def raw_back():
        dkr = dk_t[...].T
        dqkv[:, pl.ds(512, 128)] = dv_t[...].T.astype(BF16)
        for i in range(4):
            r = pl.ds(128 * i, 128)
            for raw, gain, up, at in (
                (qraw, q_gain, dqr[r], 0),
                (kraw, k_gain, dkr[128 * i : 128 * i + 128], 384),
            ):
                width = up.shape[1]
                value = raw[r]
                up = turned(up, *tables(r), -1.0)
                inverse = lax.rsqrt(head_mean(value * value) + EPSILON)
                scaled = up * gain[...]
                grad = inverse * scaled - value * inverse**3 * head_mean(scaled * value)
                dqkv[r, pl.ds(at, width)] = grad.astype(BF16)
                part = jnp.sum((up * value * inverse).reshape(16, 8, width), axis=0)
                if i == 0:
                    gain_acc[:, pl.ds(at, width)] = part
                else:
                    gain_acc[:, pl.ds(at, width)] += part

    def first_begin():
        for at in range(0, WIDTH, 256):
            rows = pl.ds(at, 256)
            value = (
                dot_nt(dqkv[:, pl.ds(0, 384)], w_q[rows, :])
                + dot_nt(dqkv[:, pl.ds(384, 128)], w_k[rows, :])
                + dot_nt(dqkv[:, pl.ds(512, 128)], w_v[rows, :])
            )
            halves[:, :, rows] = value.reshape(2, HALF, 256)
        sum_send(DH1)

    spots = (x, y, z, core)
    small_copies = [
        [
            remote(
                small.at[p],
                small_got.at[p, spots[p]],
                small_s.at[p, i],
                small_r.at[p, i],
                partner,
            )
            for i, partner in enumerate(ring[p])
        ]
        for p in range(4)
    ]

    def small_begin(p):
        for copy in small_copies[p]:
            copy.start()
        small_got[p, spots[p]] = small[p]

    def small_end(p):
        for copy in small_copies[p]:
            copy.wait_recv()
        total = small_got[p, 0] + small_got[p, 1]
        if p < 3:
            total = total + small_got[p, 2] + small_got[p, 3]
            small[p + 1] = total
        else:
            small_out[...] = total
        for copy in small_copies[p]:
            copy.wait_send()

    def each(work, *several):
        return lambda: [work(one) for one in several]

    jobs = {
        (0, "relay"): [each(tile_back, 0)],
        (0, "multiply"): [each(tile, 2, 3)],
        (0, "turn2"): [each(tile_back, 1), each(tile, 4, 5)],
        (1, "turn2"): [each(tile_back, 2), each(tile, 6), each(tile_back, 3), each(sum_send, DH2)],
        (1, "end"): [each(sum_cross, DH2)],
        (4, "turn2"): [hidden_end],
        (4, "end"): [lambda: sum_take(DH2, da), each(sum_send, FFN), mix_back],
        (5, "multiply"): [each(sum_cross, FFN)],
        (5, "turn2"): [each(head_back, 0, 1, 2, 3)],
        (6, "turn2"): [each(head_back, 4, 5), raw_back],
        (7, "multiply"): [out_end],
        (7, "turn2"): [out_take, first_begin],
        (7, "end"): [each(sum_cross, DH1)],
        (10, "multiply"): [tokens_end, each(small_begin, 0)],
        (10, "turn2"): [tokens_take],
        (10, "end"): [each(small_end, 0), each(small_begin, 1)],
        (11, "turn2"): [each(small_end, 1), each(small_begin, 2)],
        (12, "turn2"): [each(small_end, 2), each(small_begin, 3)],
        (13, "turn2"): [each(small_end, 3)],
    }

    token_load.start()
    for copy in weight_loads:
        copy.start()
    cot_load.start()
    load_tile(0)
    load_tile(1)
    act[:, pl.ds(FFL, PAD - FFL)] = jnp.zeros((TOK, PAD - FFL), BF16)
    project()
    by_rows(TOK, 128, rotate)
    for j in range(PIECES):
        attend(j)
        if j > 0:
            sum_cross(ATTN, j - 1)
    sum_cross(ATTN, PIECES - 1)
    for j in range(PIECES):
        second_norm(j)
    cot_load.wait()
    for j in range(PIECES):
        sum_take(ATTN, h2, j)
    tile(0)
    tile(1)
    multiply(0)
    for k in range(count + 2 + LATE):
        steps = (
            ("turn", turn, k - 1),
            ("relay", relay, k),
            ("multiply", multiply, k + 1),
            ("turn2", turn2, k - 2),
            ("relay2", relay2, k - 1),
            ("finish", finish, k - 2 - LATE),
            ("end", None, -1),
        )
        for name, step, at in steps:
            for job in jobs.get((k, name), ()):
                job()
            if 0 <= at < count:
                step(at)
    for k in (count - 2, count - 1):
        for o in range(2):
            for copy in first[k][o]:
                copy.wait_send()
    out_copy.wait()
    tokens_copy.wait()


def block(anywhere_in, vmem_in):
    vmem = pl.BlockSpec(memory_space=pltpu.VMEM)
    anywhere = pl.BlockSpec(memory_space=pl.ANY)
    dma = pltpu.SemaphoreType.DMA
    regular = pltpu.SemaphoreType.REGULAR
    half, rows = (HALF, WIDTH), (2, HALF, WIDTH)
    return pl.pallas_call(
        block_kernel,
        out_shape=(
            jax.ShapeDtypeStruct(rows, BF16),
            jax.ShapeDtypeStruct(rows, BF16),
            jax.ShapeDtypeStruct((48, 384), F32),
            jax.ShapeDtypeStruct((48, 128), F32),
            jax.ShapeDtypeStruct((48, 128), F32),
            jax.ShapeDtypeStruct((48, 384), F32),
            jax.ShapeDtypeStruct((48, FFL), F32),
            jax.ShapeDtypeStruct((48, FFL), F32),
            jax.ShapeDtypeStruct((48, FFL), F32),
            jax.ShapeDtypeStruct((32, 128), F32),
        ),
        in_specs=[anywhere] * len(anywhere_in) + [vmem] * len(vmem_in),
        out_specs=(anywhere,) * 2 + (vmem,) * 8,
        scratch_shapes=[
            pltpu.VMEM(rows, BF16),
            pltpu.VMEM(rows, BF16),
            pltpu.VMEM(rows, BF16),
            pltpu.VMEM(rows, BF16),
            pltpu.VMEM(rows, BF16),
            pltpu.VMEM((WIDTH, TOK), BF16),
            pltpu.VMEM((WIDTH, 384), BF16),
            pltpu.VMEM((WIDTH, 128), BF16),
            pltpu.VMEM((WIDTH, 128), BF16),
            pltpu.VMEM((384, WIDTH), BF16),
            pltpu.VMEM((2, 2, 4, 192, CMAX), F32),
            pltpu.VMEM((2, 2, 6, 96, CMAX), F32),
            pltpu.VMEM((2, 2, 4, 2, 24, CMAX), F32),
            pltpu.VMEM((2, 2, 6, 24, CMAX), F32),
            pltpu.VMEM((2, 2, 24, COLUMNS), F32),
            pltpu.VMEM((2, 24, COLUMNS), F32),
            pltpu.VMEM((2, *half), F32),
            pltpu.VMEM(half, F32),
            pltpu.VMEM(half, F32),
            pltpu.VMEM(half, F32),
            pltpu.VMEM(half, F32),
            pltpu.VMEM(half, F32),
            pltpu.VMEM((4, 32, 128), F32),
            pltpu.VMEM((4, 4, 32, 128), F32),
            pltpu.VMEM((8, 512), F32),
            pltpu.VMEM((TOK, 384), F32),
            pltpu.VMEM((TOK, 128), F32),
            pltpu.VMEM((TOK, 128), BF16),
            pltpu.VMEM((TOK, 384), BF16),
            pltpu.VMEM((TOK, 384), BF16),
            pltpu.VMEM((TOK, 128), BF16),
            pltpu.VMEM((TOK, 384), BF16),
            pltpu.VMEM((TOK, 384), F32),
            pltpu.VMEM((128, TOK), F32),
            pltpu.VMEM((128, TOK), F32),
            pltpu.VMEM((TOK, 640), BF16),
            pltpu.VMEM((TOK, PAD), BF16),
            pltpu.VMEM((TOK, 2 * FFL), BF16),
            pltpu.VMEM((2, *half), F32),
            pltpu.VMEM((3, 512, WIDTH), BF16),
            dma((2, 2, 6)),
            dma((2, 2, 6)),
            dma((2, 2, 6)),
            dma((2, 2, 6)),
            dma((len(CHUNKS), 2)),
            dma((len(CHUNKS), 2)),
            regular((4,)),
            regular((4,)),
            dma((6,)),
            dma((2, 3)),
            dma((4, 3, PIECES)),
            dma((4, 3, PIECES)),
            regular((2,)),
            dma((4, 3)),
            dma((4, 3)),
            dma((2,)),
        ],
        compiler_params=pltpu.CompilerParams(
            collective_id=0, has_side_effects=True, vmem_limit_bytes=VMEM_MIB * MIB
        ),
        name="whole",
    )(*anywhere_in, *vmem_in)


def hand_on_kernel(*refs):
    count = (len(refs) - 2) // 3
    sources, results, held = refs[:count], refs[count : 2 * count], refs[2 * count : 3 * count]
    in_sem, out_sem = refs[3 * count :]
    reads = [
        pltpu.make_async_copy(one, at, in_sem.at[i])
        for i, (one, at) in enumerate(zip(sources, held))
    ]
    writes = [
        pltpu.make_async_copy(at, one, out_sem.at[i])
        for i, (one, at) in enumerate(zip(results, held))
    ]
    for read in reads:
        read.start()
    for read, write in zip(reads, writes):
        read.wait()
        write.start()
    for write in writes:
        write.wait()


def hand_on(arrays):
    anywhere = pl.BlockSpec(memory_space=pl.ANY)
    return pl.pallas_call(
        hand_on_kernel,
        out_shape=tuple(jax.ShapeDtypeStruct(one.shape, one.dtype) for one in arrays),
        in_specs=[anywhere] * len(arrays),
        out_specs=(anywhere,) * len(arrays),
        scratch_shapes=[pltpu.VMEM(one.shape, one.dtype) for one in arrays]
        + [pltpu.SemaphoreType.DMA((len(arrays),))] * 2,
        compiler_params=pltpu.CompilerParams(vmem_limit_bytes=VMEM_MIB * MIB),
        name="hand_on",
    )(*arrays)


def per_device(
    tokens,
    segments,
    norm_one,
    w_query,
    key_projection,
    value_projection,
    w_out,
    q_gain,
    k_gain,
    norm_two,
    w_gate,
    w_up,
    w_down,
    cotangent,
):
    begin = starts_of(segments)
    outs = block(
        (
            tokens.reshape(2, HALF, WIDTH),
            cotangent.reshape(2, HALF, WIDTH),
            w_gate.T,
            w_up.T,
            w_down,
            w_query,
            key_projection,
            value_projection,
            w_out,
        ),
        (
            norm_one.reshape(1, WIDTH),
            norm_two.reshape(1, WIDTH),
            jnp.tile(q_gain, 6).reshape(1, 384),
            jnp.tile(k_gain, 2).reshape(1, 128),
            *lane_tables(begin),
            begin,
        ),
    )
    small = outs[-1]
    block_out, grad_tokens, query, key, value, out, gate, upper, down = hand_on(outs[:-1])
    norms = lax.dynamic_slice_in_dim(
        small[1:25].reshape(2, WIDTH), lax.axis_index("dp") * 48, 48, axis=1
    )
    return (
        block_out.reshape(TOK, WIDTH),
        grad_tokens.reshape(TOK, WIDTH),
        norms[0],
        query,
        key,
        value,
        out.T,
        small[0, :64],
        small[0, 64:],
        norms[1],
        gate,
        upper,
        down.T,
    )


def solution(mesh):
    placed = (
        P("dp", None),
        P("dp", None),
        P(),
        P(None, "tensor"),
        P(None, "tensor"),
        P(None, "tensor"),
        P("tensor", None),
        P(),
        P(),
        P(),
        P(None, "tensor"),
        P(None, "tensor"),
        P("tensor", None),
        P("dp", None),
    )
    return jax.shard_map(
        per_device,
        mesh=mesh,
        in_specs=placed,
        out_specs=(
            P("dp", None),
            P("dp", None),
            P("dp"),
            P("dp", "tensor"),
            P("dp", "tensor"),
            P("dp", "tensor"),
            P("tensor", "dp"),
            P(),
            P(),
            P("dp"),
            P("dp", "tensor"),
            P("dp", "tensor"),
            P("tensor", "dp"),
        ),
        check_vma=False,
    )
```

```python
import jax
import jax.numpy as jnp
import numpy as np
from jax import lax
from jax.experimental import pallas as pl
from jax.experimental.pallas import tpu as pltpu
from jax.sharding import PartitionSpec as P

HEAD_SIZE = 64


EPSILON = 1e-05
THETA = 1000000.0
FREQUENCY = np.float32(THETA) ** (-np.arange(32, dtype=np.float32) * 2 / HEAD_SIZE)


MESH = pl.DeviceIdType.MESH
F32 = jnp.float32
BF16 = jnp.bfloat16
WIDTH = 1536
TOK = 512
HALF = 256
FFL = 1728
MIB = 1 << 20
VMEM_MIB = 63


def place():
    dp = lax.axis_index("dp")
    tensor = lax.axis_index("tensor")
    x = lax.div(dp, 8)
    y = lax.rem(lax.div(dp, 2), 4)
    z = lax.div(tensor, 2) * 2 + lax.rem(dp, 2)
    return x, y, z, lax.rem(tensor, 2)


def device(x, y, z, core):
    return (x * 8 + y * 2 + lax.rem(z, 2), lax.div(z, 2) * 2 + core)


def greet(partners):
    barrier = pltpu.get_barrier_semaphore()
    for partner in partners:
        pl.semaphore_signal(barrier, inc=1, device_id=partner, device_id_type=MESH)


def await_greetings(partners):
    pl.semaphore_wait(pltpu.get_barrier_semaphore(), len(partners))


def remote(source, target, send_sem, recv_sem, partner):
    return pltpu.make_async_remote_copy(
        src_ref=source,
        dst_ref=target,
        send_sem=send_sem,
        recv_sem=recv_sem,
        device_id=partner,
        device_id_type=MESH,
    )


def by_rows(count, step, work):
    def body(i, carry):
        work(pl.ds(pl.multiple_of(i * step, step), step))
        return carry

    lax.fori_loop(0, count // step, body, 0)


CMAX = 512
COT, H2, H1, DA = range(4)
ACT, GU, QKV, MIX = range(4)
CHUNKS = (
    (COT, ACT, 0, 512),
    (COT, ACT, 512, 512),
    (COT, ACT, 1024, 512),
    (COT, ACT, 1536, 256),
    (H2, GU, 0, 512),
    (H2, GU, 512, 512),
    (H2, GU, 1024, 512),
    (H2, GU, 1536, 512),
    (H2, GU, 2048, 512),
    (H2, GU, 2560, 512),
    (H2, GU, 3072, 384),
    (DA, MIX, 0, 384),
    (H1, QKV, 0, 384),
    (H1, QKV, 384, 256),
)
COLUMNS = sum(chunk[3] for chunk in CHUNKS)
TILES = tuple((at, min(256, FFL - at)) for at in range(0, FFL, 256))
PAD = 1792
ATTN, DH2, DH1, FFN = range(4)
PIECES = 4
LATE = 4
XP, XM, YP, YM = range(4)
OPPOSITE = (XM, XP, YM, YP)
SCALE = HEAD_SIZE ** (-0.5)
HIGHEST = lax.Precision.HIGHEST


def dot_nt(left, right):
    return lax.dot_general(left, right, (((1,), (1,)), ((), ())), preferred_element_type=F32)


def dot_tn(left, right):
    return lax.dot_general(left, right, (((0,), (0,)), ((), ())), preferred_element_type=F32)


def head_mean(values):
    row = lax.broadcasted_iota(jnp.int32, (128, 128), 0)
    col = lax.broadcasted_iota(jnp.int32, (128, 128), 1)
    same = jnp.where((row < 64) == (col < 64), 1.0 / 64, 0.0)
    return jnp.concatenate(
        [
            jnp.dot(
                values[:, at : at + 128], same, precision=HIGHEST, preferred_element_type=F32
            )
            for at in range(0, values.shape[1], 128)
        ],
        axis=1,
    )


def turned(values, cos, sin_a, sin_b, sign):
    width = values.shape[1]
    copies = width // 128
    cos, sin_a, sin_b = (jnp.concatenate([t] * copies, axis=1) for t in (cos, sin_a, sin_b))
    ahead = pltpu.roll(values, width - 32, 1)
    behind = pltpu.roll(values, 32, 1)
    return values * cos + sign * (ahead * sin_a + behind * sin_b)


def block_kernel(*refs):
    tokens, cotangent, w_gate, w_up, w_down, refs = *refs[:5], refs[5:]
    projections, refs = refs[:4], refs[4:]
    norm_one, norm_two, q_line, k_line, segments, frequency, refs = *refs[:6], refs[6:]
    block_out, grad_tokens, out_q, out_k, out_v, out_o, out_gate, out_up, out_down, small_out, refs = (
        *refs[:10],
        refs[10:],
    )
    tok, cot, h1, h2, da, left_t, refs = *refs[:6], refs[6:]
    w_q, w_k, w_v, w_out, refs = *refs[:4], refs[4:]
    gain1, gain2, q_gain, k_gain, cos, sin_a, sin_b, begin, refs = *refs[:8], refs[8:]
    product, got, passed, got2, keep, got3, refs = *refs[:6], refs[6:]
    halves, sum_near, sum_far, sum_back, x1, dx1, refs = *refs[:6], refs[6:]
    small, small_got, gain_acc, refs = *refs[:3], refs[3:]
    qraw, kraw, vals, mixed, qr, kr, dmixed, dqr, dk_t, dv_t, dqkv, refs = *refs[:11], refs[11:]
    act, gu, ffn, row_buf, refs = *refs[:4], refs[4:]
    s1, r1, s2, r2, s3, r3, credit, credit2, refs = *refs[:8], refs[8:]
    load_sem, row_sem, sum_s, sum_r, free, small_s, small_r, out_sem = refs

    x, y, z, core = place()
    around = (
        device(lax.rem(x + 1, 4), y, z, core),
        device(lax.rem(x + 3, 4), y, z, core),
        device(x, lax.rem(y + 1, 4), z, core),
        device(x, lax.rem(y + 3, 4), z, core),
    )
    z_lo = lax.rem(z, 2)
    beside = device(x, y, z + 1 - 2 * z_lo, core)
    mate = device(x, y, z, 1 - core)
    across = device(x, y, lax.rem(z + 2, 4), core)
    ring = (
        [device(lax.rem(x + i, 4), y, z, core) for i in (1, 2, 3)],
        [device(x, lax.rem(y + i, 4), z, core) for i in (1, 2, 3)],
        [device(x, y, lax.rem(z + i, 4), core) for i in (1, 2, 3)],
        [mate],
    )
    partners = [one for group in ring for one in group]
    greet(partners)

    part, sum_own = halves.at[1 - core], halves.at[core]
    count = len(CHUNKS)
    place1, place2 = (x, y), (y, x)
    forward1, backward1 = (around[XP], around[YP]), (around[XM], around[YM])
    forward2, backward2 = (around[YP], around[XP]), (around[YM], around[XM])

    def new_left(k):
        return k == 0 or CHUNKS[k][0] != CHUNKS[k - 1][0]

    first, second, third = [], [], []
    starts = [sum(chunk[3] for chunk in CHUNKS[:k]) for k in range(count)]
    for k, chunk in enumerate(CHUNKS):
        slot, cols = k % 2, pl.ds(0, chunk[3])
        per1, per2, per3 = [], [], []
        for o in range(2):
            far_block = lax.rem(place1[o] + 2, 4)
            after, before = lax.rem(place1[o] + 1, 4), lax.rem(place1[o] + 3, 4)
            top, low = pl.ds(0, 96), pl.ds(96, 96)
            plan = (
                (far_block, top, forward1[o]),
                (far_block, low, backward1[o]),
                (after, low, forward1[o]),
                (before, top, backward1[o]),
                (after, top, forward1[o]),
                (before, low, backward1[o]),
            )
            per1.append(
                [
                    remote(
                        product.at[slot, o, block, rows, cols],
                        got.at[slot, o, i, :, cols],
                        s1.at[slot, o, i],
                        r1.at[slot, o, i],
                        partner,
                    )
                    for i, (block, rows, partner) in enumerate(plan)
                ]
            )
            far_block = lax.rem(place2[o] + 2, 4)
            after, before = lax.rem(place2[o] + 1, 4), lax.rem(place2[o] + 3, 4)
            plan = (
                (far_block, 0, forward2[o]),
                (far_block, 1, backward2[o]),
                (after, 1, forward2[o]),
                (before, 0, backward2[o]),
                (after, 0, forward2[o]),
                (before, 1, backward2[o]),
            )
            per2.append(
                [
                    remote(
                        passed.at[slot, o, block, half, :, cols],
                        got2.at[slot, o, i, :, cols],
                        s2.at[slot, o, i],
                        r2.at[slot, o, i],
                        partner,
                    )
                    for i, (block, half, partner) in enumerate(plan)
                ]
            )
            per3.append(
                remote(
                    keep.at[o, 1 - z_lo, :, pl.ds(starts[k], chunk[3])],
                    got3.at[o, :, pl.ds(starts[k], chunk[3])],
                    s3.at[k, o],
                    r3.at[k, o],
                    beside,
                )
            )
        first.append(per1)
        second.append(per2)
        third.append(per3)

    def multiply(k):
        slot, (left, right, start, width) = k % 2, CHUNKS[k]
        if new_left(k):
            source = (cot, h2, h1, da)[left]
            for half in range(2):
                for at in range(0, WIDTH, 384):
                    left_t[pl.ds(at, 384), pl.ds(HALF * half, HALF)] = source[
                        half, :, pl.ds(at, 384)
                    ].T
        if k >= 2:
            for o in range(2):
                for copy in first[k - 2][o]:
                    copy.wait_send()
        operand = (act, gu, dqkv, mixed)[right]

        def block(b, carry):
            rows = pl.ds(pl.multiple_of(b * 384, 384), 384)
            for at in range(0, width, 256):
                size = min(256, width - at)
                cols = pl.ds(at, size)
                tile = jnp.dot(
                    left_t[rows, :],
                    operand[:, pl.ds(start + at, size)],
                    preferred_element_type=F32,
                )
                for q in range(8):
                    product[slot, 0, b, pl.ds(24 * q, 24), cols] = tile[48 * q : 48 * q + 24]
                    to = pl.ds(pl.multiple_of(48 * b + 24 * (q % 2), 24), 24)
                    product[slot, 1, q // 2, to, cols] = tile[48 * q + 24 : 48 * q + 48]
            return carry

        lax.fori_loop(0, 4, block, 0)
        if k >= 2:
            for d in range(4):
                pl.semaphore_wait(credit.at[d], 1)
        for i in range(4):
            for o in range(2):
                first[k][o][i].start()

    def relay(k):
        slot, width = k % 2, CHUNKS[k][3]
        cols = pl.ds(0, width)
        for i, shift, base in ((0, 1, 0), (1, 3, 96)):
            for o in range(2):
                first[k][o][i].wait_recv()
                b = lax.rem(place1[o] + shift, 4)

                def add(r, o=o, i=i, b=b, base=base):
                    to = pl.ds(pl.multiple_of(r.start + base, 8), r.size)
                    product[slot, o, b, to, cols] = (
                        product[slot, o, b, to, cols] + got[slot, o, i, r, cols]
                    )

                by_rows(96, 24, add)
                first[k][o][4 + i].start()

    def turn(k):
        slot, width = k % 2, CHUNKS[k][3]
        cols = pl.ds(0, width)
        for o in range(2):
            for i in range(2, 6):
                first[k][o][i].wait_recv()
            b = place1[o]

            def add(q, carry, o=o, b=b):
                for h in range(2):
                    for half, i, j in ((0, 3, 4), (1, 2, 5)):
                        mine = pl.ds(pl.multiple_of(96 * half + 48 * q + 24 * h, 8), 24)
                        theirs = pl.ds(pl.multiple_of(48 * q + 24 * h, 8), 24)
                        passed[slot, o, 2 * half + q, h, :, cols] = (
                            product[slot, o, b, mine, cols]
                            + got[slot, o, i, theirs, cols]
                            + got[slot, o, j, theirs, cols]
                        )
                return carry

            lax.fori_loop(0, 2, add, 0)
            if k >= 2:
                for d in ((YP, YM), (XP, XM))[o]:
                    pl.semaphore_wait(credit2.at[d], 1)
            for i in range(4):
                second[k][o][i].start()
        if k + 2 < count:
            for d in range(4):
                pl.semaphore_signal(
                    credit.at[OPPOSITE[d]], inc=1, device_id=around[d], device_id_type=MESH
                )

    def relay2(k):
        slot, width = k % 2, CHUNKS[k][3]
        cols = pl.ds(0, width)
        for o in range(2):
            for i, shift in ((0, 1), (1, 3)):
                second[k][o][i].wait_recv()
                b = lax.rem(place2[o] + shift, 4)
                passed[slot, o, b, i, :, cols] = (
                    passed[slot, o, b, i, :, cols] + got2[slot, o, i, :, cols]
                )
                second[k][o][4 + i].start()

    def turn2(k):
        slot, width = k % 2, CHUNKS[k][3]
        cols = pl.ds(0, width)
        for o in range(2):
            b = place2[o]
            for h, i, j in ((0, 3, 4), (1, 2, 5)):
                second[k][o][i].wait_recv()
                second[k][o][j].wait_recv()
                keep[o, h, :, pl.ds(starts[k], width)] = (
                    passed[slot, o, b, h, :, cols]
                    + got2[slot, o, i, :, cols]
                    + got2[slot, o, j, :, cols]
                )
        for o in range(2):
            third[k][o].start()
        if k + 2 < count:
            for d in range(4):
                pl.semaphore_signal(
                    credit2.at[OPPOSITE[d]], inc=1, device_id=around[d], device_id_type=MESH
                )
        for o in range(2):
            for copy in second[k][o]:
                copy.wait_send()

    def finish(k):
        _, which, start, width = CHUNKS[k]
        cols = pl.ds(starts[k], width)
        for o in range(2):
            third[k][o].wait_recv()
            rows = pl.ds(24 * o, 24)
            value = keep[o, z_lo, :, cols] + got3[o, :, cols]
            outs, edges = {
                ACT: ((out_down,), (0, FFL)),
                GU: ((out_gate, out_up), (0, FFL, 2 * FFL)),
                QKV: ((out_q, out_k, out_v), (0, 384, 512, 640)),
                MIX: ((out_o,), (0, 384)),
            }[which]
            for out, low, high in zip(outs, edges[:-1], edges[1:]):
                low_at, high_at = max(low, start), min(high, start + width)
                if low_at < high_at:
                    out[rows, pl.ds(low_at - low, high_at - low_at)] = value[
                        :, low_at - start : high_at - start
                    ]
            third[k][o].wait_send()

    def sum_copies(a):
        pieces = PIECES if a == ATTN else 1
        size = HALF // pieces
        other, own = (ffn.at[1 - core], ffn.at[core]) if a == FFN else (part, sum_own)
        plan = ((other, sum_near, mate), (own, sum_far, across), (sum_near, sum_back, mate))
        return [
            [
                remote(
                    source.at[pl.ds(j * size, size)],
                    target.at[pl.ds(j * size, size)],
                    sum_s.at[a, i, j],
                    sum_r.at[a, i, j],
                    partner,
                )
                for j in range(pieces)
            ]
            for i, (source, target, partner) in enumerate(plan)
        ]

    near, far, back = zip(*[sum_copies(a) for a in range(4)])

    def sum_cross(a, j=0):
        near[a][j].wait_recv()
        size = HALF // len(near[a])
        own = ffn.at[core] if a == FFN else sum_own

        def add(r):
            r = pl.ds(pl.multiple_of(r.start + j * size, 16), r.size)
            own[r] = own[r] + sum_near[r]

        by_rows(size, 16, add)
        if a > 0 and j == 0:
            pl.semaphore_wait(free.at[1], 1)
        far[a][j].start()

    def sum_send(a, j=0):
        if a > 0:
            pl.semaphore_wait(free.at[0], 1)
        near[a][j].start()

    def sum_take(a, result, j=0):
        back[a][j].wait_recv()
        size = HALF // len(near[a])

        def put(r):
            r = pl.ds(pl.multiple_of(r.start + j * size, 16), r.size)
            result[1 - core, r] = sum_back[r].astype(BF16)

        by_rows(size, 16, put)
        if j + 1 == len(near[a]):
            for copy in near[a] + far[a] + back[a]:
                copy.wait_send()
            if a != DH1:
                pl.semaphore_signal(free.at[0], inc=1, device_id=mate, device_id_type=MESH)
                pl.semaphore_signal(free.at[1], inc=1, device_id=across, device_id_type=MESH)

    def norm_row(row, at):
        for i in range(12):
            small[0, pl.ds(at + i, 1), :] = row[:, 128 * i : 128 * i + 128]

    token_load = pltpu.make_async_copy(tokens, tok, load_sem.at[0])
    cot_load = pltpu.make_async_copy(cotangent, cot, load_sem.at[1])
    weight_loads = [
        pltpu.make_async_copy(source, target, load_sem.at[2 + i])
        for i, (source, target) in enumerate(zip(projections, (w_q, w_k, w_v, w_out)))
    ]

    def lay_tables():
        gain1[...] = norm_one[...].reshape(1, WIDTH)
        gain2[...] = norm_two[...].reshape(1, WIDTH)
        q_gain[...] = jnp.concatenate([q_line[...].reshape(1, HEAD_SIZE)] * 6, axis=1)
        k_gain[...] = jnp.concatenate([k_line[...].reshape(1, HEAD_SIZE)] * 2, axis=1)
        row = segments[...].astype(F32)
        starts = [
            jnp.sum(jnp.where(row < value, 1.0, 0.0), axis=1, keepdims=True)
            for value in (0.5, 1.5, 2.5)
        ]
        wide = jnp.broadcast_to(row, (128, TOK)).T
        first = jnp.where(
            wide < 0.5,
            0.0,
            jnp.where(wide < 1.5, starts[0], jnp.where(wide < 2.5, starts[1], starts[2])),
        )
        begin[...] = first.astype(jnp.int32)
        index = lax.broadcasted_iota(jnp.int32, (TOK, 128), 0).astype(F32)
        angles = (index - first) * frequency[...]
        cos[...] = jnp.cos(angles)
        sine = jnp.sin(angles)
        lane = lax.broadcasted_iota(jnp.int32, (TOK, 128), 1)
        lower = (lane < 32) | ((lane >= 64) & (lane < 96))
        sin_a[...] = jnp.where(lower, -sine, 0.0)
        sin_b[...] = jnp.where(lower, 0.0, sine)

    def project():
        token_load.wait()

        def norm(i, carry):
            for half in range(2):
                r = pl.ds(pl.multiple_of(i * 16, 16), 16)
                value = tok[half, r].astype(F32)
                inverse = lax.rsqrt(jnp.mean(value * value, axis=-1, keepdims=True) + EPSILON)
                h1[half, r] = (value * inverse * gain1[...]).astype(BF16)
            return carry

        lax.fori_loop(0, HALF // 16, norm, 0)
        for copy in weight_loads:
            copy.wait()
        value = h1[...].reshape(TOK, WIDTH)
        qraw[...] = jnp.dot(value, w_q[...], preferred_element_type=F32)
        kraw[...] = jnp.dot(value, w_k[...], preferred_element_type=F32)
        vals[...] = jnp.dot(value, w_v[...], preferred_element_type=F32).astype(BF16)

    def softmax(head, start, size, end):
        lanes, glanes = pl.ds(64 * head, 64), pl.ds(64 * (head // 3), 64)
        rows, keys = pl.ds(start, size), pl.ds(0, end)
        row = lax.broadcasted_iota(jnp.int32, (size, end), 0) + start
        col = lax.broadcasted_iota(jnp.int32, (size, end), 1)
        allowed = (col <= row) & (col >= begin[rows, pl.ds(0, 1)])
        scores = dot_nt(qr[rows, lanes], kr[keys, glanes]) * SCALE
        expo = jnp.exp(jnp.where(allowed, scores, -1e30))
        return expo * (1.0 / jnp.sum(expo, axis=-1, keepdims=True))

    def attend(j):
        size = HALF // PIECES
        for half in range(2):
            if half == 1 and j > 0:
                sum_cross(ATTN, j - 1)
            start = HALF * half + size * j
            end = -(-(start + size) // 128) * 128
            rows = pl.ds(start, size)
            for head in range(6):
                mixed[rows, pl.ds(64 * head, 64)] = jnp.dot(
                    softmax(head, start, size, end).astype(BF16),
                    vals[pl.ds(0, end), pl.ds(64 * (head // 3), 64)],
                    preferred_element_type=F32,
                ).astype(BF16)
            halves[half, pl.ds(size * j, size), :] = jnp.dot(
                mixed[rows], w_out[...], preferred_element_type=F32
            )
        if j == 0:
            await_greetings(partners)
        sum_send(ATTN, j)

    def second_norm(j):
        far[ATTN][j].wait_recv()
        size = HALF // PIECES

        def norm(r):
            r = pl.ds(pl.multiple_of(r.start + j * size, 16), r.size)
            value = tok[core, r].astype(F32) + (sum_own[r] + sum_far[r])
            inverse = lax.rsqrt(jnp.mean(value * value, axis=-1, keepdims=True) + EPSILON)
            low = (value * inverse * gain2[...]).astype(BF16)
            x1[r] = value
            h2[core, r] = low
            sum_near[r] = low.astype(F32)

        by_rows(size, 16, norm)
        back[ATTN][j].start()

    def loads_of(t):
        at, size = TILES[t]
        return [
            pltpu.make_async_copy(
                weight.at[pl.ds(at, size), :],
                row_buf.at[i, pl.ds(256 * (t % 2), size), :],
                row_sem.at[t % 2, i],
            )
            for i, weight in enumerate((w_gate, w_up, w_down))
        ]

    tile_loads = [loads_of(t) for t in range(len(TILES))]

    def load_tile(t):
        for copy in tile_loads[t]:
            copy.start()

    def tile(t):
        at, size = TILES[t]
        cols, rows = pl.ds(at, size), pl.ds(256 * (t % 2), size)
        for copy in tile_loads[t]:
            copy.wait()
        gate, up, dact = (
            dot_nt(source[...].reshape(TOK, WIDTH), row_buf[i, rows, :])
            for i, source in enumerate((h2, h2, cot))
        )
        sigmoid = jax.nn.sigmoid(gate)
        silu = gate * sigmoid
        act[:, cols] = (silu * up).astype(BF16)
        gu[:, cols] = (dact * up * sigmoid * (1.0 + gate * (1.0 - sigmoid))).astype(BF16)
        gu[:, pl.ds(FFL + at, size)] = (dact * silu).astype(BF16)

    def tile_back(p):
        at = 512 * p
        size = min(512, FFL - at)
        inputs = (
            gu[:, pl.ds(at, size)],
            gu[:, pl.ds(FFL + at, size)],
            act[:, pl.ds(at, size)],
        )
        for to in range(0, WIDTH, 512):
            cols = pl.ds(to, 512)
            weights = [row_buf[i, pl.ds(0, size), cols] for i in range(3)]
            dh2, dh2_up, down = (
                jnp.dot(value, weight, preferred_element_type=F32).reshape(2, HALF, 512)
                for value, weight in zip(inputs, weights)
            )
            if p == 0:
                halves[:, :, cols] = dh2 + dh2_up
                ffn[:, :, cols] = down
            else:
                halves[:, :, cols] += dh2 + dh2_up
                ffn[:, :, cols] += down
        for t in range(2 * p + 2, min(2 * p + 4, len(TILES))):
            load_tile(t)

    def hidden_end():
        far[DH2][0].wait_recv()

        def body(i, acc):
            r = pl.ds(pl.multiple_of(i * 16, 16), 16)
            value = x1[r]
            total = sum_own[r] + sum_far[r]
            inverse = lax.rsqrt(jnp.mean(value * value, axis=-1, keepdims=True) + EPSILON)
            scaled = total * gain2[...]
            grad = (
                cot[core, r].astype(F32)
                + inverse * scaled
                - value * inverse**3 * jnp.mean(scaled * value, axis=-1, keepdims=True)
            )
            dg = total * value * inverse
            low = grad.astype(BF16)
            dx1[r] = grad
            da[core, r] = low
            sum_near[r] = low.astype(F32)
            return acc + dg[0:8] + dg[8:16]

        acc = lax.fori_loop(0, HALF // 16, body, jnp.zeros((8, WIDTH), F32))
        back[DH2][0].start()
        small[0, pl.ds(24, 8), :] = jnp.zeros((8, 128), F32)
        norm_row(jnp.sum(acc, axis=0, keepdims=True) * 0.5, 13)

    out_copy = pltpu.make_async_copy(h2, block_out, out_sem.at[0])
    tokens_copy = pltpu.make_async_copy(cot, grad_tokens, out_sem.at[1])

    def out_end():
        far[FFN][0].wait_recv()

        def add(r):
            low = (x1[r] + (ffn[core, r] + sum_far[r])).astype(BF16)
            h2[core, r] = low
            sum_near[r] = low.astype(F32)

        by_rows(HALF, 16, add)
        back[FFN][0].start()

    def out_take():
        sum_take(FFN, h2)
        out_copy.start()

    def tokens_end():
        far[DH1][0].wait_recv()

        def body(i, acc):
            r = pl.ds(pl.multiple_of(i * 16, 16), 16)
            value = tok[core, r].astype(F32)
            total = sum_own[r] + sum_far[r]
            inverse = lax.rsqrt(jnp.mean(value * value, axis=-1, keepdims=True) + EPSILON)
            scaled = total * gain1[...]
            grad = (
                dx1[r]
                + inverse * scaled
                - value * inverse**3 * jnp.mean(scaled * value, axis=-1, keepdims=True)
            )
            dg = total * value * inverse
            low = grad.astype(BF16)
            cot[core, r] = low
            sum_near[r] = low.astype(F32)
            return acc + dg[0:8] + dg[8:16]

        acc = lax.fori_loop(0, HALF // 16, body, jnp.zeros((8, WIDTH), F32))
        back[DH1][0].start()
        norm_row(jnp.sum(acc, axis=0, keepdims=True) * 0.5, 1)
        row = gain_acc[...]
        heads = row[:, 0:128] + row[:, 128:256] + row[:, 256:384]
        heads = heads + pltpu.roll(heads, 64, 1)
        groups = row[:, 384:512] + pltpu.roll(row[:, 384:512], 64, 1)
        lane = lax.broadcasted_iota(jnp.int32, (8, 128), 1)
        both = jnp.where(lane < 64, heads, groups)
        small[0, pl.ds(0, 1), :] = jnp.sum(both, axis=0, keepdims=True)

    def tokens_take():
        sum_take(DH1, cot)
        tokens_copy.start()

    def tables(r):
        return cos[r], sin_a[r], sin_b[r]

    def rotate(r):
        for raw, gain, result in ((qraw, q_gain, qr), (kraw, k_gain, kr)):
            value = raw[r]
            inverse = lax.rsqrt(head_mean(value * value) + EPSILON)
            result[r] = turned(value * inverse * gain[...], *tables(r), 1.0).astype(BF16)

    def mix_back():
        for half in range(2):
            rows = pl.ds(HALF * half, HALF)
            dmixed[rows] = dot_nt(da[half], w_out[...]).astype(BF16)
        dk_t[...] = jnp.zeros((128, TOK), F32)
        dv_t[...] = jnp.zeros((128, TOK), F32)

    def head_back(head):
        lanes, glanes = pl.ds(64 * head, 64), pl.ds(64 * (head // 3), 64)
        for half in range(2):
            rows, keys = pl.ds(HALF * half, HALF), pl.ds(0, HALF * (half + 1))
            q, up = qr[rows, lanes], dmixed[rows, lanes]
            probs = softmax(head, HALF * half, HALF, HALF * (half + 1))
            dprobs = dot_nt(up, vals[keys, glanes])
            dscores = probs * (dprobs - jnp.sum(probs * dprobs, axis=-1, keepdims=True))
            dscores = dscores.astype(BF16)
            dqr[rows, lanes] = (
                jnp.dot(dscores, kr[keys, glanes], preferred_element_type=F32) * SCALE
            )
            dk_t[glanes, keys] += dot_tn(q, dscores) * SCALE
            dv_t[glanes, keys] += dot_tn(up, probs.astype(BF16))

    def raw_back():
        dkr = dk_t[...].T
        dqkv[:, pl.ds(512, 128)] = dv_t[...].T.astype(BF16)
        for i in range(4):
            r = pl.ds(128 * i, 128)
            for raw, gain, up, at in (
                (qraw, q_gain, dqr[r], 0),
                (kraw, k_gain, dkr[128 * i : 128 * i + 128], 384),
            ):
                width = up.shape[1]
                value = raw[r]
                up = turned(up, *tables(r), -1.0)
                inverse = lax.rsqrt(head_mean(value * value) + EPSILON)
                scaled = up * gain[...]
                grad = inverse * scaled - value * inverse**3 * head_mean(scaled * value)
                dqkv[r, pl.ds(at, width)] = grad.astype(BF16)
                part = jnp.sum((up * value * inverse).reshape(16, 8, width), axis=0)
                if i == 0:
                    gain_acc[:, pl.ds(at, width)] = part
                else:
                    gain_acc[:, pl.ds(at, width)] += part

    def first_begin():
        for at in range(0, WIDTH, 256):
            rows = pl.ds(at, 256)
            value = (
                dot_nt(dqkv[:, pl.ds(0, 384)], w_q[rows, :])
                + dot_nt(dqkv[:, pl.ds(384, 128)], w_k[rows, :])
                + dot_nt(dqkv[:, pl.ds(512, 128)], w_v[rows, :])
            )
            halves[:, :, rows] = value.reshape(2, HALF, 256)
        sum_send(DH1)

    spots = (x, y, z, core)
    small_copies = [
        [
            remote(
                small.at[p],
                small_got.at[p, spots[p]],
                small_s.at[p, i],
                small_r.at[p, i],
                partner,
            )
            for i, partner in enumerate(ring[p])
        ]
        for p in range(4)
    ]

    def small_begin(p):
        for copy in small_copies[p]:
            copy.start()
        small_got[p, spots[p]] = small[p]

    def small_end(p):
        for copy in small_copies[p]:
            copy.wait_recv()
        total = small_got[p, 0] + small_got[p, 1]
        if p < 3:
            total = total + small_got[p, 2] + small_got[p, 3]
            small[p + 1] = total
        else:
            small_out[...] = total
        for copy in small_copies[p]:
            copy.wait_send()

    def each(work, *several):
        return lambda: [work(one) for one in several]

    jobs = {
        (0, "relay"): [each(tile_back, 0)],
        (0, "multiply"): [each(tile, 2, 3)],
        (0, "turn2"): [each(tile_back, 1), each(tile, 4, 5)],
        (1, "turn2"): [each(tile_back, 2), each(tile, 6), each(tile_back, 3), each(sum_send, DH2)],
        (1, "end"): [each(sum_cross, DH2)],
        (4, "turn2"): [hidden_end],
        (4, "end"): [lambda: sum_take(DH2, da), each(sum_send, FFN), mix_back],
        (5, "multiply"): [each(sum_cross, FFN)],
        (5, "turn2"): [each(head_back, 0, 1, 2, 3)],
        (6, "turn2"): [each(head_back, 4, 5), raw_back],
        (7, "multiply"): [out_end],
        (7, "turn2"): [out_take, first_begin],
        (7, "end"): [each(sum_cross, DH1)],
        (10, "multiply"): [tokens_end, each(small_begin, 0)],
        (10, "turn2"): [tokens_take],
        (10, "end"): [each(small_end, 0), each(small_begin, 1)],
        (11, "turn2"): [each(small_end, 1), each(small_begin, 2)],
        (12, "turn2"): [each(small_end, 2), each(small_begin, 3)],
        (13, "turn2"): [each(small_end, 3)],
    }

    token_load.start()
    for copy in weight_loads:
        copy.start()
    cot_load.start()
    load_tile(0)
    load_tile(1)
    act[:, pl.ds(FFL, PAD - FFL)] = jnp.zeros((TOK, PAD - FFL), BF16)
    lay_tables()
    project()
    by_rows(TOK, 128, rotate)
    for j in range(PIECES):
        attend(j)
    sum_cross(ATTN, PIECES - 1)
    for j in range(PIECES):
        second_norm(j)
    cot_load.wait()
    for j in range(PIECES):
        sum_take(ATTN, h2, j)
    tile(0)
    tile(1)
    multiply(0)
    for k in range(count + 2 + LATE):
        steps = (
            ("turn", turn, k - 1),
            ("relay", relay, k),
            ("multiply", multiply, k + 1),
            ("turn2", turn2, k - 2),
            ("relay2", relay2, k - 1),
            ("finish", finish, k - 2 - LATE),
            ("end", None, -1),
        )
        for name, step, at in steps:
            for job in jobs.get((k, name), ()):
                job()
            if 0 <= at < count:
                step(at)
    for k in (count - 2, count - 1):
        for o in range(2):
            for copy in first[k][o]:
                copy.wait_send()
    out_copy.wait()
    tokens_copy.wait()


def block(anywhere_in, vmem_in):
    vmem = pl.BlockSpec(memory_space=pltpu.VMEM)
    anywhere = pl.BlockSpec(memory_space=pl.ANY)
    dma = pltpu.SemaphoreType.DMA
    regular = pltpu.SemaphoreType.REGULAR
    half, rows = (HALF, WIDTH), (2, HALF, WIDTH)
    return pl.pallas_call(
        block_kernel,
        out_shape=(
            jax.ShapeDtypeStruct(rows, BF16),
            jax.ShapeDtypeStruct(rows, BF16),
            jax.ShapeDtypeStruct((48, 384), F32),
            jax.ShapeDtypeStruct((48, 128), F32),
            jax.ShapeDtypeStruct((48, 128), F32),
            jax.ShapeDtypeStruct((48, 384), F32),
            jax.ShapeDtypeStruct((48, FFL), F32),
            jax.ShapeDtypeStruct((48, FFL), F32),
            jax.ShapeDtypeStruct((48, FFL), F32),
            jax.ShapeDtypeStruct((32, 128), F32),
        ),
        in_specs=[anywhere] * len(anywhere_in) + [vmem] * len(vmem_in),
        out_specs=(anywhere,) * 2 + (vmem,) * 8,
        scratch_shapes=[
            pltpu.VMEM(rows, BF16),
            pltpu.VMEM(rows, BF16),
            pltpu.VMEM(rows, BF16),
            pltpu.VMEM(rows, BF16),
            pltpu.VMEM(rows, BF16),
            pltpu.VMEM((WIDTH, TOK), BF16),
            pltpu.VMEM((WIDTH, 384), BF16),
            pltpu.VMEM((WIDTH, 128), BF16),
            pltpu.VMEM((WIDTH, 128), BF16),
            pltpu.VMEM((384, WIDTH), BF16),
            pltpu.VMEM((1, WIDTH), F32),
            pltpu.VMEM((1, WIDTH), F32),
            pltpu.VMEM((1, 384), F32),
            pltpu.VMEM((1, 128), F32),
            pltpu.VMEM((TOK, 128), F32),
            pltpu.VMEM((TOK, 128), F32),
            pltpu.VMEM((TOK, 128), F32),
            pltpu.VMEM((TOK, 128), jnp.int32),
            pltpu.VMEM((2, 2, 4, 192, CMAX), F32),
            pltpu.VMEM((2, 2, 6, 96, CMAX), F32),
            pltpu.VMEM((2, 2, 4, 2, 24, CMAX), F32),
            pltpu.VMEM((2, 2, 6, 24, CMAX), F32),
            pltpu.VMEM((2, 2, 24, COLUMNS), F32),
            pltpu.VMEM((2, 24, COLUMNS), F32),
            pltpu.VMEM((2, *half), F32),
            pltpu.VMEM(half, F32),
            pltpu.VMEM(half, F32),
            pltpu.VMEM(half, F32),
            pltpu.VMEM(half, F32),
            pltpu.VMEM(half, F32),
            pltpu.VMEM((4, 32, 128), F32),
            pltpu.VMEM((4, 4, 32, 128), F32),
            pltpu.VMEM((8, 512), F32),
            pltpu.VMEM((TOK, 384), F32),
            pltpu.VMEM((TOK, 128), F32),
            pltpu.VMEM((TOK, 128), BF16),
            pltpu.VMEM((TOK, 384), BF16),
            pltpu.VMEM((TOK, 384), BF16),
            pltpu.VMEM((TOK, 128), BF16),
            pltpu.VMEM((TOK, 384), BF16),
            pltpu.VMEM((TOK, 384), F32),
            pltpu.VMEM((128, TOK), F32),
            pltpu.VMEM((128, TOK), F32),
            pltpu.VMEM((TOK, 640), BF16),
            pltpu.VMEM((TOK, PAD), BF16),
            pltpu.VMEM((TOK, 2 * FFL), BF16),
            pltpu.VMEM((2, *half), F32),
            pltpu.VMEM((3, 512, WIDTH), BF16),
            dma((2, 2, 6)),
            dma((2, 2, 6)),
            dma((2, 2, 6)),
            dma((2, 2, 6)),
            dma((len(CHUNKS), 2)),
            dma((len(CHUNKS), 2)),
            regular((4,)),
            regular((4,)),
            dma((6,)),
            dma((2, 3)),
            dma((4, 3, PIECES)),
            dma((4, 3, PIECES)),
            regular((2,)),
            dma((4, 3)),
            dma((4, 3)),
            dma((2,)),
        ],
        compiler_params=pltpu.CompilerParams(
            collective_id=0, has_side_effects=True, vmem_limit_bytes=VMEM_MIB * MIB
        ),
        name="whole",
    )(*anywhere_in, *vmem_in)


def hand_on_kernel(*refs):
    count = (len(refs) - 2) // 3
    sources, results, held = refs[:count], refs[count : 2 * count], refs[2 * count : 3 * count]
    in_sem, out_sem = refs[3 * count :]
    reads = [
        pltpu.make_async_copy(one, at, in_sem.at[i])
        for i, (one, at) in enumerate(zip(sources, held))
    ]
    writes = [
        pltpu.make_async_copy(at, one, out_sem.at[i])
        for i, (one, at) in enumerate(zip(results, held))
    ]
    for read in reads:
        read.start()
    for read, write in zip(reads, writes):
        read.wait()
        write.start()
    for write in writes:
        write.wait()


def hand_on(arrays):
    anywhere = pl.BlockSpec(memory_space=pl.ANY)
    return pl.pallas_call(
        hand_on_kernel,
        out_shape=tuple(jax.ShapeDtypeStruct(one.shape, one.dtype) for one in arrays),
        in_specs=[anywhere] * len(arrays),
        out_specs=(anywhere,) * len(arrays),
        scratch_shapes=[pltpu.VMEM(one.shape, one.dtype) for one in arrays]
        + [pltpu.SemaphoreType.DMA((len(arrays),))] * 2,
        compiler_params=pltpu.CompilerParams(vmem_limit_bytes=VMEM_MIB * MIB),
        name="hand_on",
    )(*arrays)


def per_device(
    tokens,
    segments,
    norm_one,
    w_query,
    key_projection,
    value_projection,
    w_out,
    q_gain,
    k_gain,
    norm_two,
    w_gate,
    w_up,
    w_down,
    cotangent,
):
    outs = block(
        (
            tokens.reshape(2, HALF, WIDTH),
            cotangent.reshape(2, HALF, WIDTH),
            w_gate.T,
            w_up.T,
            w_down,
            w_query,
            key_projection,
            value_projection,
            w_out,
        ),
        (
            norm_one,
            norm_two,
            q_gain,
            k_gain,
            segments,
            np.tile(FREQUENCY, 4).reshape(1, 128),
        ),
    )
    small = outs[-1]
    block_out, grad_tokens, query, key, value, out, gate, upper, down = hand_on(outs[:-1])
    norms = lax.dynamic_slice_in_dim(
        small[1:25].reshape(2, WIDTH), lax.axis_index("dp") * 48, 48, axis=1
    )
    return (
        block_out.reshape(TOK, WIDTH),
        grad_tokens.reshape(TOK, WIDTH),
        norms[0],
        query,
        key,
        value,
        out.T,
        small[0, :64],
        small[0, 64:],
        norms[1],
        gate,
        upper,
        down.T,
    )


def solution(mesh):
    placed = (
        P("dp", None),
        P("dp", None),
        P(),
        P(None, "tensor"),
        P(None, "tensor"),
        P(None, "tensor"),
        P("tensor", None),
        P(),
        P(),
        P(),
        P(None, "tensor"),
        P(None, "tensor"),
        P("tensor", None),
        P("dp", None),
    )
    return jax.shard_map(
        per_device,
        mesh=mesh,
        in_specs=placed,
        out_specs=(
            P("dp", None),
            P("dp", None),
            P("dp"),
            P("dp", "tensor"),
            P("dp", "tensor"),
            P("dp", "tensor"),
            P("tensor", "dp"),
            P(),
            P(),
            P("dp"),
            P("dp", "tensor"),
            P("dp", "tensor"),
            P("tensor", "dp"),
        ),
        check_vma=False,
    )
```

```python
import jax
import jax.numpy as jnp
import numpy as np
from jax import lax
from jax.experimental import pallas as pl
from jax.experimental.pallas import tpu as pltpu
from jax.sharding import PartitionSpec as P

HEAD_SIZE = 64


EPSILON = 1e-05
THETA = 1000000.0
FREQUENCY = np.float32(THETA) ** (-np.arange(32, dtype=np.float32) * 2 / HEAD_SIZE)


MESH = pl.DeviceIdType.MESH
F32 = jnp.float32
BF16 = jnp.bfloat16
WIDTH = 1536
TOK = 512
HALF = 256
FFL = 1728
MIB = 1 << 20
VMEM_MIB = 63


def place():
    dp = lax.axis_index("dp")
    tensor = lax.axis_index("tensor")
    x = lax.div(dp, 8)
    y = lax.rem(lax.div(dp, 2), 4)
    z = lax.div(tensor, 2) * 2 + lax.rem(dp, 2)
    return x, y, z, lax.rem(tensor, 2)


def device(x, y, z, core):
    return (x * 8 + y * 2 + lax.rem(z, 2), lax.div(z, 2) * 2 + core)


def greet(partners):
    barrier = pltpu.get_barrier_semaphore()
    for partner in partners:
        pl.semaphore_signal(barrier, inc=1, device_id=partner, device_id_type=MESH)


def await_greetings(partners):
    pl.semaphore_wait(pltpu.get_barrier_semaphore(), len(partners))


def remote(source, target, send_sem, recv_sem, partner):
    return pltpu.make_async_remote_copy(
        src_ref=source,
        dst_ref=target,
        send_sem=send_sem,
        recv_sem=recv_sem,
        device_id=partner,
        device_id_type=MESH,
    )


def by_rows(count, step, work):
    def body(i, carry):
        work(pl.ds(pl.multiple_of(i * step, step), step))
        return carry

    lax.fori_loop(0, count // step, body, 0)


CMAX = 512
COT, H2, H1, DA = range(4)
ACT, GU, QKV, MIX = range(4)
CHUNKS = (
    (COT, ACT, 0, 512),
    (COT, ACT, 512, 512),
    (COT, ACT, 1024, 512),
    (COT, ACT, 1536, 256),
    (H2, GU, 0, 512),
    (H2, GU, 512, 512),
    (H2, GU, 1024, 512),
    (H2, GU, 1536, 512),
    (H2, GU, 2048, 512),
    (H2, GU, 2560, 512),
    (H2, GU, 3072, 384),
    (DA, MIX, 0, 384),
    (H1, QKV, 0, 384),
    (H1, QKV, 384, 256),
)
COLUMNS = sum(chunk[3] for chunk in CHUNKS)
TILES = tuple((at, min(256, FFL - at)) for at in range(0, FFL, 256))
PAD = 1792
ATTN, DH2, DH1, FFN = range(4)
PIECES = 8
LATE = 4
XP, XM, YP, YM = range(4)
OPPOSITE = (XM, XP, YM, YP)
SCALE = HEAD_SIZE ** (-0.5)


def dot_nt(left, right):
    return lax.dot_general(left, right, (((1,), (1,)), ((), ())), preferred_element_type=F32)


def dot_tn(left, right):
    return lax.dot_general(left, right, (((0,), (0,)), ((), ())), preferred_element_type=F32)


def head_mean(values):
    row = lax.broadcasted_iota(jnp.int32, (128, 128), 0)
    col = lax.broadcasted_iota(jnp.int32, (128, 128), 1)
    same = jnp.where((row < 64) == (col < 64), 1.0 / 64, 0.0)
    return jnp.concatenate(
        [
            jnp.dot(values[:, at : at + 128], same, preferred_element_type=F32)
            for at in range(0, values.shape[1], 128)
        ],
        axis=1,
    )


def turned(values, cos, sine, sign):
    width = values.shape[1]
    cos, sine = (jnp.concatenate([table] * (width // 128), axis=1) for table in (cos, sine))
    ahead = pltpu.roll(values, width - 32, 1)
    behind = pltpu.roll(values, 32, 1)
    lane = lax.broadcasted_iota(jnp.int32, values.shape, 1)
    other = jnp.where(lax.rem(lane, 64) < 32, -ahead, behind)
    return values * cos + sign * (other * sine)


def block_kernel(*refs):
    tokens, cotangent, w_gate, w_up, w_down, refs = *refs[:5], refs[5:]
    projections, refs = refs[:4], refs[4:]
    norm_one, norm_two, q_line, k_line, segments, frequency, refs = *refs[:6], refs[6:]
    block_out, grad_tokens, out_q, out_k, out_v, out_o, out_gate, out_up, out_down, small_out, refs = (
        *refs[:10],
        refs[10:],
    )
    tok, cot, h1, h2, da, left_t, refs = *refs[:6], refs[6:]
    w_q, w_k, w_v, w_out, refs = *refs[:4], refs[4:]
    gain1, gain2, q_gain, k_gain, cos, sine, begin, refs = *refs[:7], refs[7:]
    product, got, passed, got2, keep, got3, refs = *refs[:6], refs[6:]
    halves, sum_near, sum_far, sum_back, x1, dx1, refs = *refs[:6], refs[6:]
    small, small_got, gain_acc, refs = *refs[:3], refs[3:]
    qraw, kraw, vals, mixed, qr, kr, dmixed, dqr, dk_t, dv_t, dqkv, refs = *refs[:11], refs[11:]
    act, gu, ffn, row_buf, early, refs = *refs[:5], refs[5:]
    s1, r1, s2, r2, s3, r3, credit, credit2, refs = *refs[:8], refs[8:]
    load_sem, row_sem, sum_s, sum_r, free, small_s, small_r, out_sem = refs

    x, y, z, core = place()
    around = (
        device(lax.rem(x + 1, 4), y, z, core),
        device(lax.rem(x + 3, 4), y, z, core),
        device(x, lax.rem(y + 1, 4), z, core),
        device(x, lax.rem(y + 3, 4), z, core),
    )
    z_lo = lax.rem(z, 2)
    beside = device(x, y, z + 1 - 2 * z_lo, core)
    mate = device(x, y, z, 1 - core)
    across = device(x, y, lax.rem(z + 2, 4), core)
    ring = (
        [device(lax.rem(x + i, 4), y, z, core) for i in (1, 2, 3)],
        [device(x, lax.rem(y + i, 4), z, core) for i in (1, 2, 3)],
        [device(x, y, lax.rem(z + i, 4), core) for i in (1, 2, 3)],
        [mate],
    )
    partners = [one for group in ring for one in group]
    greet(partners)

    part, sum_own = halves.at[1 - core], halves.at[core]
    count = len(CHUNKS)
    place1, place2 = (x, y), (y, x)
    forward1, backward1 = (around[XP], around[YP]), (around[XM], around[YM])
    forward2, backward2 = (around[YP], around[XP]), (around[YM], around[XM])

    def new_left(k):
        return k == 0 or CHUNKS[k][0] != CHUNKS[k - 1][0]

    first, second, third = [], [], []
    starts = [sum(chunk[3] for chunk in CHUNKS[:k]) for k in range(count)]
    for k, chunk in enumerate(CHUNKS):
        slot, cols = k % 2, pl.ds(0, chunk[3])
        per1, per2, per3 = [], [], []
        for o in range(2):
            far_block = lax.rem(place1[o] + 2, 4)
            after, before = lax.rem(place1[o] + 1, 4), lax.rem(place1[o] + 3, 4)
            top, low = pl.ds(0, 96), pl.ds(96, 96)
            plan = (
                (far_block, top, forward1[o]),
                (far_block, low, backward1[o]),
                (after, low, forward1[o]),
                (before, top, backward1[o]),
                (after, top, forward1[o]),
                (before, low, backward1[o]),
            )
            per1.append(
                [
                    remote(
                        product.at[slot, o, block, rows, cols],
                        got.at[slot, o, i, :, cols],
                        s1.at[slot, o, i],
                        r1.at[slot, o, i],
                        partner,
                    )
                    for i, (block, rows, partner) in enumerate(plan)
                ]
            )
            far_block = lax.rem(place2[o] + 2, 4)
            after, before = lax.rem(place2[o] + 1, 4), lax.rem(place2[o] + 3, 4)
            plan = (
                (far_block, 0, forward2[o]),
                (far_block, 1, backward2[o]),
                (after, 1, forward2[o]),
                (before, 0, backward2[o]),
                (after, 0, forward2[o]),
                (before, 1, backward2[o]),
            )
            per2.append(
                [
                    remote(
                        passed.at[slot, o, block, half, :, cols],
                        got2.at[slot, o, i, :, cols],
                        s2.at[slot, o, i],
                        r2.at[slot, o, i],
                        partner,
                    )
                    for i, (block, half, partner) in enumerate(plan)
                ]
            )
            per3.append(
                remote(
                    keep.at[o, 1 - z_lo, :, pl.ds(starts[k], chunk[3])],
                    got3.at[o, :, pl.ds(starts[k], chunk[3])],
                    s3.at[k, o],
                    r3.at[k, o],
                    beside,
                )
            )
        first.append(per1)
        second.append(per2)
        third.append(per3)

    def lay_left(left):
        source = (cot, h2, h1, da)[left]
        for half in range(2):
            for at in range(0, WIDTH, 384):
                left_t[pl.ds(at, 384), pl.ds(HALF * half, HALF)] = source[
                    half, :, pl.ds(at, 384)
                ].T

    def multiply(k):
        slot, (left, right, start, width) = k % 2, CHUNKS[k]
        if k > 0 and new_left(k):
            lay_left(left)
        if k >= 2:
            for o in range(2):
                for copy in first[k - 2][o]:
                    copy.wait_send()
        operand = (act, gu, dqkv, mixed)[right]

        def block(b, carry):
            rows = pl.ds(pl.multiple_of(b * 384, 384), 384)
            for at in range(0, width, 256):
                size = min(256, width - at)
                cols = pl.ds(at, size)
                tile = jnp.dot(
                    left_t[rows, :],
                    operand[:, pl.ds(start + at, size)],
                    preferred_element_type=F32,
                )
                for q in range(8):
                    product[slot, 0, b, pl.ds(24 * q, 24), cols] = tile[48 * q : 48 * q + 24]
                    to = pl.ds(pl.multiple_of(48 * b + 24 * (q % 2), 24), 24)
                    product[slot, 1, q // 2, to, cols] = tile[48 * q + 24 : 48 * q + 48]
            return carry

        lax.fori_loop(0, 4, block, 0)
        if k >= 2:
            for d in range(4):
                pl.semaphore_wait(credit.at[d], 1)
        for i in range(4):
            for o in range(2):
                first[k][o][i].start()

    def relay(k):
        slot, width = k % 2, CHUNKS[k][3]
        cols = pl.ds(0, width)
        for i, shift, base in ((0, 1, 0), (1, 3, 96)):
            for o in range(2):
                first[k][o][i].wait_recv()
                b = lax.rem(place1[o] + shift, 4)

                def add(r, o=o, i=i, b=b, base=base):
                    to = pl.ds(pl.multiple_of(r.start + base, 8), r.size)
                    product[slot, o, b, to, cols] = (
                        product[slot, o, b, to, cols] + got[slot, o, i, r, cols]
                    )

                by_rows(96, 24, add)
                first[k][o][4 + i].start()

    def turn(k):
        slot, width = k % 2, CHUNKS[k][3]
        cols = pl.ds(0, width)
        for o in range(2):
            for i in range(2, 6):
                first[k][o][i].wait_recv()
            b = place1[o]

            def add(q, carry, o=o, b=b):
                for h in range(2):
                    for half, i, j in ((0, 3, 4), (1, 2, 5)):
                        mine = pl.ds(pl.multiple_of(96 * half + 48 * q + 24 * h, 8), 24)
                        theirs = pl.ds(pl.multiple_of(48 * q + 24 * h, 8), 24)
                        passed[slot, o, 2 * half + q, h, :, cols] = (
                            product[slot, o, b, mine, cols]
                            + got[slot, o, i, theirs, cols]
                            + got[slot, o, j, theirs, cols]
                        )
                return carry

            lax.fori_loop(0, 2, add, 0)
            if k >= 2:
                for d in ((YP, YM), (XP, XM))[o]:
                    pl.semaphore_wait(credit2.at[d], 1)
            for i in range(4):
                second[k][o][i].start()
        if k + 2 < count:
            for d in range(4):
                pl.semaphore_signal(
                    credit.at[OPPOSITE[d]], inc=1, device_id=around[d], device_id_type=MESH
                )

    def relay2(k):
        slot, width = k % 2, CHUNKS[k][3]
        cols = pl.ds(0, width)
        for o in range(2):
            for i, shift in ((0, 1), (1, 3)):
                second[k][o][i].wait_recv()
                b = lax.rem(place2[o] + shift, 4)
                passed[slot, o, b, i, :, cols] = (
                    passed[slot, o, b, i, :, cols] + got2[slot, o, i, :, cols]
                )
                second[k][o][4 + i].start()

    def turn2(k):
        slot, width = k % 2, CHUNKS[k][3]
        cols = pl.ds(0, width)
        for o in range(2):
            b = place2[o]
            for h, i, j in ((0, 3, 4), (1, 2, 5)):
                second[k][o][i].wait_recv()
                second[k][o][j].wait_recv()
                keep[o, h, :, pl.ds(starts[k], width)] = (
                    passed[slot, o, b, h, :, cols]
                    + got2[slot, o, i, :, cols]
                    + got2[slot, o, j, :, cols]
                )
        for o in range(2):
            third[k][o].start()
        if k + 2 < count:
            for d in range(4):
                pl.semaphore_signal(
                    credit2.at[OPPOSITE[d]], inc=1, device_id=around[d], device_id_type=MESH
                )
        for o in range(2):
            for copy in second[k][o]:
                copy.wait_send()

    def finish(k):
        _, which, start, width = CHUNKS[k]
        cols = pl.ds(starts[k], width)
        for o in range(2):
            third[k][o].wait_recv()
            rows = pl.ds(24 * o, 24)
            value = keep[o, z_lo, :, cols] + got3[o, :, cols]
            outs, edges = {
                ACT: ((out_down,), (0, FFL)),
                GU: ((out_gate, out_up), (0, FFL, 2 * FFL)),
                QKV: ((out_q, out_k, out_v), (0, 384, 512, 640)),
                MIX: ((out_o,), (0, 384)),
            }[which]
            for out, low, high in zip(outs, edges[:-1], edges[1:]):
                low_at, high_at = max(low, start), min(high, start + width)
                if low_at < high_at:
                    out[rows, pl.ds(low_at - low, high_at - low_at)] = value[
                        :, low_at - start : high_at - start
                    ]
            third[k][o].wait_send()

    def sum_copies(a):
        pieces = PIECES if a == ATTN else 1
        size = HALF // pieces
        other, own = (ffn.at[1 - core], ffn.at[core]) if a == FFN else (part, sum_own)
        plan = ((other, sum_near, mate), (own, sum_far, across), (sum_near, sum_back, mate))
        return [
            [
                remote(
                    source.at[pl.ds(j * size, size)],
                    target.at[pl.ds(j * size, size)],
                    sum_s.at[a, i, j],
                    sum_r.at[a, i, j],
                    partner,
                )
                for j in range(pieces)
            ]
            for i, (source, target, partner) in enumerate(plan)
        ]

    near, far, back = zip(*[sum_copies(a) for a in range(4)])

    def sum_cross(a, j=0):
        near[a][j].wait_recv()
        size = HALF // len(near[a])
        own = ffn.at[core] if a == FFN else sum_own

        def add(r):
            r = pl.ds(pl.multiple_of(r.start + j * size, 16), r.size)
            own[r] = own[r] + sum_near[r]

        by_rows(size, 16, add)
        if a > 0 and j == 0:
            pl.semaphore_wait(free.at[1], 1)
        far[a][j].start()

    def sum_send(a, j=0):
        if a > 0:
            pl.semaphore_wait(free.at[0], 1)
        near[a][j].start()

    def sum_take(a, result, j=0):
        back[a][j].wait_recv()
        size = HALF // len(near[a])

        def put(r):
            r = pl.ds(pl.multiple_of(r.start + j * size, 16), r.size)
            result[1 - core, r] = sum_back[r].astype(BF16)

        by_rows(size, 16, put)
        if j + 1 == len(near[a]):
            for copy in near[a] + far[a] + back[a]:
                copy.wait_send()
            if a != DH1:
                pl.semaphore_signal(free.at[0], inc=1, device_id=mate, device_id_type=MESH)
                pl.semaphore_signal(free.at[1], inc=1, device_id=across, device_id_type=MESH)

    def norm_row(row, at):
        for i in range(12):
            small[0, pl.ds(at + i, 1), :] = row[:, 128 * i : 128 * i + 128]

    token_load = pltpu.make_async_copy(tokens, tok, load_sem.at[0])
    cot_load = pltpu.make_async_copy(cotangent, cot, load_sem.at[1])
    weight_loads = [
        pltpu.make_async_copy(source, target, load_sem.at[2 + i])
        for i, (source, target) in enumerate(zip(projections, (w_q, w_k, w_v, w_out)))
    ]

    def lay_tables():
        gain1[...] = norm_one[...].reshape(1, WIDTH)
        gain2[...] = norm_two[...].reshape(1, WIDTH)
        q_gain[...] = jnp.concatenate([q_line[...].reshape(1, HEAD_SIZE)] * 6, axis=1)
        k_gain[...] = jnp.concatenate([k_line[...].reshape(1, HEAD_SIZE)] * 2, axis=1)
        row = segments[...].astype(F32)
        starts = [
            jnp.sum(jnp.where(row < value, 1.0, 0.0), axis=1, keepdims=True)
            for value in (0.5, 1.5, 2.5)
        ]
        wide = jnp.broadcast_to(row, (128, TOK)).T
        first = jnp.where(
            wide < 0.5,
            0.0,
            jnp.where(wide < 1.5, starts[0], jnp.where(wide < 2.5, starts[1], starts[2])),
        )
        begin[...] = first.astype(jnp.int32)
        index = lax.broadcasted_iota(jnp.int32, (TOK, 128), 0).astype(F32)
        angles = (index - first) * frequency[...]
        cos[...] = jnp.cos(angles)
        sine[...] = jnp.sin(angles)

    def project():
        token_load.wait()

        def norm(i, carry):
            for half in range(2):
                r = pl.ds(pl.multiple_of(i * 16, 16), 16)
                value = tok[half, r].astype(F32)
                inverse = lax.rsqrt(jnp.mean(value * value, axis=-1, keepdims=True) + EPSILON)
                h1[half, r] = (value * inverse * gain1[...]).astype(BF16)
            return carry

        lax.fori_loop(0, HALF // 16, norm, 0)
        for copy in weight_loads:
            copy.wait()
        value = h1[...].reshape(TOK, WIDTH)
        qraw[...] = jnp.dot(value, w_q[...], preferred_element_type=F32)
        kraw[...] = jnp.dot(value, w_k[...], preferred_element_type=F32)
        vals[...] = jnp.dot(value, w_v[...], preferred_element_type=F32).astype(BF16)

    def softmax(head, start, size, end):
        lanes, glanes = pl.ds(64 * head, 64), pl.ds(64 * (head // 3), 64)
        rows, keys = pl.ds(start, size), pl.ds(0, end)
        row = lax.broadcasted_iota(jnp.int32, (size, end), 0) + start
        col = lax.broadcasted_iota(jnp.int32, (size, end), 1)
        allowed = (col <= row) & (col >= begin[rows, pl.ds(0, 1)])
        scores = dot_nt(qr[rows, lanes], kr[keys, glanes]) * SCALE
        expo = jnp.exp(jnp.where(allowed, scores, -1e30))
        return expo * (1.0 / jnp.sum(expo, axis=-1, keepdims=True))

    def attend(j):
        size = HALF // PIECES
        for half in range(2):
            if half == 1 and j > 0:
                sum_cross(ATTN, j - 1)
            start = HALF * half + size * j
            end = -(-(start + size) // 128) * 128
            rows = pl.ds(start, size)
            for head in range(6):
                mixed[rows, pl.ds(64 * head, 64)] = jnp.dot(
                    softmax(head, start, size, end).astype(BF16),
                    vals[pl.ds(0, end), pl.ds(64 * (head // 3), 64)],
                    preferred_element_type=F32,
                ).astype(BF16)
            halves[half, pl.ds(size * j, size), :] = jnp.dot(
                mixed[rows], w_out[...], preferred_element_type=F32
            )
        if j == 0:
            await_greetings(partners)
        sum_send(ATTN, j)

    def second_norm(j):
        far[ATTN][j].wait_recv()
        size = HALF // PIECES

        def norm(r):
            r = pl.ds(pl.multiple_of(r.start + j * size, 16), r.size)
            value = tok[core, r].astype(F32) + (sum_own[r] + sum_far[r])
            inverse = lax.rsqrt(jnp.mean(value * value, axis=-1, keepdims=True) + EPSILON)
            low = (value * inverse * gain2[...]).astype(BF16)
            x1[r] = value
            h2[core, r] = low
            sum_near[r] = low.astype(F32)

        by_rows(size, 16, norm)
        back[ATTN][j].start()

    def loads_of(t):
        at, size = TILES[t]
        return [
            pltpu.make_async_copy(
                weight.at[pl.ds(at, size), :],
                row_buf.at[i, pl.ds(256 * (t % 2), size), :],
                row_sem.at[t % 2, i],
            )
            for i, weight in enumerate((w_gate, w_up, w_down))
        ]

    tile_loads = [loads_of(t) for t in range(len(TILES))]

    def load_tile(t):
        for copy in tile_loads[t]:
            copy.start()

    def tile(t):
        at, size = TILES[t]
        cols, rows = pl.ds(at, size), pl.ds(256 * (t % 2), size)
        if t < 2:
            dact = early[t]
        else:
            for copy in tile_loads[t]:
                copy.wait()
            dact = dot_nt(cot[...].reshape(TOK, WIDTH), row_buf[2, rows, :])
        gate, up = (
            dot_nt(h2[...].reshape(TOK, WIDTH), row_buf[i, rows, :]) for i in range(2)
        )
        sigmoid = jax.nn.sigmoid(gate)
        silu = gate * sigmoid
        act[:, cols] = (silu * up).astype(BF16)
        gu[:, cols] = (dact * up * sigmoid * (1.0 + gate * (1.0 - sigmoid))).astype(BF16)
        gu[:, pl.ds(FFL + at, size)] = (dact * silu).astype(BF16)

    def tile_ahead(t):
        for copy in tile_loads[t]:
            copy.wait()
        early[t] = dot_nt(cot[...].reshape(TOK, WIDTH), row_buf[2, pl.ds(256 * t, 256), :])

    def tile_back(p):
        at = 512 * p
        size = min(512, FFL - at)
        inputs = (
            gu[:, pl.ds(at, size)],
            gu[:, pl.ds(FFL + at, size)],
            act[:, pl.ds(at, size)],
        )
        for to in range(0, WIDTH, 512):
            cols = pl.ds(to, 512)
            weights = [row_buf[i, pl.ds(0, size), cols] for i in range(3)]
            dh2, dh2_up, down = (
                jnp.dot(value, weight, preferred_element_type=F32).reshape(2, HALF, 512)
                for value, weight in zip(inputs, weights)
            )
            if p == 0:
                halves[:, :, cols] = dh2 + dh2_up
                ffn[:, :, cols] = down
            else:
                halves[:, :, cols] += dh2 + dh2_up
                ffn[:, :, cols] += down
        for t in range(2 * p + 2, min(2 * p + 4, len(TILES))):
            load_tile(t)

    def hidden_end():
        far[DH2][0].wait_recv()

        def body(i, acc):
            r = pl.ds(pl.multiple_of(i * 16, 16), 16)
            value = x1[r]
            total = sum_own[r] + sum_far[r]
            inverse = lax.rsqrt(jnp.mean(value * value, axis=-1, keepdims=True) + EPSILON)
            scaled = total * gain2[...]
            grad = (
                cot[core, r].astype(F32)
                + inverse * scaled
                - value * inverse**3 * jnp.mean(scaled * value, axis=-1, keepdims=True)
            )
            dg = total * value * inverse
            low = grad.astype(BF16)
            dx1[r] = grad
            da[core, r] = low
            sum_near[r] = low.astype(F32)
            return acc + dg[0:8] + dg[8:16]

        acc = lax.fori_loop(0, HALF // 16, body, jnp.zeros((8, WIDTH), F32))
        back[DH2][0].start()
        small[0, pl.ds(24, 8), :] = jnp.zeros((8, 128), F32)
        norm_row(jnp.sum(acc, axis=0, keepdims=True) * 0.5, 13)

    out_copy = pltpu.make_async_copy(h2, block_out, out_sem.at[0])
    tokens_copy = pltpu.make_async_copy(cot, grad_tokens, out_sem.at[1])

    def out_end():
        far[FFN][0].wait_recv()

        def add(r):
            low = (x1[r] + (ffn[core, r] + sum_far[r])).astype(BF16)
            h2[core, r] = low
            sum_near[r] = low.astype(F32)

        by_rows(HALF, 16, add)
        back[FFN][0].start()

    def out_take():
        sum_take(FFN, h2)
        out_copy.start()

    def tokens_end():
        far[DH1][0].wait_recv()

        def body(i, acc):
            r = pl.ds(pl.multiple_of(i * 16, 16), 16)
            value = tok[core, r].astype(F32)
            total = sum_own[r] + sum_far[r]
            inverse = lax.rsqrt(jnp.mean(value * value, axis=-1, keepdims=True) + EPSILON)
            scaled = total * gain1[...]
            grad = (
                dx1[r]
                + inverse * scaled
                - value * inverse**3 * jnp.mean(scaled * value, axis=-1, keepdims=True)
            )
            dg = total * value * inverse
            low = grad.astype(BF16)
            cot[core, r] = low
            sum_near[r] = low.astype(F32)
            return acc + dg[0:8] + dg[8:16]

        acc = lax.fori_loop(0, HALF // 16, body, jnp.zeros((8, WIDTH), F32))
        back[DH1][0].start()
        norm_row(jnp.sum(acc, axis=0, keepdims=True) * 0.5, 1)
        row = gain_acc[...]
        heads = row[:, 0:128] + row[:, 128:256] + row[:, 256:384]
        heads = heads + pltpu.roll(heads, 64, 1)
        groups = row[:, 384:512] + pltpu.roll(row[:, 384:512], 64, 1)
        lane = lax.broadcasted_iota(jnp.int32, (8, 128), 1)
        both = jnp.where(lane < 64, heads, groups)
        small[0, pl.ds(0, 1), :] = jnp.sum(both, axis=0, keepdims=True)

    def tokens_take():
        sum_take(DH1, cot)
        tokens_copy.start()

    def tables(r):
        return cos[r], sine[r]

    def rotate(r):
        for raw, gain, result in ((qraw, q_gain, qr), (kraw, k_gain, kr)):
            value = raw[r]
            inverse = lax.rsqrt(head_mean(value * value) + EPSILON)
            result[r] = turned(value * inverse * gain[...], *tables(r), 1.0).astype(BF16)

    def mix_back():
        for half in range(2):
            rows = pl.ds(HALF * half, HALF)
            dmixed[rows] = dot_nt(da[half], w_out[...]).astype(BF16)
        dk_t[...] = jnp.zeros((128, TOK), F32)
        dv_t[...] = jnp.zeros((128, TOK), F32)

    def head_back(head):
        lanes, glanes = pl.ds(64 * head, 64), pl.ds(64 * (head // 3), 64)
        for half in range(2):
            rows, keys = pl.ds(HALF * half, HALF), pl.ds(0, HALF * (half + 1))
            q, up = qr[rows, lanes], dmixed[rows, lanes]
            probs = softmax(head, HALF * half, HALF, HALF * (half + 1))
            dprobs = dot_nt(up, vals[keys, glanes])
            dscores = probs * (dprobs - jnp.sum(probs * dprobs, axis=-1, keepdims=True))
            dscores = dscores.astype(BF16)
            dqr[rows, lanes] = (
                jnp.dot(dscores, kr[keys, glanes], preferred_element_type=F32) * SCALE
            )
            dk_t[glanes, keys] += dot_tn(q, dscores) * SCALE
            dv_t[glanes, keys] += dot_tn(up, probs.astype(BF16))

    def raw_back():
        dkr = dk_t[...].T
        dqkv[:, pl.ds(512, 128)] = dv_t[...].T.astype(BF16)
        for i in range(4):
            r = pl.ds(128 * i, 128)
            for raw, gain, up, at in (
                (qraw, q_gain, dqr[r], 0),
                (kraw, k_gain, dkr[128 * i : 128 * i + 128], 384),
            ):
                width = up.shape[1]
                value = raw[r]
                up = turned(up, *tables(r), -1.0)
                inverse = lax.rsqrt(head_mean(value * value) + EPSILON)
                scaled = up * gain[...]
                grad = inverse * scaled - value * inverse**3 * head_mean(scaled * value)
                dqkv[r, pl.ds(at, width)] = grad.astype(BF16)
                part = jnp.sum((up * value * inverse).reshape(16, 8, width), axis=0)
                if i == 0:
                    gain_acc[:, pl.ds(at, width)] = part
                else:
                    gain_acc[:, pl.ds(at, width)] += part

    def first_begin():
        for at in range(0, WIDTH, 256):
            rows = pl.ds(at, 256)
            value = (
                dot_nt(dqkv[:, pl.ds(0, 384)], w_q[rows, :])
                + dot_nt(dqkv[:, pl.ds(384, 128)], w_k[rows, :])
                + dot_nt(dqkv[:, pl.ds(512, 128)], w_v[rows, :])
            )
            halves[:, :, rows] = value.reshape(2, HALF, 256)
        sum_send(DH1)

    spots = (x, y, z, core)
    small_copies = [
        [
            remote(
                small.at[p],
                small_got.at[p, spots[p]],
                small_s.at[p, i],
                small_r.at[p, i],
                partner,
            )
            for i, partner in enumerate(ring[p])
        ]
        for p in range(4)
    ]

    def small_begin(p):
        for copy in small_copies[p]:
            copy.start()
        small_got[p, spots[p]] = small[p]

    def small_end(p):
        for copy in small_copies[p]:
            copy.wait_recv()
        total = small_got[p, 0] + small_got[p, 1]
        if p < 3:
            total = total + small_got[p, 2] + small_got[p, 3]
            small[p + 1] = total
        else:
            small_out[...] = total
        for copy in small_copies[p]:
            copy.wait_send()

    def each(work, *several):
        return lambda: [work(one) for one in several]

    jobs = {
        (0, "relay"): [each(tile_back, 0)],
        (0, "multiply"): [each(tile, 2, 3)],
        (0, "turn2"): [each(tile_back, 1), each(tile, 4, 5)],
        (1, "turn2"): [each(tile_back, 2), each(tile, 6), each(tile_back, 3), each(sum_send, DH2)],
        (1, "end"): [each(sum_cross, DH2)],
        (4, "end"): [hidden_end],
        (5, "turn2"): [lambda: sum_take(DH2, da), each(sum_send, FFN), mix_back, each(head_back, 0, 1)],
        (5, "end"): [each(sum_cross, FFN)],
        (6, "turn2"): [each(head_back, 2, 3, 4, 5)],
        (7, "turn2"): [raw_back],
        (8, "multiply"): [out_end],
        (8, "turn2"): [out_take, first_begin],
        (8, "end"): [each(sum_cross, DH1)],
        (11, "multiply"): [tokens_end, each(small_begin, 0)],
        (11, "turn2"): [tokens_take],
        (11, "end"): [each(small_end, 0), each(small_begin, 1)],
        (12, "turn2"): [each(small_end, 1), each(small_begin, 2)],
        (13, "turn2"): [each(small_end, 2), each(small_begin, 3)],
        (14, "turn2"): [each(small_end, 3)],
    }

    token_load.start()
    for copy in weight_loads:
        copy.start()
    cot_load.start()
    load_tile(0)
    load_tile(1)
    act[:, pl.ds(FFL, PAD - FFL)] = jnp.zeros((TOK, PAD - FFL), BF16)
    lay_tables()
    project()
    by_rows(TOK, 128, rotate)
    for j in range(PIECES):
        attend(j)
    sum_cross(ATTN, PIECES - 1)
    cot_load.wait()
    lay_left(COT)
    tile_ahead(0)
    tile_ahead(1)
    for j in range(PIECES):
        second_norm(j)
    for j in range(PIECES):
        sum_take(ATTN, h2, j)
    tile(0)
    tile(1)
    multiply(0)
    for k in range(count + 2 + LATE):
        steps = (
            ("turn", turn, k - 1),
            ("relay", relay, k),
            ("multiply", multiply, k + 1),
            ("turn2", turn2, k - 2),
            ("relay2", relay2, k - 1),
            ("finish", finish, k - 2 - LATE),
            ("end", None, -1),
        )
        for name, step, at in steps:
            for job in jobs.get((k, name), ()):
                job()
            if 0 <= at < count:
                step(at)
    for k in (count - 2, count - 1):
        for o in range(2):
            for copy in first[k][o]:
                copy.wait_send()
    out_copy.wait()
    tokens_copy.wait()


def block(anywhere_in, vmem_in):
    vmem = pl.BlockSpec(memory_space=pltpu.VMEM)
    anywhere = pl.BlockSpec(memory_space=pl.ANY)
    dma = pltpu.SemaphoreType.DMA
    regular = pltpu.SemaphoreType.REGULAR
    half, rows = (HALF, WIDTH), (2, HALF, WIDTH)
    return pl.pallas_call(
        block_kernel,
        out_shape=(
            jax.ShapeDtypeStruct(rows, BF16),
            jax.ShapeDtypeStruct(rows, BF16),
            jax.ShapeDtypeStruct((48, 384), F32),
            jax.ShapeDtypeStruct((48, 128), F32),
            jax.ShapeDtypeStruct((48, 128), F32),
            jax.ShapeDtypeStruct((48, 384), F32),
            jax.ShapeDtypeStruct((48, FFL), F32),
            jax.ShapeDtypeStruct((48, FFL), F32),
            jax.ShapeDtypeStruct((48, FFL), F32),
            jax.ShapeDtypeStruct((32, 128), F32),
        ),
        in_specs=[anywhere] * len(anywhere_in) + [vmem] * len(vmem_in),
        out_specs=(anywhere,) * 2 + (vmem,) * 8,
        scratch_shapes=[
            pltpu.VMEM(rows, BF16),
            pltpu.VMEM(rows, BF16),
            pltpu.VMEM(rows, BF16),
            pltpu.VMEM(rows, BF16),
            pltpu.VMEM(rows, BF16),
            pltpu.VMEM((WIDTH, TOK), BF16),
            pltpu.VMEM((WIDTH, 384), BF16),
            pltpu.VMEM((WIDTH, 128), BF16),
            pltpu.VMEM((WIDTH, 128), BF16),
            pltpu.VMEM((384, WIDTH), BF16),
            pltpu.VMEM((1, WIDTH), F32),
            pltpu.VMEM((1, WIDTH), F32),
            pltpu.VMEM((1, 384), F32),
            pltpu.VMEM((1, 128), F32),
            pltpu.VMEM((TOK, 128), F32),
            pltpu.VMEM((TOK, 128), F32),
            pltpu.VMEM((TOK, 128), jnp.int32),
            pltpu.VMEM((2, 2, 4, 192, CMAX), F32),
            pltpu.VMEM((2, 2, 6, 96, CMAX), F32),
            pltpu.VMEM((2, 2, 4, 2, 24, CMAX), F32),
            pltpu.VMEM((2, 2, 6, 24, CMAX), F32),
            pltpu.VMEM((2, 2, 24, COLUMNS), F32),
            pltpu.VMEM((2, 24, COLUMNS), F32),
            pltpu.VMEM((2, *half), F32),
            pltpu.VMEM(half, F32),
            pltpu.VMEM(half, F32),
            pltpu.VMEM(half, F32),
            pltpu.VMEM(half, F32),
            pltpu.VMEM(half, F32),
            pltpu.VMEM((4, 32, 128), F32),
            pltpu.VMEM((4, 4, 32, 128), F32),
            pltpu.VMEM((8, 512), F32),
            pltpu.VMEM((TOK, 384), F32),
            pltpu.VMEM((TOK, 128), F32),
            pltpu.VMEM((TOK, 128), BF16),
            pltpu.VMEM((TOK, 384), BF16),
            pltpu.VMEM((TOK, 384), BF16),
            pltpu.VMEM((TOK, 128), BF16),
            pltpu.VMEM((TOK, 384), BF16),
            pltpu.VMEM((TOK, 384), F32),
            pltpu.VMEM((128, TOK), F32),
            pltpu.VMEM((128, TOK), F32),
            pltpu.VMEM((TOK, 640), BF16),
            pltpu.VMEM((TOK, PAD), BF16),
            pltpu.VMEM((TOK, 2 * FFL), BF16),
            pltpu.VMEM((2, *half), F32),
            pltpu.VMEM((3, 512, WIDTH), BF16),
            pltpu.VMEM((2, TOK, 256), F32),
            dma((2, 2, 6)),
            dma((2, 2, 6)),
            dma((2, 2, 6)),
            dma((2, 2, 6)),
            dma((len(CHUNKS), 2)),
            dma((len(CHUNKS), 2)),
            regular((4,)),
            regular((4,)),
            dma((6,)),
            dma((2, 3)),
            dma((4, 3, PIECES)),
            dma((4, 3, PIECES)),
            regular((2,)),
            dma((4, 3)),
            dma((4, 3)),
            dma((2,)),
        ],
        compiler_params=pltpu.CompilerParams(
            collective_id=0, has_side_effects=True, vmem_limit_bytes=VMEM_MIB * MIB
        ),
        name="whole",
    )(*anywhere_in, *vmem_in)


def hand_on_kernel(*refs):
    count = (len(refs) - 2) // 3
    sources, results, held = refs[:count], refs[count : 2 * count], refs[2 * count : 3 * count]
    in_sem, out_sem = refs[3 * count :]
    reads = [
        pltpu.make_async_copy(one, at, in_sem.at[i])
        for i, (one, at) in enumerate(zip(sources, held))
    ]
    writes = [
        pltpu.make_async_copy(at, one, out_sem.at[i])
        for i, (one, at) in enumerate(zip(results, held))
    ]
    for read in reads:
        read.start()
    for read, write in zip(reads, writes):
        read.wait()
        write.start()
    for write in writes:
        write.wait()


def hand_on(arrays):
    anywhere = pl.BlockSpec(memory_space=pl.ANY)
    return pl.pallas_call(
        hand_on_kernel,
        out_shape=tuple(jax.ShapeDtypeStruct(one.shape, one.dtype) for one in arrays),
        in_specs=[anywhere] * len(arrays),
        out_specs=(anywhere,) * len(arrays),
        scratch_shapes=[pltpu.VMEM(one.shape, one.dtype) for one in arrays]
        + [pltpu.SemaphoreType.DMA((len(arrays),))] * 2,
        compiler_params=pltpu.CompilerParams(vmem_limit_bytes=VMEM_MIB * MIB),
        name="hand_on",
    )(*arrays)


def per_device(
    tokens,
    segments,
    norm_one,
    w_query,
    key_projection,
    value_projection,
    w_out,
    q_gain,
    k_gain,
    norm_two,
    w_gate,
    w_up,
    w_down,
    cotangent,
):
    outs = block(
        (
            tokens.reshape(2, HALF, WIDTH),
            cotangent.reshape(2, HALF, WIDTH),
            w_gate.T,
            w_up.T,
            w_down,
            w_query,
            key_projection,
            value_projection,
            w_out,
        ),
        (
            norm_one,
            norm_two,
            q_gain,
            k_gain,
            segments,
            np.tile(FREQUENCY, 4).reshape(1, 128),
        ),
    )
    small = outs[-1]
    block_out, grad_tokens, query, key, value, out, gate, upper, down = hand_on(outs[:-1])
    norms = lax.dynamic_slice_in_dim(
        small[1:25].reshape(2, WIDTH), lax.axis_index("dp") * 48, 48, axis=1
    )
    return (
        block_out.reshape(TOK, WIDTH),
        grad_tokens.reshape(TOK, WIDTH),
        norms[0],
        query,
        key,
        value,
        out.T,
        small[0, :64],
        small[0, 64:],
        norms[1],
        gate,
        upper,
        down.T,
    )


def solution(mesh):
    placed = (
        P("dp", None),
        P("dp", None),
        P(),
        P(None, "tensor"),
        P(None, "tensor"),
        P(None, "tensor"),
        P("tensor", None),
        P(),
        P(),
        P(),
        P(None, "tensor"),
        P(None, "tensor"),
        P("tensor", None),
        P("dp", None),
    )
    return jax.shard_map(
        per_device,
        mesh=mesh,
        in_specs=placed,
        out_specs=(
            P("dp", None),
            P("dp", None),
            P("dp"),
            P("dp", "tensor"),
            P("dp", "tensor"),
            P("dp", "tensor"),
            P("tensor", "dp"),
            P(),
            P(),
            P("dp"),
            P("dp", "tensor"),
            P("dp", "tensor"),
            P("tensor", "dp"),
        ),
        check_vma=False,
    )
```

```python
import jax
import jax.numpy as jnp
import numpy as np
from jax import lax
from jax.experimental import pallas as pl
from jax.experimental.pallas import tpu as pltpu
from jax.sharding import PartitionSpec as P

HEAD_SIZE = 64


EPSILON = 1e-05
THETA = 1000000.0
FREQUENCY = np.float32(THETA) ** (-np.arange(32, dtype=np.float32) * 2 / HEAD_SIZE)


MESH = pl.DeviceIdType.MESH
F32 = jnp.float32
BF16 = jnp.bfloat16
WIDTH = 1536
TOK = 512
HALF = 256
FFL = 1728
MIB = 1 << 20
VMEM_MIB = 63


def place():
    dp = lax.axis_index("dp")
    tensor = lax.axis_index("tensor")
    x = lax.div(dp, 8)
    y = lax.rem(lax.div(dp, 2), 4)
    z = lax.div(tensor, 2) * 2 + lax.rem(dp, 2)
    return x, y, z, lax.rem(tensor, 2)


def device(x, y, z, core):
    return (x * 8 + y * 2 + lax.rem(z, 2), lax.div(z, 2) * 2 + core)


def greet(partners):
    barrier = pltpu.get_barrier_semaphore()
    for partner in partners:
        pl.semaphore_signal(barrier, inc=1, device_id=partner, device_id_type=MESH)


def await_greetings(partners):
    pl.semaphore_wait(pltpu.get_barrier_semaphore(), len(partners))


def remote(source, target, send_sem, recv_sem, partner):
    return pltpu.make_async_remote_copy(
        src_ref=source,
        dst_ref=target,
        send_sem=send_sem,
        recv_sem=recv_sem,
        device_id=partner,
        device_id_type=MESH,
    )


def by_rows(count, step, work):
    def body(i, carry):
        work(pl.ds(pl.multiple_of(i * step, step), step))
        return carry

    lax.fori_loop(0, count // step, body, 0)


CMAX = 512
COT, H2, H1, DA = range(4)
ACT, GU, QKV, MIX = range(4)
CHUNKS = (
    (COT, ACT, 0, 512),
    (COT, ACT, 512, 512),
    (COT, ACT, 1024, 512),
    (COT, ACT, 1536, 256),
    (H2, GU, 0, 512),
    (H2, GU, 512, 512),
    (H2, GU, 1024, 512),
    (H2, GU, 1536, 512),
    (H2, GU, 2048, 512),
    (H2, GU, 2560, 512),
    (H2, GU, 3072, 384),
    (DA, MIX, 0, 384),
    (H1, QKV, 0, 384),
    (H1, QKV, 384, 256),
)
COLUMNS = sum(chunk[3] for chunk in CHUNKS)
TILES = tuple((at, min(256, FFL - at)) for at in range(0, FFL, 256))
PAD = 1792
ATTN, DH2, DH1, FFN = range(4)
PIECES = 8
LATE = 4
XP, XM, YP, YM = range(4)
OPPOSITE = (XM, XP, YM, YP)
SCALE = HEAD_SIZE ** (-0.5)


def dot_nt(left, right):
    return lax.dot_general(left, right, (((1,), (1,)), ((), ())), preferred_element_type=F32)


def dot_tn(left, right):
    return lax.dot_general(left, right, (((0,), (0,)), ((), ())), preferred_element_type=F32)


def head_mean(values):
    row = lax.broadcasted_iota(jnp.int32, (128, 128), 0)
    col = lax.broadcasted_iota(jnp.int32, (128, 128), 1)
    same = jnp.where((row < 64) == (col < 64), 1.0 / 64, 0.0)
    return jnp.concatenate(
        [
            jnp.dot(values[:, at : at + 128], same, preferred_element_type=F32)
            for at in range(0, values.shape[1], 128)
        ],
        axis=1,
    )


def turned(values, cos, sine, sign):
    width = values.shape[1]
    cos, sine = (jnp.concatenate([table] * (width // 128), axis=1) for table in (cos, sine))
    ahead = pltpu.roll(values, width - 32, 1)
    behind = pltpu.roll(values, 32, 1)
    lane = lax.broadcasted_iota(jnp.int32, values.shape, 1)
    other = jnp.where(lax.rem(lane, 64) < 32, -ahead, behind)
    return values * cos + sign * (other * sine)


def block_kernel(*refs):
    tokens, cotangent, w_gate, w_up, w_down, refs = *refs[:5], refs[5:]
    projections, refs = refs[:4], refs[4:]
    norm_one, norm_two, q_line, k_line, segments, frequency, refs = *refs[:6], refs[6:]
    block_out, grad_tokens, out_q, out_k, out_v, out_o, out_gate, out_up, out_down, small_out, refs = (
        *refs[:10],
        refs[10:],
    )
    tok, cot, h1, h2, da, left_t, refs = *refs[:6], refs[6:]
    w_q, w_k, w_v, w_out, refs = *refs[:4], refs[4:]
    gain1, gain2, q_gain, k_gain, cos, sine, begin, refs = *refs[:7], refs[7:]
    product, got, passed, got2, keep, got3, refs = *refs[:6], refs[6:]
    halves, sum_near, sum_far, sum_back, x1, dx1, refs = *refs[:6], refs[6:]
    small, small_got, gain_acc, refs = *refs[:3], refs[3:]
    qraw, kraw, vals, mixed, qr, kr, dmixed, dqr, dk_t, dv_t, dqkv, refs = *refs[:11], refs[11:]
    act, gu, ffn, row_buf, early, refs = *refs[:5], refs[5:]
    s1, r1, s2, r2, s3, r3, credit, credit2, refs = *refs[:8], refs[8:]
    load_sem, row_sem, sum_s, sum_r, free, small_s, small_r, out_sem = refs

    x, y, z, core = place()
    around = (
        device(lax.rem(x + 1, 4), y, z, core),
        device(lax.rem(x + 3, 4), y, z, core),
        device(x, lax.rem(y + 1, 4), z, core),
        device(x, lax.rem(y + 3, 4), z, core),
    )
    z_lo = lax.rem(z, 2)
    beside = device(x, y, z + 1 - 2 * z_lo, core)
    mate = device(x, y, z, 1 - core)
    across = device(x, y, lax.rem(z + 2, 4), core)
    ring = (
        [device(lax.rem(x + i, 4), y, z, core) for i in (1, 2, 3)],
        [device(x, lax.rem(y + i, 4), z, core) for i in (1, 2, 3)],
        [device(x, y, lax.rem(z + i, 4), core) for i in (1, 2, 3)],
        [mate],
    )
    partners = [one for group in ring for one in group]
    greet(partners)

    part, sum_own = halves.at[1 - core], halves.at[core]
    count = len(CHUNKS)
    place1, place2 = (x, y), (y, x)
    forward1, backward1 = (around[XP], around[YP]), (around[XM], around[YM])
    forward2, backward2 = (around[YP], around[XP]), (around[YM], around[XM])

    def new_left(k):
        return k == 0 or CHUNKS[k][0] != CHUNKS[k - 1][0]

    first, second, third = [], [], []
    starts = [sum(chunk[3] for chunk in CHUNKS[:k]) for k in range(count)]
    for k, chunk in enumerate(CHUNKS):
        slot, cols = k % 2, pl.ds(0, chunk[3])
        per1, per2, per3 = [], [], []
        for o in range(2):
            far_block = lax.rem(place1[o] + 2, 4)
            after, before = lax.rem(place1[o] + 1, 4), lax.rem(place1[o] + 3, 4)
            top, low = pl.ds(0, 96), pl.ds(96, 96)
            plan = (
                (far_block, top, forward1[o]),
                (far_block, low, backward1[o]),
                (after, low, forward1[o]),
                (before, top, backward1[o]),
                (after, top, forward1[o]),
                (before, low, backward1[o]),
            )
            per1.append(
                [
                    remote(
                        product.at[slot, o, block, rows, cols],
                        got.at[slot, o, i, :, cols],
                        s1.at[slot, o, i],
                        r1.at[slot, o, i],
                        partner,
                    )
                    for i, (block, rows, partner) in enumerate(plan)
                ]
            )
            far_block = lax.rem(place2[o] + 2, 4)
            after, before = lax.rem(place2[o] + 1, 4), lax.rem(place2[o] + 3, 4)
            plan = (
                (far_block, 0, forward2[o]),
                (far_block, 1, backward2[o]),
                (after, 1, forward2[o]),
                (before, 0, backward2[o]),
                (after, 0, forward2[o]),
                (before, 1, backward2[o]),
            )
            per2.append(
                [
                    remote(
                        passed.at[slot, o, block, half, :, cols],
                        got2.at[slot, o, i, :, cols],
                        s2.at[slot, o, i],
                        r2.at[slot, o, i],
                        partner,
                    )
                    for i, (block, half, partner) in enumerate(plan)
                ]
            )
            per3.append(
                remote(
                    keep.at[o, 1 - z_lo, :, pl.ds(starts[k], chunk[3])],
                    got3.at[o, :, pl.ds(starts[k], chunk[3])],
                    s3.at[k, o],
                    r3.at[k, o],
                    beside,
                )
            )
        first.append(per1)
        second.append(per2)
        third.append(per3)

    def lay_left(left):
        source = (cot, h2, h1, da)[left]
        for half in range(2):
            for at in range(0, WIDTH, 384):
                left_t[pl.ds(at, 384), pl.ds(HALF * half, HALF)] = source[
                    half, :, pl.ds(at, 384)
                ].T

    def multiply(k):
        slot, (left, right, start, width) = k % 2, CHUNKS[k]
        if k > 0 and new_left(k):
            lay_left(left)
        if k >= 2:
            for o in range(2):
                for copy in first[k - 2][o]:
                    copy.wait_send()
        operand = (act, gu, dqkv, mixed)[right]

        def block(b, carry):
            rows = pl.ds(pl.multiple_of(b * 384, 384), 384)
            for at in range(0, width, 256):
                size = min(256, width - at)
                cols = pl.ds(at, size)
                tile = jnp.dot(
                    left_t[rows, :],
                    operand[:, pl.ds(start + at, size)],
                    preferred_element_type=F32,
                )
                for q in range(8):
                    product[slot, 0, b, pl.ds(24 * q, 24), cols] = tile[48 * q : 48 * q + 24]
                    to = pl.ds(pl.multiple_of(48 * b + 24 * (q % 2), 24), 24)
                    product[slot, 1, q // 2, to, cols] = tile[48 * q + 24 : 48 * q + 48]
            return carry

        lax.fori_loop(0, 4, block, 0)
        if k >= 2:
            for d in range(4):
                pl.semaphore_wait(credit.at[d], 1)
        for i in range(4):
            for o in range(2):
                first[k][o][i].start()

    def relay(k):
        slot, width = k % 2, CHUNKS[k][3]
        cols = pl.ds(0, width)
        for i, shift, base in ((0, 1, 0), (1, 3, 96)):
            for o in range(2):
                first[k][o][i].wait_recv()
                b = lax.rem(place1[o] + shift, 4)

                def add(r, o=o, i=i, b=b, base=base):
                    to = pl.ds(pl.multiple_of(r.start + base, 8), r.size)
                    product[slot, o, b, to, cols] = (
                        product[slot, o, b, to, cols] + got[slot, o, i, r, cols]
                    )

                by_rows(96, 24, add)
                first[k][o][4 + i].start()

    def turn(k):
        slot, width = k % 2, CHUNKS[k][3]
        cols = pl.ds(0, width)
        for o in range(2):
            for i in range(2, 6):
                first[k][o][i].wait_recv()
            b = place1[o]

            def add(q, carry, o=o, b=b):
                for h in range(2):
                    for half, i, j in ((0, 3, 4), (1, 2, 5)):
                        mine = pl.ds(pl.multiple_of(96 * half + 48 * q + 24 * h, 8), 24)
                        theirs = pl.ds(pl.multiple_of(48 * q + 24 * h, 8), 24)
                        passed[slot, o, 2 * half + q, h, :, cols] = (
                            product[slot, o, b, mine, cols]
                            + got[slot, o, i, theirs, cols]
                            + got[slot, o, j, theirs, cols]
                        )
                return carry

            lax.fori_loop(0, 2, add, 0)
            if k >= 2:
                for d in ((YP, YM), (XP, XM))[o]:
                    pl.semaphore_wait(credit2.at[d], 1)
            for i in range(4):
                second[k][o][i].start()
        if k + 2 < count:
            for d in range(4):
                pl.semaphore_signal(
                    credit.at[OPPOSITE[d]], inc=1, device_id=around[d], device_id_type=MESH
                )

    def relay2(k):
        slot, width = k % 2, CHUNKS[k][3]
        cols = pl.ds(0, width)
        for o in range(2):
            for i, shift in ((0, 1), (1, 3)):
                second[k][o][i].wait_recv()
                b = lax.rem(place2[o] + shift, 4)
                passed[slot, o, b, i, :, cols] = (
                    passed[slot, o, b, i, :, cols] + got2[slot, o, i, :, cols]
                )
                second[k][o][4 + i].start()

    def turn2(k):
        slot, width = k % 2, CHUNKS[k][3]
        cols = pl.ds(0, width)
        for o in range(2):
            b = place2[o]
            for h, i, j in ((0, 3, 4), (1, 2, 5)):
                second[k][o][i].wait_recv()
                second[k][o][j].wait_recv()
                keep[o, h, :, pl.ds(starts[k], width)] = (
                    passed[slot, o, b, h, :, cols]
                    + got2[slot, o, i, :, cols]
                    + got2[slot, o, j, :, cols]
                )
        for o in range(2):
            third[k][o].start()
        if k + 2 < count:
            for d in range(4):
                pl.semaphore_signal(
                    credit2.at[OPPOSITE[d]], inc=1, device_id=around[d], device_id_type=MESH
                )
        for o in range(2):
            for copy in second[k][o]:
                copy.wait_send()

    def finish(k):
        _, which, start, width = CHUNKS[k]
        cols = pl.ds(starts[k], width)
        for o in range(2):
            third[k][o].wait_recv()
            rows = pl.ds(24 * o, 24)
            value = keep[o, z_lo, :, cols] + got3[o, :, cols]
            outs, edges = {
                ACT: ((out_down,), (0, FFL)),
                GU: ((out_gate, out_up), (0, FFL, 2 * FFL)),
                QKV: ((out_q, out_k, out_v), (0, 384, 512, 640)),
                MIX: ((out_o,), (0, 384)),
            }[which]
            for out, low, high in zip(outs, edges[:-1], edges[1:]):
                low_at, high_at = max(low, start), min(high, start + width)
                if low_at < high_at:
                    out[rows, pl.ds(low_at - low, high_at - low_at)] = value[
                        :, low_at - start : high_at - start
                    ]
            third[k][o].wait_send()

    def sum_copies(a):
        pieces = PIECES if a == ATTN else 1
        size = HALF // pieces
        other, own = (ffn.at[1 - core], ffn.at[core]) if a == FFN else (part, sum_own)
        plan = ((other, sum_near, mate), (own, sum_far, across), (sum_near, sum_back, mate))
        return [
            [
                remote(
                    source.at[pl.ds(j * size, size)],
                    target.at[pl.ds(j * size, size)],
                    sum_s.at[a, i, j],
                    sum_r.at[a, i, j],
                    partner,
                )
                for j in range(pieces)
            ]
            for i, (source, target, partner) in enumerate(plan)
        ]

    near, far, back = zip(*[sum_copies(a) for a in range(4)])

    def sum_cross(a, j=0):
        near[a][j].wait_recv()
        size = HALF // len(near[a])
        own = ffn.at[core] if a == FFN else sum_own

        def add(r):
            r = pl.ds(pl.multiple_of(r.start + j * size, 16), r.size)
            own[r] = own[r] + sum_near[r]

        by_rows(size, 16, add)
        if a > 0 and j == 0:
            pl.semaphore_wait(free.at[1], 1)
        far[a][j].start()

    def sum_send(a, j=0):
        if a > 0:
            pl.semaphore_wait(free.at[0], 1)
        near[a][j].start()

    def sum_take(a, result, j=0):
        back[a][j].wait_recv()
        size = HALF // len(near[a])

        def put(r):
            r = pl.ds(pl.multiple_of(r.start + j * size, 16), r.size)
            result[1 - core, r] = sum_back[r].astype(BF16)

        by_rows(size, 16, put)
        if j + 1 == len(near[a]):
            for copy in near[a] + far[a] + back[a]:
                copy.wait_send()
            if a != DH1:
                pl.semaphore_signal(free.at[0], inc=1, device_id=mate, device_id_type=MESH)
                pl.semaphore_signal(free.at[1], inc=1, device_id=across, device_id_type=MESH)

    def norm_row(row, at):
        for i in range(12):
            small[0, pl.ds(at + i, 1), :] = row[:, 128 * i : 128 * i + 128]

    token_load = pltpu.make_async_copy(tokens, tok, load_sem.at[0])
    cot_load = pltpu.make_async_copy(cotangent, cot, load_sem.at[1])
    weight_loads = [
        pltpu.make_async_copy(source, target, load_sem.at[2 + i])
        for i, (source, target) in enumerate(zip(projections, (w_q, w_k, w_v, w_out)))
    ]

    def lay_tables():
        gain1[...] = norm_one[...].reshape(1, WIDTH)
        gain2[...] = norm_two[...].reshape(1, WIDTH)
        q_gain[...] = jnp.concatenate([q_line[...].reshape(1, HEAD_SIZE)] * 6, axis=1)
        k_gain[...] = jnp.concatenate([k_line[...].reshape(1, HEAD_SIZE)] * 2, axis=1)
        row = segments[...].astype(F32)
        starts = [
            jnp.sum(jnp.where(row < value, 1.0, 0.0), axis=1, keepdims=True)
            for value in (0.5, 1.5, 2.5)
        ]
        wide = jnp.broadcast_to(row, (128, TOK)).T
        first = jnp.where(
            wide < 0.5,
            0.0,
            jnp.where(wide < 1.5, starts[0], jnp.where(wide < 2.5, starts[1], starts[2])),
        )
        begin[...] = first.astype(jnp.int32)
        position = lax.broadcasted_iota(jnp.int32, (TOK, 128), 0).astype(F32) - first
        lane = lax.broadcasted_iota(jnp.int32, (128, 128), 1)
        packed = position[:128]
        for g in range(1, 4):
            packed = jnp.where(lane < 32 * g, packed, position[128 * g : 128 * g + 128])
        angles = packed * frequency[...]
        for table, value in ((cos, jnp.cos(angles)), (sine, jnp.sin(angles))):
            for g in range(4):
                mine = value if g == 0 else pltpu.roll(value, 128 - 32 * g, 1)
                mine = jnp.where(lane < 32, mine, 0.0)
                mine = mine + pltpu.roll(mine, 32, 1)
                table[pl.ds(128 * g, 128)] = mine + pltpu.roll(mine, 64, 1)

    def project():
        token_load.wait()

        def norm(i, carry):
            for half in range(2):
                r = pl.ds(pl.multiple_of(i * 16, 16), 16)
                value = tok[half, r].astype(F32)
                inverse = lax.rsqrt(jnp.mean(value * value, axis=-1, keepdims=True) + EPSILON)
                h1[half, r] = (value * inverse * gain1[...]).astype(BF16)
            return carry

        lax.fori_loop(0, HALF // 16, norm, 0)
        for copy in weight_loads:
            copy.wait()
        value = h1[...].reshape(TOK, WIDTH)
        qraw[...] = jnp.dot(value, w_q[...], preferred_element_type=F32)
        kraw[...] = jnp.dot(value, w_k[...], preferred_element_type=F32)
        vals[...] = jnp.dot(value, w_v[...], preferred_element_type=F32).astype(BF16)

    def softmax(head, start, size, end):
        lanes, glanes = pl.ds(64 * head, 64), pl.ds(64 * (head // 3), 64)
        rows, keys = pl.ds(start, size), pl.ds(0, end)
        row = lax.broadcasted_iota(jnp.int32, (size, end), 0) + start
        col = lax.broadcasted_iota(jnp.int32, (size, end), 1)
        allowed = (col <= row) & (col >= begin[rows, pl.ds(0, 1)])
        scores = dot_nt(qr[rows, lanes], kr[keys, glanes]) * SCALE
        expo = jnp.exp(jnp.where(allowed, scores, -1e30))
        return expo * (1.0 / jnp.sum(expo, axis=-1, keepdims=True))

    def attend(j):
        size = HALF // PIECES
        for half in range(2):
            if half == 1 and j > 0:
                sum_cross(ATTN, j - 1)
            start = HALF * half + size * j
            end = -(-(start + size) // 128) * 128
            rows = pl.ds(start, size)
            for head in range(6):
                mixed[rows, pl.ds(64 * head, 64)] = jnp.dot(
                    softmax(head, start, size, end).astype(BF16),
                    vals[pl.ds(0, end), pl.ds(64 * (head // 3), 64)],
                    preferred_element_type=F32,
                ).astype(BF16)
            halves[half, pl.ds(size * j, size), :] = jnp.dot(
                mixed[rows], w_out[...], preferred_element_type=F32
            )
        if j == 0:
            await_greetings(partners)
        sum_send(ATTN, j)

    def second_norm(j):
        far[ATTN][j].wait_recv()
        size = HALF // PIECES

        def norm(r):
            r = pl.ds(pl.multiple_of(r.start + j * size, 16), r.size)
            value = tok[core, r].astype(F32) + (sum_own[r] + sum_far[r])
            inverse = lax.rsqrt(jnp.mean(value * value, axis=-1, keepdims=True) + EPSILON)
            low = (value * inverse * gain2[...]).astype(BF16)
            x1[r] = value
            h2[core, r] = low
            sum_near[r] = low.astype(F32)

        by_rows(size, 16, norm)
        back[ATTN][j].start()

    def loads_of(t):
        at, size = TILES[t]
        return [
            pltpu.make_async_copy(
                weight.at[pl.ds(at, size), :],
                row_buf.at[i, pl.ds(256 * (t % 2), size), :],
                row_sem.at[t % 2, i],
            )
            for i, weight in enumerate((w_gate, w_up, w_down))
        ]

    tile_loads = [loads_of(t) for t in range(len(TILES))]

    def load_tile(t):
        for copy in tile_loads[t]:
            copy.start()

    def tile(t):
        at, size = TILES[t]
        cols, rows = pl.ds(at, size), pl.ds(256 * (t % 2), size)
        if t < 2:
            dact = early[t]
        else:
            for copy in tile_loads[t]:
                copy.wait()
            dact = dot_nt(cot[...].reshape(TOK, WIDTH), row_buf[2, rows, :])
        gate, up = (
            dot_nt(h2[...].reshape(TOK, WIDTH), row_buf[i, rows, :]) for i in range(2)
        )
        sigmoid = jax.nn.sigmoid(gate)
        silu = gate * sigmoid
        act[:, cols] = (silu * up).astype(BF16)
        gu[:, cols] = (dact * up * sigmoid * (1.0 + gate * (1.0 - sigmoid))).astype(BF16)
        gu[:, pl.ds(FFL + at, size)] = (dact * silu).astype(BF16)

    def tile_ahead(t):
        for copy in tile_loads[t]:
            copy.wait()
        early[t] = dot_nt(cot[...].reshape(TOK, WIDTH), row_buf[2, pl.ds(256 * t, 256), :])

    def tile_back(p):
        at = 512 * p
        size = min(512, FFL - at)
        inputs = (
            gu[:, pl.ds(at, size)],
            gu[:, pl.ds(FFL + at, size)],
            act[:, pl.ds(at, size)],
        )
        for to in range(0, WIDTH, 512):
            cols = pl.ds(to, 512)
            weights = [row_buf[i, pl.ds(0, size), cols] for i in range(3)]
            dh2, dh2_up, down = (
                jnp.dot(value, weight, preferred_element_type=F32).reshape(2, HALF, 512)
                for value, weight in zip(inputs, weights)
            )
            if p == 0:
                halves[:, :, cols] = dh2 + dh2_up
                ffn[:, :, cols] = down
            else:
                halves[:, :, cols] += dh2 + dh2_up
                ffn[:, :, cols] += down
        for t in range(2 * p + 2, min(2 * p + 4, len(TILES))):
            load_tile(t)

    def hidden_end():
        far[DH2][0].wait_recv()

        def body(i, acc):
            r = pl.ds(pl.multiple_of(i * 16, 16), 16)
            value = x1[r]
            total = sum_own[r] + sum_far[r]
            inverse = lax.rsqrt(jnp.mean(value * value, axis=-1, keepdims=True) + EPSILON)
            scaled = total * gain2[...]
            grad = (
                cot[core, r].astype(F32)
                + inverse * scaled
                - value * inverse**3 * jnp.mean(scaled * value, axis=-1, keepdims=True)
            )
            dg = total * value * inverse
            low = grad.astype(BF16)
            dx1[r] = grad
            da[core, r] = low
            sum_near[r] = low.astype(F32)
            return acc + dg[0:8] + dg[8:16]

        acc = lax.fori_loop(0, HALF // 16, body, jnp.zeros((8, WIDTH), F32))
        back[DH2][0].start()
        small[0, pl.ds(24, 8), :] = jnp.zeros((8, 128), F32)
        norm_row(jnp.sum(acc, axis=0, keepdims=True) * 0.5, 13)

    out_copy = pltpu.make_async_copy(h2, block_out, out_sem.at[0])
    tokens_copy = pltpu.make_async_copy(cot, grad_tokens, out_sem.at[1])

    def out_end():
        far[FFN][0].wait_recv()

        def add(r):
            low = (x1[r] + (ffn[core, r] + sum_far[r])).astype(BF16)
            h2[core, r] = low
            sum_near[r] = low.astype(F32)

        by_rows(HALF, 16, add)
        back[FFN][0].start()

    def out_take():
        sum_take(FFN, h2)
        out_copy.start()

    def tokens_end():
        far[DH1][0].wait_recv()

        def body(i, acc):
            r = pl.ds(pl.multiple_of(i * 16, 16), 16)
            value = tok[core, r].astype(F32)
            total = sum_own[r] + sum_far[r]
            inverse = lax.rsqrt(jnp.mean(value * value, axis=-1, keepdims=True) + EPSILON)
            scaled = total * gain1[...]
            grad = (
                dx1[r]
                + inverse * scaled
                - value * inverse**3 * jnp.mean(scaled * value, axis=-1, keepdims=True)
            )
            dg = total * value * inverse
            low = grad.astype(BF16)
            cot[core, r] = low
            sum_near[r] = low.astype(F32)
            return acc + dg[0:8] + dg[8:16]

        acc = lax.fori_loop(0, HALF // 16, body, jnp.zeros((8, WIDTH), F32))
        back[DH1][0].start()
        norm_row(jnp.sum(acc, axis=0, keepdims=True) * 0.5, 1)
        row = gain_acc[...]
        heads = row[:, 0:128] + row[:, 128:256] + row[:, 256:384]
        heads = heads + pltpu.roll(heads, 64, 1)
        groups = row[:, 384:512] + pltpu.roll(row[:, 384:512], 64, 1)
        lane = lax.broadcasted_iota(jnp.int32, (8, 128), 1)
        both = jnp.where(lane < 64, heads, groups)
        small[0, pl.ds(0, 1), :] = jnp.sum(both, axis=0, keepdims=True)

    def tokens_take():
        sum_take(DH1, cot)
        tokens_copy.start()

    def tables(r):
        return cos[r], sine[r]

    def rotate(r):
        for raw, gain, result in ((qraw, q_gain, qr), (kraw, k_gain, kr)):
            value = raw[r]
            inverse = lax.rsqrt(head_mean(value * value) + EPSILON)
            result[r] = turned(value * inverse * gain[...], *tables(r), 1.0).astype(BF16)

    def mix_back():
        for half in range(2):
            rows = pl.ds(HALF * half, HALF)
            dmixed[rows] = dot_nt(da[half], w_out[...]).astype(BF16)
        dk_t[...] = jnp.zeros((128, TOK), F32)
        dv_t[...] = jnp.zeros((128, TOK), F32)

    def head_back(head):
        lanes, glanes = pl.ds(64 * head, 64), pl.ds(64 * (head // 3), 64)
        for half in range(2):
            rows, keys = pl.ds(HALF * half, HALF), pl.ds(0, HALF * (half + 1))
            q, up = qr[rows, lanes], dmixed[rows, lanes]
            probs = softmax(head, HALF * half, HALF, HALF * (half + 1))
            dprobs = dot_nt(up, vals[keys, glanes])
            dscores = probs * (dprobs - jnp.sum(probs * dprobs, axis=-1, keepdims=True))
            dscores = dscores.astype(BF16)
            dqr[rows, lanes] = (
                jnp.dot(dscores, kr[keys, glanes], preferred_element_type=F32) * SCALE
            )
            dk_t[glanes, keys] += dot_tn(q, dscores) * SCALE
            dv_t[glanes, keys] += dot_tn(up, probs.astype(BF16))

    def raw_back():
        dkr = dk_t[...].T
        dqkv[:, pl.ds(512, 128)] = dv_t[...].T.astype(BF16)
        for i in range(4):
            r = pl.ds(128 * i, 128)
            for raw, gain, up, at in (
                (qraw, q_gain, dqr[r], 0),
                (kraw, k_gain, dkr[128 * i : 128 * i + 128], 384),
            ):
                width = up.shape[1]
                value = raw[r]
                up = turned(up, *tables(r), -1.0)
                inverse = lax.rsqrt(head_mean(value * value) + EPSILON)
                scaled = up * gain[...]
                grad = inverse * scaled - value * inverse**3 * head_mean(scaled * value)
                dqkv[r, pl.ds(at, width)] = grad.astype(BF16)
                part = jnp.sum((up * value * inverse).reshape(16, 8, width), axis=0)
                if i == 0:
                    gain_acc[:, pl.ds(at, width)] = part
                else:
                    gain_acc[:, pl.ds(at, width)] += part

    def first_begin():
        for at in range(0, WIDTH, 256):
            rows = pl.ds(at, 256)
            value = (
                dot_nt(dqkv[:, pl.ds(0, 384)], w_q[rows, :])
                + dot_nt(dqkv[:, pl.ds(384, 128)], w_k[rows, :])
                + dot_nt(dqkv[:, pl.ds(512, 128)], w_v[rows, :])
            )
            halves[:, :, rows] = value.reshape(2, HALF, 256)
        sum_send(DH1)

    spots = (x, y, z, core)
    small_copies = [
        [
            remote(
                small.at[p],
                small_got.at[p, spots[p]],
                small_s.at[p, i],
                small_r.at[p, i],
                partner,
            )
            for i, partner in enumerate(ring[p])
        ]
        for p in range(4)
    ]

    def small_begin(p):
        for copy in small_copies[p]:
            copy.start()
        small_got[p, spots[p]] = small[p]

    def small_end(p):
        for copy in small_copies[p]:
            copy.wait_recv()
        total = small_got[p, 0] + small_got[p, 1]
        if p < 3:
            total = total + small_got[p, 2] + small_got[p, 3]
            small[p + 1] = total
        else:
            small_out[...] = total
        for copy in small_copies[p]:
            copy.wait_send()

    def each(work, *several):
        return lambda: [work(one) for one in several]

    jobs = {
        (0, "relay"): [each(tile_back, 0)],
        (0, "multiply"): [each(tile, 2, 3)],
        (0, "turn2"): [each(tile_back, 1), each(tile, 4, 5)],
        (1, "turn2"): [each(tile_back, 2), each(tile, 6), each(tile_back, 3), each(sum_send, DH2)],
        (1, "end"): [each(sum_cross, DH2)],
        (4, "end"): [hidden_end],
        (5, "turn2"): [lambda: sum_take(DH2, da), each(sum_send, FFN), mix_back, each(head_back, 0, 1)],
        (5, "end"): [each(sum_cross, FFN)],
        (6, "turn2"): [each(head_back, 2, 3, 4, 5)],
        (7, "turn2"): [raw_back],
        (8, "multiply"): [out_end],
        (8, "turn2"): [out_take, first_begin],
        (8, "end"): [each(sum_cross, DH1)],
        (11, "multiply"): [tokens_end, each(small_begin, 0)],
        (11, "turn2"): [tokens_take],
        (11, "end"): [each(small_end, 0), each(small_begin, 1)],
        (12, "turn2"): [each(small_end, 1), each(small_begin, 2)],
        (13, "turn2"): [each(small_end, 2), each(small_begin, 3)],
        (14, "turn2"): [each(small_end, 3)],
    }

    token_load.start()
    for copy in weight_loads:
        copy.start()
    cot_load.start()
    load_tile(0)
    load_tile(1)
    act[:, pl.ds(FFL, PAD - FFL)] = jnp.zeros((TOK, PAD - FFL), BF16)
    lay_tables()
    project()
    by_rows(TOK, 128, rotate)
    for j in range(PIECES):
        attend(j)
    sum_cross(ATTN, PIECES - 1)
    cot_load.wait()
    lay_left(COT)
    tile_ahead(0)
    tile_ahead(1)
    for j in range(PIECES):
        second_norm(j)
    for j in range(PIECES):
        sum_take(ATTN, h2, j)
    tile(0)
    tile(1)
    multiply(0)
    for k in range(count + 2 + LATE):
        steps = (
            ("turn", turn, k - 1),
            ("relay", relay, k),
            ("multiply", multiply, k + 1),
            ("turn2", turn2, k - 2),
            ("relay2", relay2, k - 1),
            ("finish", finish, k - 2 - LATE),
            ("end", None, -1),
        )
        for name, step, at in steps:
            for job in jobs.get((k, name), ()):
                job()
            if 0 <= at < count:
                step(at)
    for k in (count - 2, count - 1):
        for o in range(2):
            for copy in first[k][o]:
                copy.wait_send()
    out_copy.wait()
    tokens_copy.wait()


def block(anywhere_in, vmem_in):
    vmem = pl.BlockSpec(memory_space=pltpu.VMEM)
    anywhere = pl.BlockSpec(memory_space=pl.ANY)
    dma = pltpu.SemaphoreType.DMA
    regular = pltpu.SemaphoreType.REGULAR
    half, rows = (HALF, WIDTH), (2, HALF, WIDTH)
    return pl.pallas_call(
        block_kernel,
        out_shape=(
            jax.ShapeDtypeStruct(rows, BF16),
            jax.ShapeDtypeStruct(rows, BF16),
            jax.ShapeDtypeStruct((48, 384), F32),
            jax.ShapeDtypeStruct((48, 128), F32),
            jax.ShapeDtypeStruct((48, 128), F32),
            jax.ShapeDtypeStruct((48, 384), F32),
            jax.ShapeDtypeStruct((48, FFL), F32),
            jax.ShapeDtypeStruct((48, FFL), F32),
            jax.ShapeDtypeStruct((48, FFL), F32),
            jax.ShapeDtypeStruct((32, 128), F32),
        ),
        in_specs=[anywhere] * len(anywhere_in) + [vmem] * len(vmem_in),
        out_specs=(anywhere,) * 2 + (vmem,) * 8,
        scratch_shapes=[
            pltpu.VMEM(rows, BF16),
            pltpu.VMEM(rows, BF16),
            pltpu.VMEM(rows, BF16),
            pltpu.VMEM(rows, BF16),
            pltpu.VMEM(rows, BF16),
            pltpu.VMEM((WIDTH, TOK), BF16),
            pltpu.VMEM((WIDTH, 384), BF16),
            pltpu.VMEM((WIDTH, 128), BF16),
            pltpu.VMEM((WIDTH, 128), BF16),
            pltpu.VMEM((384, WIDTH), BF16),
            pltpu.VMEM((1, WIDTH), F32),
            pltpu.VMEM((1, WIDTH), F32),
            pltpu.VMEM((1, 384), F32),
            pltpu.VMEM((1, 128), F32),
            pltpu.VMEM((TOK, 128), F32),
            pltpu.VMEM((TOK, 128), F32),
            pltpu.VMEM((TOK, 128), jnp.int32),
            pltpu.VMEM((2, 2, 4, 192, CMAX), F32),
            pltpu.VMEM((2, 2, 6, 96, CMAX), F32),
            pltpu.VMEM((2, 2, 4, 2, 24, CMAX), F32),
            pltpu.VMEM((2, 2, 6, 24, CMAX), F32),
            pltpu.VMEM((2, 2, 24, COLUMNS), F32),
            pltpu.VMEM((2, 24, COLUMNS), F32),
            pltpu.VMEM((2, *half), F32),
            pltpu.VMEM(half, F32),
            pltpu.VMEM(half, F32),
            pltpu.VMEM(half, F32),
            pltpu.VMEM(half, F32),
            pltpu.VMEM(half, F32),
            pltpu.VMEM((4, 32, 128), F32),
            pltpu.VMEM((4, 4, 32, 128), F32),
            pltpu.VMEM((8, 512), F32),
            pltpu.VMEM((TOK, 384), F32),
            pltpu.VMEM((TOK, 128), F32),
            pltpu.VMEM((TOK, 128), BF16),
            pltpu.VMEM((TOK, 384), BF16),
            pltpu.VMEM((TOK, 384), BF16),
            pltpu.VMEM((TOK, 128), BF16),
            pltpu.VMEM((TOK, 384), BF16),
            pltpu.VMEM((TOK, 384), F32),
            pltpu.VMEM((128, TOK), F32),
            pltpu.VMEM((128, TOK), F32),
            pltpu.VMEM((TOK, 640), BF16),
            pltpu.VMEM((TOK, PAD), BF16),
            pltpu.VMEM((TOK, 2 * FFL), BF16),
            pltpu.VMEM((2, *half), F32),
            pltpu.VMEM((3, 512, WIDTH), BF16),
            pltpu.VMEM((2, TOK, 256), F32),
            dma((2, 2, 6)),
            dma((2, 2, 6)),
            dma((2, 2, 6)),
            dma((2, 2, 6)),
            dma((len(CHUNKS), 2)),
            dma((len(CHUNKS), 2)),
            regular((4,)),
            regular((4,)),
            dma((6,)),
            dma((2, 3)),
            dma((4, 3, PIECES)),
            dma((4, 3, PIECES)),
            regular((2,)),
            dma((4, 3)),
            dma((4, 3)),
            dma((2,)),
        ],
        compiler_params=pltpu.CompilerParams(
            collective_id=0, has_side_effects=True, vmem_limit_bytes=VMEM_MIB * MIB
        ),
        name="whole",
    )(*anywhere_in, *vmem_in)


def hand_on_kernel(*refs):
    count = (len(refs) - 2) // 3
    sources, results, held = refs[:count], refs[count : 2 * count], refs[2 * count : 3 * count]
    in_sem, out_sem = refs[3 * count :]
    reads = [
        pltpu.make_async_copy(one, at, in_sem.at[i])
        for i, (one, at) in enumerate(zip(sources, held))
    ]
    writes = [
        pltpu.make_async_copy(at, one, out_sem.at[i])
        for i, (one, at) in enumerate(zip(results, held))
    ]
    for read in reads:
        read.start()
    for read, write in zip(reads, writes):
        read.wait()
        write.start()
    for write in writes:
        write.wait()


def hand_on(arrays):
    anywhere = pl.BlockSpec(memory_space=pl.ANY)
    return pl.pallas_call(
        hand_on_kernel,
        out_shape=tuple(jax.ShapeDtypeStruct(one.shape, one.dtype) for one in arrays),
        in_specs=[anywhere] * len(arrays),
        out_specs=(anywhere,) * len(arrays),
        scratch_shapes=[pltpu.VMEM(one.shape, one.dtype) for one in arrays]
        + [pltpu.SemaphoreType.DMA((len(arrays),))] * 2,
        compiler_params=pltpu.CompilerParams(vmem_limit_bytes=VMEM_MIB * MIB),
        name="hand_on",
    )(*arrays)


def per_device(
    tokens,
    segments,
    norm_one,
    w_query,
    key_projection,
    value_projection,
    w_out,
    q_gain,
    k_gain,
    norm_two,
    w_gate,
    w_up,
    w_down,
    cotangent,
):
    outs = block(
        (
            tokens.reshape(2, HALF, WIDTH),
            cotangent.reshape(2, HALF, WIDTH),
            w_gate.T,
            w_up.T,
            w_down,
            w_query,
            key_projection,
            value_projection,
            w_out,
        ),
        (
            norm_one,
            norm_two,
            q_gain,
            k_gain,
            segments,
            np.tile(FREQUENCY, 4).reshape(1, 128),
        ),
    )
    small = outs[-1]
    block_out, grad_tokens, query, key, value, out, gate, upper, down = hand_on(outs[:-1])
    norms = lax.dynamic_slice_in_dim(
        small[1:25].reshape(2, WIDTH), lax.axis_index("dp") * 48, 48, axis=1
    )
    return (
        block_out.reshape(TOK, WIDTH),
        grad_tokens.reshape(TOK, WIDTH),
        norms[0],
        query,
        key,
        value,
        out.T,
        small[0, :64],
        small[0, 64:],
        norms[1],
        gate,
        upper,
        down.T,
    )


def solution(mesh):
    placed = (
        P("dp", None),
        P("dp", None),
        P(),
        P(None, "tensor"),
        P(None, "tensor"),
        P(None, "tensor"),
        P("tensor", None),
        P(),
        P(),
        P(),
        P(None, "tensor"),
        P(None, "tensor"),
        P("tensor", None),
        P("dp", None),
    )
    return jax.shard_map(
        per_device,
        mesh=mesh,
        in_specs=placed,
        out_specs=(
            P("dp", None),
            P("dp", None),
            P("dp"),
            P("dp", "tensor"),
            P("dp", "tensor"),
            P("dp", "tensor"),
            P("tensor", "dp"),
            P(),
            P(),
            P("dp"),
            P("dp", "tensor"),
            P("dp", "tensor"),
            P("tensor", "dp"),
        ),
        check_vma=False,
    )
```
